128 devices in a mesh: fsdp: 16 (over y, x_hi, core), roll: 8 (over z, x_lo).
Axes of the slice: x: 4 (x_hi: 2, x_lo: 2; x = x_hi * 2 + x_lo), y: 4, z: 4, core: 2. Of those that a mesh axis runs over, the one named last changes fastest.
Arguments:
- activations: bfloat16 [16384, 5120], P('fsdp'), may hold values from -6 to 6
- cotangent: bfloat16 [16384, 5120], P('fsdp', 'roll'), may hold values from -0.125 to 0.125
- first_moment: float32 [5120, 5120], P('fsdp', 'roll'), may hold values from -4 to 4
- second_moment: float32 [5120, 5120], P('fsdp', 'roll'), may hold values from 0.05 to 5
- sketch: float32 [5120, 128], P('roll'), may hold values from -0.078125 to 0.078125
Outputs:
- new_first: float32 [5120, 5120], P('fsdp', 'roll')
- new_second: float32 [5120, 5120], P('fsdp', 'roll')
- rebuilt: bfloat16 [5120, 5120], P('roll')
The draws below stay inside these ranges and needn't reach their ends.
All inputs are finite; a program needn't handle non-finite values.
Results may differ from the reference program's by a relative error of at most 0.006.
Values may be sent and summed in bfloat16 or wider, within the bound.
A program may use at most 192 MiB of HBM per device.

```python
import math
import jax
import jax.numpy as jnp
from jax import lax

D = 5120
RANK = 128
TOK_DEV = 1024
TOKENS = 16384
N_FSDP = 16


def strengthened(values, rng, source, target, shards_of, factor):
    def block_of(dim):
        return (jnp.arange(values.shape[dim]) // (values.shape[dim] // shards_of)).reshape((-1,) + (1,) * (values.ndim - 1 - dim))

    first = jax.random.permutation(rng, shards_of)[block_of(target)]
    second = (block_of(target) + shards_of // 2) % shards_of
    return jnp.where((block_of(source) == first) | (block_of(source) == second), factor * values, values)


def shard_levels(stream_key, dims, split, low, largest):
    factor_of, own = 1.0, jax.random.fold_in(stream_key, 6)
    for position, parts in split:
        heights = jnp.exp(jax.random.uniform(jax.random.fold_in(own, position), (parts,), jnp.float32, low / len(split), largest / len(split)))
        factor_of = factor_of * jnp.repeat(heights, dims[position] // parts).reshape([-1 if axis == position else 1 for axis in range(len(dims))])
    return factor_of


def scatter_about(stream_key, dims, width, most, cuts=(), held_as=jnp.bfloat16):
    gain = shard_levels(stream_key, dims, cuts, -0.22, 0.18) if cuts else 1.0
    entries = jax.random.normal(stream_key, dims, jnp.float32) * width * gain
    return jnp.minimum(jnp.maximum(entries, -most), most).astype(held_as)


def heavy_noise(rng, dims, width, reach, pieces, heavy, dtype=jnp.bfloat16):
    entries = width * jax.random.normal(rng, dims, jnp.float32)
    if pieces:
        entries = entries * shard_levels(rng, dims, pieces, -0.22, 0.18)
    return jnp.clip(strengthened(entries, jax.random.fold_in(rng, 3), *heavy), -reach, reach).astype(dtype)


def setup_inputs(seed: int = 0) -> dict:
    splits = jax.random.split(jax.random.key(seed), 6)
    return {
        "activations": heavy_noise(splits[0], (TOKENS, D), 1.0, 6.0, ((0, 16),), (0, 1, 16, 2.0)),
        "cotangent": scatter_about(splits[1], (TOKENS, D), (TOKENS ** -0.5), 0.125, ((0, 16), (1, 8))),
        "first_moment": scatter_about(splits[2], (D, D), 0.3, 4.0, ((0, 16), (1, 8)), jnp.float32),
        "second_moment": jnp.clip(jnp.exp(math.log(5.0) - 4.6051702 * jax.random.uniform(splits[3], (D, D), jnp.float32) ** shard_levels(splits[3], (D, D), ((0, 16), (1, 8)), -0.2, 0.2)), 0.05, 5.0),
        "sketch": scatter_about(splits[4], (D, RANK), D ** -0.5, 0.078125, ((0, 8),), jnp.float32),
    }


beta_one = 0.9
beta_two = 0.95
epsilon = 1e-08
hp = lax.Precision.HIGHEST

def reference(activations, cotangent, first_moment, second_moment, sketch):
    act_groups = activations.reshape(N_FSDP, TOK_DEV, D)
    cot_groups = cotangent.reshape(N_FSDP, TOK_DEV, D)

    def add_group(total, pair):
        part = lax.dot_general(pair[0].astype(jnp.float32), pair[1].astype(jnp.float32), (((0,), (0,)), ((), ())), preferred_element_type=jnp.float32)
        return (total + part, None)
    grad, unused = lax.scan(add_group, jnp.zeros((D, D), jnp.float32), (act_groups, cot_groups))
    new_first = beta_one * first_moment + (1.0 - beta_one) * grad
    new_second = beta_two * second_moment + (1.0 - beta_two) * grad * grad
    direction = new_first / (1.0 - beta_one ** 20) / (jnp.sqrt(new_second / (1.0 - beta_two ** 20)) + epsilon)
    sketched = jnp.dot(direction, sketch, precision=hp)
    gram = jnp.dot(sketched.T, sketched, precision=hp)
    lower = jnp.linalg.cholesky(gram)
    basis = lax.linalg.triangular_solve(lower, sketched.T, left_side=True, lower=True).T
    coeffs = jnp.dot(basis.T, direction, precision=hp)
    basis_low = basis.astype(jnp.bfloat16)
    coeffs_low = coeffs.astype(jnp.bfloat16)
    rebuilt = jnp.dot(basis_low.astype(jnp.float32), coeffs_low.astype(jnp.float32), preferred_element_type=jnp.float32).astype(jnp.bfloat16)
    return (new_first, new_second, rebuilt)
```

```python
import functools

import jax
import jax.numpy as jnp
from jax import lax
from jax.experimental import pallas as pl
from jax.experimental.pallas import tpu as pltpu
from jax.sharding import PartitionSpec as P

beta_one = 0.9
beta_two = 0.95
epsilon = 1e-08
hp = lax.Precision.HIGHEST
MESH = pl.DeviceIdType.MESH
f32, bf16 = jnp.float32, jnp.bfloat16
DN0 = (((0,), (0,)), ((), ()))

D, TOK, RANK = 5120, 1024, 128
COLS = 640
ROWS = 320
HALF = 160
PIECE = ROWS // 8

ORDER = ((2, 1), (2, 0), (1, 1), (3, 1), (1, 0), (3, 0), (0, 1), (0, 0))
SEMS = 96


def looped(total, step, body):
    def one(i, carry):
        body(pl.multiple_of(i * step, step))
        return carry
    lax.fori_loop(0, total // step, one, 0)


def kernel(
    act, cot, first, second, sketch,
    new_first, new_second, gram_out, s_out, r_out,
    abuf, cbuf, pbuf, own, psend, crecv, ysend, y1recv, y2recv, xsend, xrecv,
    mbuf, vbuf, dbuf, skbuf, rpart, rrecv, rfull, gpart, gcrecv, gslots, ghalf,
    spart, screcv, sslots,
    lsem, ssem, rsem,
):
    f, r = lax.axis_index("fsdp"), lax.axis_index("roll")
    y, xh, c = f // 4, (f // 2) % 2, f % 2
    z, xl = r // 2, r % 2
    q = f // 2

    def dev(y=y, xh=xh, c=c, z=z, xl=xl):
        return {"fsdp": (y * 2 + xh) * 2 + c, "roll": z * 2 + xl}

    sibling = dev(c=1 - c)
    plus, minus = dev(y=(y + 1) % 4), dev(y=(y + 3) % 4)
    across = dev(xh=1 - xh)

    def chip(k):
        other = (q + k) % 8
        return {"fsdp": other * 2 + c, "roll": r}, other

    def roller(k):
        other = (r + k) % 8
        return {"fsdp": f, "roll": other}, other

    def around_x(k):
        other = (xh * 2 + xl + k) % 4
        return dev(xh=other // 2, xl=other % 2)

    used = [0]

    def remote(src, dst, where):
        i = used[0]
        used[0] += 1
        return pltpu.make_async_remote_copy(
            src_ref=src, dst_ref=dst, send_sem=ssem.at[i], recv_sem=rsem.at[i],
            device_id=where, device_id_type=MESH,
        )

    pending = []

    def send(src, dst, where):
        copy = remote(src, dst, where)
        copy.start()
        pending.append(copy)
        return copy

    loads = []
    c_load = pltpu.make_async_copy(cot, cbuf, lsem.at[8])
    c_load.start()
    for k, (dy, dxh) in enumerate(ORDER):
        block = ((y + dy) % 4) * 2 + (xh + dxh) % 2
        load = pltpu.make_async_copy(
            act.at[:, pl.ds(pl.multiple_of(block * 640, 640), 640)], abuf.at[k], lsem.at[k]
        )
        load.start()
        loads.append(load)
    late = [
        pltpu.make_async_copy(first, mbuf, lsem.at[9]),
        pltpu.make_async_copy(second, vbuf, lsem.at[10]),
        pltpu.make_async_copy(sketch, skbuf, lsem.at[11]),
    ]
    for load in late:
        load.start()

    barrier = pltpu.get_barrier_semaphore()
    greeted = [sibling] + [chip(k)[0] for k in range(1, 8)] + [roller(k)[0] for k in range(1, 8)] + [dev(xh=1 - xh, xl=1 - xl)]
    for other in greeted:
        pl.semaphore_signal(barrier, inc=1, device_id=other, device_id_type=MESH)
    c_load.wait()

    mine = pl.multiple_of(c * ROWS, ROWS)
    theirs = pl.multiple_of((1 - c) * ROWS, ROWS)
    halves = []

    def compute(k):
        loads[k].wait()
        pbuf[...] = lax.dot_general(abuf[k], cbuf[...], DN0, preferred_element_type=f32)

        def split(o):
            psend[k, pl.ds(o, 32)] = pbuf[pl.ds(theirs + o, 32)].astype(bf16)
            own[k, pl.ds(o, 32)] = pbuf[pl.ds(mine + o, 32)]
        looped(ROWS, 32, split)
        if k == 0:
            pl.semaphore_wait(barrier, len(greeted))
        halves.append(send(psend.at[k], crecv.at[k], sibling))

    step_one, step_two = {}, {}

    def post(k):
        dy, dxh = ORDER[k]
        halves[k].wait_recv()
        if dy == 2:
            def add(o):
                ysend[k, pl.ds(o, 32)] = (own[k, pl.ds(o, 32)] + crecv[k, pl.ds(o, 32)].astype(f32)).astype(bf16)
            looped(ROWS, 32, add)
            for way, where in enumerate((plus, minus)):
                step_one[way, dxh] = send(
                    ysend.at[k, pl.ds(way * HALF, HALF)], y1recv.at[way, dxh], where)
        elif dy == 0:
            def add(o):
                own[k, pl.ds(o, 32)] = own[k, pl.ds(o, 32)] + crecv[k, pl.ds(o, 32)].astype(f32)
            looped(ROWS, 32, add)
        else:
            way = 0 if dy == 1 else 1
            alone = (1 - way) * HALF

            def add(o):
                ysend[k, pl.ds(alone + o, 32)] = (
                    own[k, pl.ds(alone + o, 32)] + crecv[k, pl.ds(alone + o, 32)].astype(f32)).astype(bf16)
            looped(HALF, 32, add)
            step_two[way, dxh, 1] = send(
                ysend.at[k, pl.ds(alone, HALF)], y2recv.at[way, dxh, pl.ds(alone, HALF)],
                plus if way == 0 else minus)

    def accumulate(dxh):
        for way, dy in ((0, 1), (1, 3)):
            k = ORDER.index((dy, dxh))
            step_one[way, dxh].wait_recv()
            start = way * HALF

            def add(o):
                ysend[k, pl.ds(start + o, 32)] = (
                    own[k, pl.ds(start + o, 32)] + crecv[k, pl.ds(start + o, 32)].astype(f32)
                    + y1recv[way, dxh, pl.ds(o, 32)].astype(f32)).astype(bf16)
            looped(HALF, 32, add)
            step_two[way, dxh, 0] = send(
                ysend.at[k, pl.ds(start, HALF)], y2recv.at[way, dxh, pl.ds(start, HALF)],
                plus if way == 0 else minus)

    for k in range(8):
        compute(k)
        if k >= 1:
            post(k - 1)
        if k == 6:
            accumulate(1)
    post(7)
    accumulate(0)

    crossing = []
    for part in range(2):
        o0 = part * HALF
        for way in range(2):
            step_two[way, 1, 0 if way == part else 1].wait_recv()

        def add(o):
            at = pl.ds(o0 + o, 32)
            xsend[at] = (own[6, at] + y2recv[0, 1, at].astype(f32) + y2recv[1, 1, at].astype(f32)).astype(bf16)
        looped(HALF, 32, add)
        crossing.append(send(xsend.at[pl.ds(o0, HALF)], xrecv.at[pl.ds(o0, HALF)], across))
    for load in late:
        load.wait()
    stores = []
    for part in range(2):
        o0 = part * HALF
        for way in range(2):
            step_two[way, 0, 0 if way == part else 1].wait_recv()
        crossing[part].wait_recv()

        def adam(o):
            at = pl.ds(o0 + o, 16)
            grad = (own[7, at] + y2recv[0, 0, at].astype(f32) + y2recv[1, 0, at].astype(f32)
                    + xrecv[at].astype(f32))
            new_m = beta_one * mbuf[at] + (1.0 - beta_one) * grad
            new_v = beta_two * vbuf[at] + (1.0 - beta_two) * grad * grad
            mbuf[at] = new_m
            vbuf[at] = new_v
            dbuf[at] = new_m / (1.0 - beta_one**20) / (jnp.sqrt(new_v / (1.0 - beta_two**20)) + epsilon)
        looped(HALF, 16, adam)
    for i, (src, dst) in enumerate(((mbuf, new_first), (vbuf, new_second))):
        store = pltpu.make_async_copy(src, dst, lsem.at[i])
        store.start()
        stores.append(store)

    rpart[...] = jnp.dot(dbuf[...], skbuf[...], precision=hp, preferred_element_type=f32)
    parts = []
    for k in range(1, 8):
        where, other = roller(k)
        parts.append(send(rpart.at[pl.ds(pl.multiple_of(other * PIECE, 8), PIECE)], rrecv.at[k - 1], where))
    my_piece = pl.ds(pl.multiple_of(r * PIECE, 8), PIECE)
    total = rpart[my_piece]
    for k in range(7):
        parts[k].wait_recv()
        total = total + rrecv[k]
    rfull[my_piece] = total
    parts = [send(rfull.at[my_piece], rfull.at[my_piece], roller(k)[0]) for k in range(1, 8)]
    for part in parts:
        part.wait_recv()

    gpart[...] = lax.dot_general(rfull[...], rfull[...], DN0, precision=hp, preferred_element_type=f32)
    my_half = pl.ds(pl.multiple_of(c * 64, 64), 64)
    other_half = pl.ds(pl.multiple_of((1 - c) * 64, 64), 64)
    copy = send(gpart.at[other_half], gcrecv, sibling)
    spart[...] = lax.dot_general(rfull[...], dbuf[...], DN0, precision=hp, preferred_element_type=f32)
    scopy = send(spart.at[other_half], screcv, sibling)
    copy.wait_recv()
    gslots[q] = gpart[my_half] + gcrecv[...]
    parts = [send(gslots.at[q], gslots.at[q], chip(k)[0]) for k in range(1, 8)]

    scopy.wait_recv()
    spart[my_half] = spart[my_half] + screcv[...]
    sparts = []
    for k in range(1, 8):
        where, other = chip(k)
        sparts.append(send(spart.at[pl.ds(pl.multiple_of(c * 64 + other * 8, 8), 8)], sslots.at[q], where))
    sslots[q] = spart[pl.ds(pl.multiple_of(c * 64 + q * 8, 8), 8)]

    for part in parts:
        part.wait_recv()
    total = gslots[0]
    for k in range(1, 8):
        total = total + gslots[k]
    ghalf[c] = total
    copy = send(ghalf.at[c], ghalf.at[c], sibling)

    for part in sparts:
        part.wait_recv()
    total = sslots[0]
    for k in range(1, 8):
        total = total + sslots[k]
    s, t = c * y + (1 - c) * z, c * z + (1 - c) * y
    row = pl.ds(pl.multiple_of(xh * 8, 8), 8)
    s_out[c, s, t, xl, row] = total
    parts = [
        send(s_out.at[c, s, t, xl, row], s_out.at[c, s, t, xl, row], around_x(k)) for k in range(1, 4)
    ]

    @pl.when((y == z) & (xh == xl))
    def _():
        r_out[c] = rfull[...]
    rcopies = []
    for k in range(1, 8):
        rcopies.append(remote(r_out.at[c], r_out.at[c], chip(k)[0]))

    @pl.when((y == z) & (xh == xl))
    def _():
        for rcopy in rcopies:
            rcopy.start()

    for part in parts:
        part.wait_recv()

    def along_t(k):
        return dev(y=(y + (1 - c) * k) % 4, z=(z + c * k) % 4)

    def along_s(k):
        return dev(y=(y + c * k) % 4, z=(z + (1 - c) * k) % 4)
    parts = [send(s_out.at[c, s, t], s_out.at[c, s, t], along_t(k)) for k in (1, 3, 2)]
    for part in parts:
        part.wait_recv()
    parts = [send(s_out.at[c, s], s_out.at[c, s], along_s(k)) for k in (1, 3, 2)]

    copy.wait_recv()
    gram_out[0:64] = ghalf[0]
    gram_out[64:128] = ghalf[1]
    for k in range(1, 8):
        @pl.when((z * 2 + xl + k) % 8 == q)
        def _():
            rcopies[k - 1].wait_recv()
    rcopy = send(r_out.at[c], r_out.at[c], sibling)

    copies = [send(s_out.at[c, s], s_out.at[c, s], sibling)]
    for k, part in zip((1, 3, 2), parts):
        part.wait_recv()
        have = (s + 4 - k) % 4
        copies.append(send(s_out.at[c, have], s_out.at[c, have], sibling))
    rcopy.wait_recv()
    for part in copies:
        part.wait_recv()

    for part in pending:
        part.wait_send()

    @pl.when((y == z) & (xh == xl))
    def _():
        for part in rcopies:
            part.wait_send()
    for store in stores:
        store.wait()


def local(activations, cotangent, first_moment, second_moment, sketch):
    any_spec, vmem = pl.BlockSpec(memory_space=pl.ANY), pl.BlockSpec(memory_space=pltpu.VMEM)
    state = jax.ShapeDtypeStruct((ROWS, COLS), f32)
    new_first, new_second, gram, s_all, r_all = pl.pallas_call(
        kernel,
        name="step",
        out_shape=(
            state, state,
            jax.ShapeDtypeStruct((RANK, RANK), f32),
            jax.ShapeDtypeStruct((2, 4, 4, 2, 16, COLS), f32),
            jax.ShapeDtypeStruct((2, ROWS, RANK), f32),
        ),
        in_specs=[any_spec] * 5,
        out_specs=(any_spec, any_spec, vmem, vmem, vmem),
        scratch_shapes=[
            pltpu.VMEM((8, TOK, 640), bf16),
            pltpu.VMEM((TOK, COLS), bf16),
            pltpu.VMEM((640, COLS), f32),
            pltpu.VMEM((8, ROWS, COLS), f32),
            pltpu.VMEM((8, ROWS, COLS), bf16),
            pltpu.VMEM((8, ROWS, COLS), bf16),
            pltpu.VMEM((6, ROWS, COLS), bf16),
            pltpu.VMEM((2, 2, HALF, COLS), bf16),
            pltpu.VMEM((2, 2, ROWS, COLS), bf16),
            pltpu.VMEM((ROWS, COLS), bf16),
            pltpu.VMEM((ROWS, COLS), bf16),
            pltpu.VMEM((ROWS, COLS), f32),
            pltpu.VMEM((ROWS, COLS), f32),
            pltpu.VMEM((ROWS, COLS), f32),
            pltpu.VMEM((COLS, RANK), f32),
            pltpu.VMEM((ROWS, RANK), f32),
            pltpu.VMEM((7, PIECE, RANK), f32),
            pltpu.VMEM((ROWS, RANK), f32),
            pltpu.VMEM((RANK, RANK), f32),
            pltpu.VMEM((64, RANK), f32),
            pltpu.VMEM((8, 64, RANK), f32),
            pltpu.VMEM((2, 64, RANK), f32),
            pltpu.VMEM((RANK, COLS), f32),
            pltpu.VMEM((64, COLS), f32),
            pltpu.VMEM((8, 8, COLS), f32),
            pltpu.SemaphoreType.DMA((12,)),
            pltpu.SemaphoreType.DMA((SEMS,)),
            pltpu.SemaphoreType.DMA((SEMS,)),
        ],
        compiler_params=pltpu.CompilerParams(
            collective_id=0, has_side_effects=True, vmem_limit_bytes=58 << 20),
    )(activations, cotangent, first_moment, second_moment, sketch)
    lower = jnp.linalg.cholesky(gram)
    inverse = lax.linalg.triangular_solve(lower, jnp.eye(RANK, dtype=f32), left_side=True, lower=True)
    low = s_all[0].transpose(1, 3, 0, 2, 4)
    high = s_all[1].transpose(0, 3, 1, 2, 4)
    s_full = jnp.stack([low, high]).reshape(RANK, D)
    coeffs = jnp.dot(inverse, s_full, precision=hp).astype(bf16)
    basis = lax.dot_general(r_all.reshape(2 * ROWS, RANK), inverse, (((1,), (1,)), ((), ())), precision=hp).astype(bf16)
    rebuilt = jnp.dot(basis, coeffs, preferred_element_type=f32).astype(bf16)
    return new_first, new_second, rebuilt


def solution(mesh):
    placed = (P("fsdp", None), P("fsdp", "roll"), P("fsdp", "roll"), P("fsdp", "roll"), P("roll", None))
    return jax.shard_map(
        local,
        mesh=mesh,
        in_specs=placed,
        out_specs=(P("fsdp", "roll"), P("fsdp", "roll"), P("roll", None)),
        check_vma=False,
    )
```

```python
import functools

import jax
import jax.numpy as jnp
from jax import lax
from jax.experimental import pallas as pl
from jax.experimental.pallas import tpu as pltpu
from jax.sharding import PartitionSpec as P

beta_one = 0.9
beta_two = 0.95
epsilon = 1e-08
hp = lax.Precision.HIGHEST
MESH = pl.DeviceIdType.MESH
f32, bf16 = jnp.float32, jnp.bfloat16
DN0 = (((0,), (0,)), ((), ()))
DN1 = (((1,), (1,)), ((), ()))

D, TOK, RANK = 5120, 1024, 128
COLS = 640
ROWS = 320
HALF = 160
PIECE = ROWS // 8

ORDER = ((2, 1), (2, 0), (1, 1), (3, 1), (1, 0), (3, 0), (0, 1), (0, 0))
SEMS = 96


def looped(total, step, body):
    def one(i, carry):
        body(pl.multiple_of(i * step, step))
        return carry
    lax.fori_loop(0, total // step, one, 0)


def split3(v):
    a = v.astype(bf16).astype(f32); v = v - a
    b = v.astype(bf16).astype(f32)
    return a, b, (v - b).astype(bf16).astype(f32)

def factor_inverse(gram_ref, inv_ref):
    lane = lax.broadcasted_iota(jnp.int32, (8, 128), 1)
    sub = lax.broadcasted_iota(jnp.int32, (8, 128), 0)
    panels = [gram_ref[8 * i:8 * i + 8, :] for i in range(16)]
    for k in range(16):
        panel = panels[k]
        scale = jnp.zeros((8, 128), f32)
        for j in range(8):
            p = 8 * k + j
            col = jnp.broadcast_to(panel[:, p:p + 1], (8, 128))
            pivot = jnp.broadcast_to(col[j:j + 1, :], (8, 128))
            recip = 1.0 / pivot
            scale = jnp.where(sub == j, recip, scale)
            m = jnp.where(sub > j, -col * recip, 0.0)
            row = jnp.broadcast_to(jnp.where(lane[j:j + 1] == p, 1.0, panel[j:j + 1, :]), (8, 128))
            panel = jnp.where((lane == p) & (sub > j), 0.0, panel) + m * row
        panels[k] = panel
        if k < 15:
            inside = (lane >= 8 * k) & (lane < 8 * k + 8)
            ext = jnp.where(inside & (lane - 8 * k > sub), 0.0, panel)
            ext = jnp.where(inside & (lane - 8 * k == sub), 1.0, ext)
            lhs = -panel * scale
            a1, a2, a3 = split3(lhs)
            b1, b2, b3 = split3(ext)
            left = jnp.concatenate([a1, a1, a2, a2, a1, a3], axis=0).astype(bf16)
            right = jnp.concatenate([b1, b2, b1, b2, b3, b1], axis=0).astype(bf16)
            upd = lax.dot_general(left, right, DN0, preferred_element_type=f32)
            for i in range(k + 1, 16):
                panels[i] = jnp.where(inside, 0.0, panels[i]) + upd[8 * i:8 * i + 8, :]
        yield k
    for k in range(16):
        at = lane == sub + 8 * k
        d = jnp.sum(jnp.where(at, panels[k], 0.0), axis=1, keepdims=True)
        m = jnp.where(lane < sub + 8 * k, panels[k], jnp.where(at, 1.0, 0.0))
        inv_ref[8 * k:8 * k + 8, :] = m * lax.rsqrt(d)


def kernel(
    act, cot, first, second, sketch,
    new_first, new_second, coeffs_out, basis_out,
    abuf, cbuf, pbuf, own, psend, crecv, ysend, y1recv, y2recv, xsend, xrecv,
    mbuf, vbuf, dbuf, skbuf, rpart, rrecv, rfull, r_out, gpart, gcrecv, gslots, gfull,
    spart, screcv, sslots, s_out, inverse,
    lsem, ssem, rsem,
):
    f, r = lax.axis_index("fsdp"), lax.axis_index("roll")
    y, xh, c = f // 4, (f // 2) % 2, f % 2
    z, xl = r // 2, r % 2
    q = f // 2

    def dev(y=y, xh=xh, c=c, z=z, xl=xl):
        return {"fsdp": (y * 2 + xh) * 2 + c, "roll": z * 2 + xl}

    sibling = dev(c=1 - c)
    plus, minus = dev(y=(y + 1) % 4), dev(y=(y + 3) % 4)
    across = dev(xh=1 - xh)

    def chip(k):
        other = (q + k) % 8
        return {"fsdp": other * 2 + c, "roll": r}, other

    def roller(k):
        other = (r + k) % 8
        return {"fsdp": f, "roll": other}, other

    def around_x(k):
        other = (xh * 2 + xl + k) % 4
        return dev(xh=other // 2, xl=other % 2)

    used = [0]

    def remote(src, dst, where):
        i = used[0]
        used[0] += 1
        return pltpu.make_async_remote_copy(
            src_ref=src, dst_ref=dst, send_sem=ssem.at[i], recv_sem=rsem.at[i],
            device_id=where, device_id_type=MESH,
        )

    pending = []

    def send(src, dst, where):
        copy = remote(src, dst, where)
        copy.start()
        pending.append(copy)
        return copy

    loads = []
    c_load = pltpu.make_async_copy(cot, cbuf, lsem.at[8])
    c_load.start()
    for k, (dy, dxh) in enumerate(ORDER):
        block = ((y + dy) % 4) * 2 + (xh + dxh) % 2
        load = pltpu.make_async_copy(
            act.at[:, pl.ds(pl.multiple_of(block * 640, 640), 640)], abuf.at[k], lsem.at[k]
        )
        load.start()
        loads.append(load)
    late = [
        pltpu.make_async_copy(first, mbuf, lsem.at[9]),
        pltpu.make_async_copy(second, vbuf, lsem.at[10]),
        pltpu.make_async_copy(sketch, skbuf, lsem.at[11]),
    ]
    for load in late:
        load.start()

    barrier = pltpu.get_barrier_semaphore()
    greeted = [sibling] + [chip(k)[0] for k in range(1, 8)] + [roller(k)[0] for k in range(1, 8)] + [dev(xh=1 - xh, xl=1 - xl)]
    for other in greeted:
        pl.semaphore_signal(barrier, inc=1, device_id=other, device_id_type=MESH)
    c_load.wait()

    mine = pl.multiple_of(c * ROWS, ROWS)
    theirs = pl.multiple_of((1 - c) * ROWS, ROWS)
    halves = []

    def compute(k):
        loads[k].wait()
        pbuf[...] = lax.dot_general(abuf[k], cbuf[...], DN0, preferred_element_type=f32)

        def split(o):
            psend[k, pl.ds(o, 32)] = pbuf[pl.ds(theirs + o, 32)].astype(bf16)
            own[k, pl.ds(o, 32)] = pbuf[pl.ds(mine + o, 32)]
        looped(ROWS, 32, split)
        if k == 0:
            pl.semaphore_wait(barrier, len(greeted))
        halves.append(send(psend.at[k], crecv.at[k], sibling))

    step_one, step_two = {}, {}

    def post(k):
        dy, dxh = ORDER[k]
        halves[k].wait_recv()
        if dy == 2:
            def add(o):
                ysend[k, pl.ds(o, 32)] = (own[k, pl.ds(o, 32)] + crecv[k, pl.ds(o, 32)].astype(f32)).astype(bf16)
            looped(ROWS, 32, add)
            for way, where in enumerate((plus, minus)):
                step_one[way, dxh] = send(
                    ysend.at[k, pl.ds(way * HALF, HALF)], y1recv.at[way, dxh], where)
        elif dy == 0:
            def add(o):
                own[k, pl.ds(o, 32)] = own[k, pl.ds(o, 32)] + crecv[k, pl.ds(o, 32)].astype(f32)
            looped(ROWS, 32, add)
        else:
            way = 0 if dy == 1 else 1
            alone = (1 - way) * HALF

            def add(o):
                ysend[k, pl.ds(alone + o, 32)] = (
                    own[k, pl.ds(alone + o, 32)] + crecv[k, pl.ds(alone + o, 32)].astype(f32)).astype(bf16)
            looped(HALF, 32, add)
            step_two[way, dxh, 1] = send(
                ysend.at[k, pl.ds(alone, HALF)], y2recv.at[way, dxh, pl.ds(alone, HALF)],
                plus if way == 0 else minus)

    def accumulate(dxh):
        for way, dy in ((0, 1), (1, 3)):
            k = ORDER.index((dy, dxh))
            step_one[way, dxh].wait_recv()
            start = way * HALF

            def add(o):
                ysend[k, pl.ds(start + o, 32)] = (
                    own[k, pl.ds(start + o, 32)] + crecv[k, pl.ds(start + o, 32)].astype(f32)
                    + y1recv[way, dxh, pl.ds(o, 32)].astype(f32)).astype(bf16)
            looped(HALF, 32, add)
            step_two[way, dxh, 0] = send(
                ysend.at[k, pl.ds(start, HALF)], y2recv.at[way, dxh, pl.ds(start, HALF)],
                plus if way == 0 else minus)

    for k in range(8):
        compute(k)
        if k >= 1:
            post(k - 1)
        if k == 6:
            accumulate(1)
    post(7)
    accumulate(0)

    crossing = []
    for part in range(2):
        o0 = part * HALF
        for way in range(2):
            step_two[way, 1, 0 if way == part else 1].wait_recv()

        def add(o):
            at = pl.ds(o0 + o, 32)
            xsend[at] = (own[6, at] + y2recv[0, 1, at].astype(f32) + y2recv[1, 1, at].astype(f32)).astype(bf16)
        looped(HALF, 32, add)
        crossing.append(send(xsend.at[pl.ds(o0, HALF)], xrecv.at[pl.ds(o0, HALF)], across))
    for load in late:
        load.wait()
    stores = []
    for part in range(2):
        o0 = part * HALF
        for way in range(2):
            step_two[way, 0, 0 if way == part else 1].wait_recv()
        crossing[part].wait_recv()

        def adam(o):
            at = pl.ds(o0 + o, 16)
            grad = (own[7, at] + y2recv[0, 0, at].astype(f32) + y2recv[1, 0, at].astype(f32)
                    + xrecv[at].astype(f32))
            new_m = beta_one * mbuf[at] + (1.0 - beta_one) * grad
            new_v = beta_two * vbuf[at] + (1.0 - beta_two) * grad * grad
            mbuf[at] = new_m
            vbuf[at] = new_v
            dbuf[at] = new_m / (1.0 - beta_one**20) / (jnp.sqrt(new_v / (1.0 - beta_two**20)) + epsilon)
        looped(HALF, 16, adam)
    for i, (src, dst) in enumerate(((mbuf, new_first), (vbuf, new_second))):
        store = pltpu.make_async_copy(src, dst, lsem.at[i])
        store.start()
        stores.append(store)

    rpart[...] = jnp.dot(dbuf[...], skbuf[...], precision=hp, preferred_element_type=f32)
    parts = []
    for k in range(1, 8):
        where, other = roller(k)
        parts.append(send(rpart.at[pl.ds(pl.multiple_of(other * PIECE, 8), PIECE)], rrecv.at[k - 1], where))
    my_piece = pl.ds(pl.multiple_of(r * PIECE, 8), PIECE)
    total = rpart[my_piece]
    for k in range(7):
        parts[k].wait_recv()
        total = total + rrecv[k]
    rfull[my_piece] = total
    parts = [send(rfull.at[my_piece], rfull.at[my_piece], roller(k)[0]) for k in range(1, 8)]
    swap = remote(rfull.at[my_piece], r_out.at[c, my_piece], dev(y=z, xh=xl, z=y, xl=xh))
    own_piece = pl.ds(pl.multiple_of(q * PIECE, 8), PIECE)
    swapped = (y != z) | (xh != xl)

    @pl.when(swapped)
    def _():
        swap.start()

    @pl.when(jnp.logical_not(swapped))
    def _():
        r_out[c, own_piece] = rfull[my_piece]
    for part in parts:
        part.wait_recv()

    my_half = pl.ds(pl.multiple_of(c * 64, 64), 64)
    other_half = pl.ds(pl.multiple_of((1 - c) * 64, 64), 64)
    my_rows = pl.ds(pl.multiple_of(c * 64 + q * 8, 8), 8)
    gpart[...] = lax.dot_general(rfull[...], rfull[...], DN0, precision=hp, preferred_element_type=f32)
    gcopy = send(gpart.at[other_half], gcrecv, sibling)
    spart[...] = lax.dot_general(rfull[...], dbuf[...], DN0, precision=hp, preferred_element_type=f32)
    scopy = send(spart.at[other_half], screcv, sibling)

    def scatter(mine, slots):
        sent = []
        for k in range(1, 8):
            where, other = chip(k)
            sent.append(send(mine.at[pl.ds(pl.multiple_of(c * 64 + other * 8, 8), 8)], slots.at[q], where))
        slots[q] = mine[my_rows]
        return sent

    def gathered(sent, slots):
        for part in sent:
            part.wait_recv()
        total = slots[0]
        for k in range(1, 8):
            total = total + slots[k]
        return total

    gcopy.wait_recv()
    gpart[my_half] = gpart[my_half] + gcrecv[...]
    gsent = scatter(gpart, gslots)
    scopy.wait_recv()
    spart[my_half] = spart[my_half] + screcv[...]
    ssent = scatter(spart, sslots)
    gfull[my_rows] = gathered(gsent, gslots)
    gsent = [send(gfull.at[my_rows], gfull.at[my_rows], chip(k)[0]) for k in range(1, 8)]

    @pl.when(swapped)
    def _():
        swap.wait_recv()
    rsent = [send(r_out.at[c, own_piece], r_out.at[c, own_piece], chip(k)[0]) for k in range(1, 8)]

    s, t = c * y + (1 - c) * z, c * z + (1 - c) * y
    row = pl.ds(pl.multiple_of(xh * 8, 8), 8)
    s_out[c, s, t, xl, row] = gathered(ssent, sslots)
    ssent = [send(s_out.at[c, s, t, xl, row], s_out.at[c, s, t, xl, row], around_x(k)) for k in range(1, 4)]
    for part in gsent:
        part.wait_recv()
    gcopy = send(gfull.at[my_half], gfull.at[my_half], sibling)

    def along_t(k):
        return dev(y=(y + (1 - c) * k) % 4, z=(z + c * k) % 4)

    def along_s(k):
        return dev(y=(y + c * k) % 4, z=(z + (1 - c) * k) % 4)

    gcopy.wait_recv()
    steps = factor_inverse(gfull, inverse)
    next(steps)
    for part in ssent:
        part.wait_recv()
    ssent = [send(s_out.at[c, s, t], s_out.at[c, s, t], along_t(k)) for k in (1, 3, 2)]
    for _ in range(4):
        next(steps)
    for part in ssent:
        part.wait_recv()
    ssent = [send(s_out.at[c, s], s_out.at[c, s], along_s(k)) for k in (1, 3, 2)]
    copies = [send(s_out.at[c, s], s_out.at[c, s], sibling)]
    for _ in range(2):
        next(steps)
    for part in rsent:
        part.wait_recv()
    rcopy = send(r_out.at[c], r_out.at[c], sibling)
    for k, part in zip((1, 3, 2), ssent):
        for _ in range(3):
            next(steps)
        part.wait_recv()
        have = (s + 4 - k) % 4
        copies.append(send(s_out.at[c, have], s_out.at[c, have], sibling))
    for _ in steps:
        pass
    rcopy.wait_recv()
    for core in range(2):
        basis_out[core * ROWS:(core + 1) * ROWS] = lax.dot_general(
            r_out[core], inverse[...], DN1, precision=hp, preferred_element_type=f32).astype(bf16)
    for part in copies:
        part.wait_recv()

    def block(i, carry):
        bz, bxl = i // 2, i % 2
        rows = [s_out[0, bz, by, bxl] for by in range(4)] + [s_out[1, by, bz, bxl] for by in range(4)]
        coeffs_out[:, pl.ds(pl.multiple_of(i * COLS, COLS), COLS)] = jnp.dot(
            inverse[...], jnp.concatenate(rows, axis=0), precision=hp, preferred_element_type=f32).astype(bf16)
        return carry
    lax.fori_loop(0, 8, block, 0)

    for part in pending:
        part.wait_send()

    @pl.when(swapped)
    def _():
        swap.wait_send()
    for store in stores:
        store.wait()


def rebuild(basis, coeffs, first, second, rebuilt, new_first, new_second, bbuf, cbuf, obuf, sem):
    copies = [pltpu.make_async_copy(basis, bbuf, sem.at[2])]
    copies += [pltpu.make_async_copy(coeffs.at[:, pl.ds(i * 1280, 1280)], cbuf.at[i], sem.at[3 + i]) for i in range(4)]
    kept = [pltpu.make_async_copy(first, new_first, sem.at[0]), pltpu.make_async_copy(second, new_second, sem.at[1])]
    for copy in copies + kept:
        copy.start()
    copies[0].wait()
    for i in range(4):
        copies[1 + i].wait()
        columns = pl.ds(i * 1280, 1280)
        for j in range(2):
            rows = pl.ds(j * ROWS, ROWS)
            obuf[i, rows] = jnp.dot(bbuf[rows], cbuf[i], preferred_element_type=f32).astype(bf16)
            copy = pltpu.make_async_copy(obuf.at[i, rows], rebuilt.at[rows, columns], sem.at[7 + 2 * i + j])
            copy.start()
            kept.append(copy)
    for copy in kept:
        copy.wait()


def local(activations, cotangent, first_moment, second_moment, sketch):
    hbm, vmem = pl.BlockSpec(memory_space=pltpu.HBM), pl.BlockSpec(memory_space=pltpu.VMEM)
    state = jax.ShapeDtypeStruct((ROWS, COLS), f32)
    first, second, coeffs, basis = pl.pallas_call(
        kernel,
        name="step",
        out_shape=(
            state, state,
            jax.ShapeDtypeStruct((RANK, D), bf16),
            jax.ShapeDtypeStruct((2 * ROWS, RANK), bf16),
        ),
        in_specs=[hbm] * 5,
        out_specs=(hbm, hbm, vmem, vmem),
        scratch_shapes=[
            pltpu.VMEM((8, TOK, 640), bf16),
            pltpu.VMEM((TOK, COLS), bf16),
            pltpu.VMEM((640, COLS), f32),
            pltpu.VMEM((8, ROWS, COLS), f32),
            pltpu.VMEM((8, ROWS, COLS), bf16),
            pltpu.VMEM((8, ROWS, COLS), bf16),
            pltpu.VMEM((6, ROWS, COLS), bf16),
            pltpu.VMEM((2, 2, HALF, COLS), bf16),
            pltpu.VMEM((2, 2, ROWS, COLS), bf16),
            pltpu.VMEM((ROWS, COLS), bf16),
            pltpu.VMEM((ROWS, COLS), bf16),
            pltpu.VMEM((ROWS, COLS), f32),
            pltpu.VMEM((ROWS, COLS), f32),
            pltpu.VMEM((ROWS, COLS), f32),
            pltpu.VMEM((COLS, RANK), f32),
            pltpu.VMEM((ROWS, RANK), f32),
            pltpu.VMEM((7, PIECE, RANK), f32),
            pltpu.VMEM((ROWS, RANK), f32),
            pltpu.VMEM((2, ROWS, RANK), f32),
            pltpu.VMEM((RANK, RANK), f32),
            pltpu.VMEM((64, RANK), f32),
            pltpu.VMEM((8, 8, RANK), f32),
            pltpu.VMEM((RANK, RANK), f32),
            pltpu.VMEM((RANK, COLS), f32),
            pltpu.VMEM((64, COLS), f32),
            pltpu.VMEM((8, 8, COLS), f32),
            pltpu.VMEM((2, 4, 4, 2, 16, COLS), f32),
            pltpu.VMEM((RANK, RANK), f32),
            pltpu.SemaphoreType.DMA((12,)),
            pltpu.SemaphoreType.DMA((SEMS,)),
            pltpu.SemaphoreType.DMA((SEMS,)),
        ],
        compiler_params=pltpu.CompilerParams(
            collective_id=0, has_side_effects=True, vmem_limit_bytes=58 << 20),
    )(activations, cotangent, first_moment, second_moment, sketch)
    rebuilt, new_first, new_second = pl.pallas_call(
        rebuild,
        name="rebuild",
        out_shape=(jax.ShapeDtypeStruct((COLS, D), bf16), state, state),
        in_specs=[hbm] * 4,
        out_specs=(hbm,) * 3,
        scratch_shapes=[
            pltpu.VMEM((2 * ROWS, RANK), bf16),
            pltpu.VMEM((4, RANK, 1280), bf16),
            pltpu.VMEM((4, COLS, 1280), bf16),
            pltpu.SemaphoreType.DMA((15,)),
        ],
        compiler_params=pltpu.CompilerParams(vmem_limit_bytes=60 << 20),
    )(basis, coeffs, first, second)
    return new_first, new_second, rebuilt


def solution(mesh):
    placed = (P("fsdp", None), P("fsdp", "roll"), P("fsdp", "roll"), P("fsdp", "roll"), P("roll", None))
    return jax.shard_map(
        local,
        mesh=mesh,
        in_specs=placed,
        out_specs=(P("fsdp", "roll"), P("fsdp", "roll"), P("roll", None)),
        check_vma=False,
    )
```

```python
import functools

import jax
import jax.numpy as jnp
from jax import lax
from jax.experimental import pallas as pl
from jax.experimental.pallas import tpu as pltpu
from jax.sharding import PartitionSpec as P

beta_one = 0.9
beta_two = 0.95
epsilon = 1e-08
hp = lax.Precision.HIGHEST
MESH = pl.DeviceIdType.MESH
f32, bf16 = jnp.float32, jnp.bfloat16
DN0 = (((0,), (0,)), ((), ()))
DN1 = (((1,), (1,)), ((), ()))

D, TOK, RANK = 5120, 1024, 128
COLS = 640
ROWS = 320
XROWS = 128
XHALF = XROWS // 2
HALF = (ROWS - XROWS) // 2
PIECE = ROWS // 8

ORDER = ((2, 1), (2, 0), (1, 1), (3, 1), (1, 0), (3, 0), (0, 1), (0, 0))
SEMS = 112


def looped(total, step, body):
    def one(i, carry):
        body(pl.multiple_of(i * step, step))
        return carry
    lax.fori_loop(0, total // step, one, 0)


def split3(v):
    a = v.astype(bf16).astype(f32); v = v - a
    b = v.astype(bf16).astype(f32)
    return a, b, (v - b).astype(bf16).astype(f32)

def factor_inverse(gram_ref, inv_ref):
    lane = lax.broadcasted_iota(jnp.int32, (8, 128), 1)
    sub = lax.broadcasted_iota(jnp.int32, (8, 128), 0)
    panels = [gram_ref[8 * i:8 * i + 8, :] for i in range(16)]
    for k in range(16):
        panel = panels[k]
        scale = jnp.zeros((8, 128), f32)
        for j in range(8):
            p = 8 * k + j
            col = jnp.broadcast_to(panel[:, p:p + 1], (8, 128))
            pivot = jnp.broadcast_to(col[j:j + 1, :], (8, 128))
            recip = 1.0 / pivot
            scale = jnp.where(sub == j, recip, scale)
            m = jnp.where(sub > j, -col * recip, 0.0)
            row = jnp.broadcast_to(jnp.where(lane[j:j + 1] == p, 1.0, panel[j:j + 1, :]), (8, 128))
            panel = jnp.where((lane == p) & (sub > j), 0.0, panel) + m * row
        panels[k] = panel
        if k < 15:
            inside = (lane >= 8 * k) & (lane < 8 * k + 8)
            ext = jnp.where(inside & (lane - 8 * k > sub), 0.0, panel)
            ext = jnp.where(inside & (lane - 8 * k == sub), 1.0, ext)
            lhs = -panel * scale
            a1, a2, a3 = split3(lhs)
            b1, b2, b3 = split3(ext)
            left = jnp.concatenate([a1, a1, a2, a2, a1, a3], axis=0).astype(bf16)
            right = jnp.concatenate([b1, b2, b1, b2, b3, b1], axis=0).astype(bf16)
            upd = lax.dot_general(left, right, DN0, preferred_element_type=f32)
            for i in range(k + 1, 16):
                panels[i] = jnp.where(inside, 0.0, panels[i]) + upd[8 * i:8 * i + 8, :]
        yield k
    for k in range(16):
        at = lane == sub + 8 * k
        d = jnp.sum(jnp.where(at, panels[k], 0.0), axis=1, keepdims=True)
        m = jnp.where(lane < sub + 8 * k, panels[k], jnp.where(at, 1.0, 0.0))
        inv_ref[8 * k:8 * k + 8, :] = m * lax.rsqrt(d)


def kernel(
    act, cot, first, second, sketch,
    new_first, new_second, coeffs_out, basis_out,
    abuf, cbuf, pbuf, own, psend, crecv, ysend, y1recv, y1x, y2recv, xfsend, xfrecv, xsend, xrecv,
    mbuf, vbuf, dbuf, skbuf, rpart, rrecv, rfull, r_out, gpart, gcrecv, gslots, gfull,
    spart, screcv, sslots, s_out, inverse,
    lsem, ssem, rsem,
):
    f, r = lax.axis_index("fsdp"), lax.axis_index("roll")
    y, xh, c = f // 4, (f // 2) % 2, f % 2
    z, xl = r // 2, r % 2
    q = f // 2

    def dev(y=y, xh=xh, c=c, z=z, xl=xl):
        return {"fsdp": (y * 2 + xh) * 2 + c, "roll": z * 2 + xl}

    sibling = dev(c=1 - c)
    plus, minus = dev(y=(y + 1) % 4), dev(y=(y + 3) % 4)
    across = dev(xh=1 - xh)

    def chip(k):
        other = (q + k) % 8
        return {"fsdp": other * 2 + c, "roll": r}, other

    def roller(k):
        other = (r + k) % 8
        return {"fsdp": f, "roll": other}, other

    def around_x(k):
        other = (xh * 2 + xl + k) % 4
        return dev(xh=other // 2, xl=other % 2)

    used = [0]

    def remote(src, dst, where):
        i = used[0]
        used[0] += 1
        return pltpu.make_async_remote_copy(
            src_ref=src, dst_ref=dst, send_sem=ssem.at[i], recv_sem=rsem.at[i],
            device_id=where, device_id_type=MESH,
        )

    pending = []

    def send(src, dst, where):
        copy = remote(src, dst, where)
        copy.start()
        pending.append(copy)
        return copy

    loads = []
    c_load = pltpu.make_async_copy(cot, cbuf, lsem.at[8])
    c_load.start()
    for k, (dy, dxh) in enumerate(ORDER):
        block = ((y + dy) % 4) * 2 + (xh + dxh) % 2
        load = pltpu.make_async_copy(
            act.at[:, pl.ds(pl.multiple_of(block * 640, 640), 640)], abuf.at[k], lsem.at[k]
        )
        load.start()
        loads.append(load)
    late = [
        pltpu.make_async_copy(first, mbuf, lsem.at[9]),
        pltpu.make_async_copy(second, vbuf, lsem.at[10]),
        pltpu.make_async_copy(sketch, skbuf, lsem.at[11]),
    ]
    for load in late:
        load.start()

    barrier = pltpu.get_barrier_semaphore()
    greeted = [sibling] + [chip(k)[0] for k in range(1, 8)] + [roller(k)[0] for k in range(1, 8)] + [dev(xh=1 - xh, xl=1 - xl)]
    for other in greeted:
        pl.semaphore_signal(barrier, inc=1, device_id=other, device_id_type=MESH)
    c_load.wait()

    mine = pl.multiple_of(c * ROWS, ROWS)
    theirs = pl.multiple_of((1 - c) * ROWS, ROWS)
    halves = []

    def compute(k):
        loads[k].wait()
        pbuf[...] = lax.dot_general(abuf[k], cbuf[...], DN0, preferred_element_type=f32)

        def split(o):
            psend[k, pl.ds(o, 32)] = pbuf[pl.ds(theirs + o, 32)].astype(bf16)
            own[k, pl.ds(o, 32)] = pbuf[pl.ds(mine + o, 32)]
        looped(ROWS, 32, split)
        if k == 0:
            pl.semaphore_wait(barrier, len(greeted))
        halves.append(send(psend.at[k], crecv.at[k], sibling))

    step_one, step_two, first_x, one_x, two_x = {}, {}, {}, {}, {}
    ways = (plus, minus)

    def summed(k, at):
        return own[k, at] + crecv[k, at].astype(f32)

    def post(k):
        dy, dxh = ORDER[k]
        halves[k].wait_recv()
        if dxh == 1:
            def add(o):
                xfsend[dy, pl.ds(o, 32)] = summed(k, pl.ds(o, 32)).astype(bf16)
            looped(XROWS, 32, add)
            first_x[dy] = send(xfsend.at[dy], xfrecv.at[dy], across)
        if dy == 2:
            def add(o):
                at = pl.ds(XROWS + o, 32)
                ysend[k, at] = summed(k, at).astype(bf16)
            looped(ROWS - XROWS, 32, add)
            for way, where in enumerate(ways):
                step_one[way, dxh] = send(
                    ysend.at[k, pl.ds(XROWS + way * HALF, HALF)], y1recv.at[way, dxh], where)
        elif dy != 0:
            way = 0 if dy == 1 else 1
            alone = XROWS + (1 - way) * HALF

            def add(o):
                at = pl.ds(alone + o, 32)
                ysend[k, at] = summed(k, at).astype(bf16)
            looped(HALF, 32, add)
            step_two[way, dxh, 1] = send(
                ysend.at[k, pl.ds(alone, HALF)], y2recv.at[way, dxh, pl.ds(alone, HALF)], ways[way])

    def accumulate(dxh):
        for way, dy in ((0, 1), (1, 3)):
            k = ORDER.index((dy, dxh))
            step_one[way, dxh].wait_recv()
            start = XROWS + way * HALF

            def add(o):
                at = pl.ds(start + o, 32)
                ysend[k, at] = (summed(k, at) + y1recv[way, dxh, pl.ds(o, 32)].astype(f32)).astype(bf16)
            looped(HALF, 32, add)
            step_two[way, dxh, 0] = send(
                ysend.at[k, pl.ds(start, HALF)], y2recv.at[way, dxh, pl.ds(start, HALF)], ways[way])

    def crossed(dy):
        k = ORDER.index((dy, 0))
        first_x[dy].wait_recv()
        start, size = {2: (0, XROWS), 1: (XHALF, XHALF), 3: (0, XHALF)}[dy]

        def add(o):
            at = pl.ds(start + o, 32)
            ysend[k, at] = (summed(k, at) + xfrecv[dy, at].astype(f32)).astype(bf16)
        looped(size, 32, add)
        if dy == 2:
            for way, where in enumerate(ways):
                one_x[way] = send(ysend.at[k, pl.ds(way * XHALF, XHALF)], y1x.at[way], where)
        else:
            way = 0 if dy == 1 else 1
            two_x[way, 1] = send(ysend.at[k, pl.ds(start, XHALF)], y2recv.at[way, 0, pl.ds(start, XHALF)], ways[way])

    def crossed_accumulate():
        for way, dy in ((0, 1), (1, 3)):
            k = ORDER.index((dy, 0))
            one_x[way].wait_recv()
            start = way * XHALF

            def add(o):
                at = pl.ds(start + o, 32)
                ysend[k, at] = (summed(k, at) + xfrecv[dy, at].astype(f32)
                                + y1x[way, pl.ds(o, 32)].astype(f32)).astype(bf16)
            looped(XHALF, 32, add)
            two_x[way, 0] = send(ysend.at[k, pl.ds(start, XHALF)], y2recv.at[way, 0, pl.ds(start, XHALF)], ways[way])

    for k in range(8):
        compute(k)
        if k >= 1:
            post(k - 1)
        if k == 4:
            accumulate(1)
        if k == 5:
            crossed(2)
    post(7)
    accumulate(0)
    crossed(1)
    crossed(3)

    crossing = []
    for part in range(2):
        o0 = XROWS + part * HALF
        for way in range(2):
            step_two[way, 1, 0 if way == part else 1].wait_recv()

        def add(o):
            at = pl.ds(o0 + o, 32)
            xsend[pl.ds(part * HALF + o, 32)] = (
                summed(6, at) + y2recv[0, 1, at].astype(f32) + y2recv[1, 1, at].astype(f32)).astype(bf16)
        looped(HALF, 32, add)
        crossing.append(send(xsend.at[pl.ds(part * HALF, HALF)], xrecv.at[pl.ds(part * HALF, HALF)], across))
        if part == 0:
            crossed_accumulate()
    for load in late:
        load.wait()

    def adam(at, far):
        grad = summed(7, at) + y2recv[0, 0, at].astype(f32) + y2recv[1, 0, at].astype(f32) + far
        new_m = beta_one * mbuf[at] + (1.0 - beta_one) * grad
        new_v = beta_two * vbuf[at] + (1.0 - beta_two) * grad * grad
        mbuf[at] = new_m
        vbuf[at] = new_v
        dbuf[at] = new_m / (1.0 - beta_one**20) / (jnp.sqrt(new_v / (1.0 - beta_two**20)) + epsilon)

    stores = []
    first_x[0].wait_recv()
    for way in range(2):
        for part in range(2):
            two_x[way, part].wait_recv()
    looped(XROWS, 16, lambda o: adam(pl.ds(o, 16), xfrecv[0, pl.ds(o, 16)].astype(f32)))
    for part in range(2):
        for way in range(2):
            step_two[way, 0, 0 if way == part else 1].wait_recv()
        crossing[part].wait_recv()
        o0 = part * HALF
        looped(HALF, 16, lambda o: adam(pl.ds(XROWS + o0 + o, 16), xrecv[pl.ds(o0 + o, 16)].astype(f32)))
    for i, (src, dst) in enumerate(((mbuf, new_first), (vbuf, new_second))):
        store = pltpu.make_async_copy(src, dst, lsem.at[i])
        store.start()
        stores.append(store)

    rpart[...] = jnp.dot(dbuf[...], skbuf[...], precision=hp, preferred_element_type=f32)
    parts = []
    for k in range(1, 8):
        where, other = roller(k)
        parts.append(send(rpart.at[pl.ds(pl.multiple_of(other * PIECE, 8), PIECE)], rrecv.at[k - 1], where))
    my_piece = pl.ds(pl.multiple_of(r * PIECE, 8), PIECE)
    total = rpart[my_piece]
    for k in range(7):
        parts[k].wait_recv()
        total = total + rrecv[k]
    rfull[my_piece] = total
    parts = [send(rfull.at[my_piece], rfull.at[my_piece], roller(k)[0]) for k in range(1, 8)]
    swap = remote(rfull.at[my_piece], r_out.at[c, my_piece], dev(y=z, xh=xl, z=y, xl=xh))
    own_piece = pl.ds(pl.multiple_of(q * PIECE, 8), PIECE)
    swapped = (y != z) | (xh != xl)

    @pl.when(swapped)
    def _():
        swap.start()

    @pl.when(jnp.logical_not(swapped))
    def _():
        r_out[c, own_piece] = rfull[my_piece]
    for part in parts:
        part.wait_recv()

    my_half = pl.ds(pl.multiple_of(c * 64, 64), 64)
    other_half = pl.ds(pl.multiple_of((1 - c) * 64, 64), 64)
    my_rows = pl.ds(pl.multiple_of(c * 64 + q * 8, 8), 8)
    gpart[...] = lax.dot_general(rfull[...], rfull[...], DN0, precision=hp, preferred_element_type=f32)
    gcopy = send(gpart.at[other_half], gcrecv, sibling)
    spart[...] = lax.dot_general(rfull[...], dbuf[...], DN0, precision=hp, preferred_element_type=f32)
    scopy = send(spart.at[other_half], screcv, sibling)

    def scatter(mine, slots):
        sent = []
        for k in range(1, 8):
            where, other = chip(k)
            sent.append(send(mine.at[pl.ds(pl.multiple_of(c * 64 + other * 8, 8), 8)], slots.at[q], where))
        slots[q] = mine[my_rows]
        return sent

    def gathered(sent, slots):
        for part in sent:
            part.wait_recv()
        total = slots[0]
        for k in range(1, 8):
            total = total + slots[k]
        return total

    gcopy.wait_recv()
    gpart[my_half] = gpart[my_half] + gcrecv[...]
    gsent = scatter(gpart, gslots)
    scopy.wait_recv()
    spart[my_half] = spart[my_half] + screcv[...]
    ssent = scatter(spart, sslots)
    gfull[my_rows] = gathered(gsent, gslots)
    gsent = [send(gfull.at[my_rows], gfull.at[my_rows], chip(k)[0]) for k in range(1, 8)]

    @pl.when(swapped)
    def _():
        swap.wait_recv()
    rsent = [send(r_out.at[c, own_piece], r_out.at[c, own_piece], chip(k)[0]) for k in range(1, 8)]

    s, t = c * y + (1 - c) * z, c * z + (1 - c) * y
    row = pl.ds(pl.multiple_of(xh * 8, 8), 8)
    s_out[c, s, t, xl, row] = gathered(ssent, sslots)
    ssent = [send(s_out.at[c, s, t, xl, row], s_out.at[c, s, t, xl, row], around_x(k)) for k in range(1, 4)]
    for part in gsent:
        part.wait_recv()
    gcopy = send(gfull.at[my_half], gfull.at[my_half], sibling)

    def along_t(k):
        return dev(y=(y + (1 - c) * k) % 4, z=(z + c * k) % 4)

    def along_s(k):
        return dev(y=(y + c * k) % 4, z=(z + (1 - c) * k) % 4)

    gcopy.wait_recv()
    steps = factor_inverse(gfull, inverse)
    next(steps)
    for part in ssent:
        part.wait_recv()
    ssent = [send(s_out.at[c, s, t], s_out.at[c, s, t], along_t(k)) for k in (1, 3, 2)]
    for _ in range(4):
        next(steps)
    for part in ssent:
        part.wait_recv()
    ssent = [send(s_out.at[c, s], s_out.at[c, s], along_s(k)) for k in (1, 3, 2)]
    copies = [send(s_out.at[c, s], s_out.at[c, s], sibling)]
    for _ in range(2):
        next(steps)
    for part in rsent:
        part.wait_recv()
    rcopy = send(r_out.at[c], r_out.at[c], sibling)
    for k, part in zip((1, 3, 2), ssent):
        for _ in range(3):
            next(steps)
        part.wait_recv()
        have = (s + 4 - k) % 4
        copies.append(send(s_out.at[c, have], s_out.at[c, have], sibling))
    for _ in steps:
        pass
    rcopy.wait_recv()
    for core in range(2):
        basis_out[core * ROWS:(core + 1) * ROWS] = lax.dot_general(
            r_out[core], inverse[...], DN1, precision=hp, preferred_element_type=f32).astype(bf16)
    for part in copies:
        part.wait_recv()

    def block(i, carry):
        bz, bxl = i // 2, i % 2
        rows = [s_out[0, bz, by, bxl] for by in range(4)] + [s_out[1, by, bz, bxl] for by in range(4)]
        coeffs_out[:, pl.ds(pl.multiple_of(i * COLS, COLS), COLS)] = jnp.dot(
            inverse[...], jnp.concatenate(rows, axis=0), precision=hp, preferred_element_type=f32).astype(bf16)
        return carry
    lax.fori_loop(0, 8, block, 0)

    for part in pending:
        part.wait_send()

    @pl.when(swapped)
    def _():
        swap.wait_send()
    for store in stores:
        store.wait()


def rebuild(basis, coeffs, first, second, rebuilt, new_first, new_second, bbuf, cbuf, obuf, state, sem):
    copies = [pltpu.make_async_copy(basis, bbuf, sem.at[2])]
    copies += [pltpu.make_async_copy(coeffs.at[:, pl.ds(i * 1280, 1280)], cbuf.at[i], sem.at[3 + i]) for i in range(4)]
    moved = [pltpu.make_async_copy(first, state.at[0], sem.at[0]), pltpu.make_async_copy(second, state.at[1], sem.at[1])]
    for copy in copies + moved:
        copy.start()
    kept = []
    copies[0].wait()
    for i in range(4):
        copies[1 + i].wait()
        columns = pl.ds(i * 1280, 1280)
        for j in range(2):
            rows = pl.ds(j * ROWS, ROWS)
            obuf[i, rows] = jnp.dot(bbuf[rows], cbuf[i], preferred_element_type=f32).astype(bf16)
            copy = pltpu.make_async_copy(obuf.at[i, rows], rebuilt.at[rows, columns], sem.at[7 + 2 * i + j])
            copy.start()
            kept.append(copy)
        if i < 2:
            moved[i].wait()
            copy = pltpu.make_async_copy(state.at[i], (new_first, new_second)[i], sem.at[i])
            copy.start()
            kept.append(copy)
    for copy in kept:
        copy.wait()


def local(activations, cotangent, first_moment, second_moment, sketch):
    hbm, vmem = pl.BlockSpec(memory_space=pltpu.HBM), pl.BlockSpec(memory_space=pltpu.VMEM)
    state = jax.ShapeDtypeStruct((ROWS, COLS), f32)
    first, second, coeffs, basis = pl.pallas_call(
        kernel,
        name="step",
        out_shape=(
            state, state,
            jax.ShapeDtypeStruct((RANK, D), bf16),
            jax.ShapeDtypeStruct((2 * ROWS, RANK), bf16),
        ),
        in_specs=[hbm] * 5,
        out_specs=(hbm, hbm, vmem, vmem),
        scratch_shapes=[
            pltpu.VMEM((8, TOK, 640), bf16),
            pltpu.VMEM((TOK, COLS), bf16),
            pltpu.VMEM((640, COLS), f32),
            pltpu.VMEM((8, ROWS, COLS), f32),
            pltpu.VMEM((8, ROWS, COLS), bf16),
            pltpu.VMEM((8, ROWS, COLS), bf16),
            pltpu.VMEM((6, ROWS, COLS), bf16),
            pltpu.VMEM((2, 2, HALF, COLS), bf16),
            pltpu.VMEM((2, XHALF, COLS), bf16),
            pltpu.VMEM((2, 2, ROWS, COLS), bf16),
            pltpu.VMEM((4, XROWS, COLS), bf16),
            pltpu.VMEM((4, XROWS, COLS), bf16),
            pltpu.VMEM((2 * HALF, COLS), bf16),
            pltpu.VMEM((2 * HALF, COLS), bf16),
            pltpu.VMEM((ROWS, COLS), f32),
            pltpu.VMEM((ROWS, COLS), f32),
            pltpu.VMEM((ROWS, COLS), f32),
            pltpu.VMEM((COLS, RANK), f32),
            pltpu.VMEM((ROWS, RANK), f32),
            pltpu.VMEM((7, PIECE, RANK), f32),
            pltpu.VMEM((ROWS, RANK), f32),
            pltpu.VMEM((2, ROWS, RANK), f32),
            pltpu.VMEM((RANK, RANK), f32),
            pltpu.VMEM((64, RANK), f32),
            pltpu.VMEM((8, 8, RANK), f32),
            pltpu.VMEM((RANK, RANK), f32),
            pltpu.VMEM((RANK, COLS), f32),
            pltpu.VMEM((64, COLS), f32),
            pltpu.VMEM((8, 8, COLS), f32),
            pltpu.VMEM((2, 4, 4, 2, 16, COLS), f32),
            pltpu.VMEM((RANK, RANK), f32),
            pltpu.SemaphoreType.DMA((12,)),
            pltpu.SemaphoreType.DMA((SEMS,)),
            pltpu.SemaphoreType.DMA((SEMS,)),
        ],
        compiler_params=pltpu.CompilerParams(
            collective_id=0, has_side_effects=True, vmem_limit_bytes=58 << 20),
    )(activations, cotangent, first_moment, second_moment, sketch)
    rebuilt, new_first, new_second = pl.pallas_call(
        rebuild,
        name="rebuild",
        out_shape=(jax.ShapeDtypeStruct((COLS, D), bf16), state, state),
        in_specs=[hbm] * 4,
        out_specs=(hbm,) * 3,
        scratch_shapes=[
            pltpu.VMEM((2 * ROWS, RANK), bf16),
            pltpu.VMEM((4, RANK, 1280), bf16),
            pltpu.VMEM((4, COLS, 1280), bf16),
            pltpu.VMEM((2, ROWS, COLS), f32),
            pltpu.SemaphoreType.DMA((15,)),
        ],
        compiler_params=pltpu.CompilerParams(vmem_limit_bytes=60 << 20),
    )(basis, coeffs, first, second)
    return new_first, new_second, rebuilt


def solution(mesh):
    placed = (P("fsdp", None), P("fsdp", "roll"), P("fsdp", "roll"), P("fsdp", "roll"), P("roll", None))
    return jax.shard_map(
        local,
        mesh=mesh,
        in_specs=placed,
        out_specs=(P("fsdp", "roll"), P("fsdp", "roll"), P("roll", None)),
        check_vma=False,
    )
```

```python
import functools

import jax
import jax.numpy as jnp
from jax import lax
from jax.experimental import pallas as pl
from jax.experimental.pallas import tpu as pltpu
from jax.sharding import PartitionSpec as P

beta_one = 0.9
beta_two = 0.95
epsilon = 1e-08
hp = lax.Precision.HIGHEST
MESH = pl.DeviceIdType.MESH
f32, bf16 = jnp.float32, jnp.bfloat16
DN0 = (((0,), (0,)), ((), ()))
DN1 = (((1,), (1,)), ((), ()))

D, TOK, RANK = 5120, 1024, 128
COLS = 640
ROWS = 320
XROWS = 128
XHALF = XROWS // 2
HALF = (ROWS - XROWS) // 2
PIECE = ROWS // 8

ORDER = ((2, 1), (2, 0), (1, 1), (3, 1), (1, 0), (3, 0), (0, 1), (0, 0))
SEMS = 112


def looped(total, step, body):
    def one(i, carry):
        body(pl.multiple_of(i * step, step))
        return carry
    lax.fori_loop(0, total // step, one, 0)


def split3(v):
    a = v.astype(bf16).astype(f32); v = v - a
    b = v.astype(bf16).astype(f32)
    return a, b, (v - b).astype(bf16).astype(f32)

def factor_inverse(gram_ref, inv_ref):
    lane = lax.broadcasted_iota(jnp.int32, (8, 128), 1)
    sub = lax.broadcasted_iota(jnp.int32, (8, 128), 0)
    panels = [gram_ref[8 * i:8 * i + 8, :] for i in range(16)]

    def down(v, j):
        return jnp.broadcast_to(v[j:j + 1, :], (8, 128))

    for k in range(16):
        panel = panels[k]
        last = k == 15
        cols = [jnp.broadcast_to(panel[:, 8 * k + j:8 * k + j + 1], (8, 128)) for j in range(8)]
        if not last:
            ahead = panels[k + 1]
            acols = [jnp.broadcast_to(ahead[:, 8 * k + j:8 * k + j + 1], (8, 128)) for j in range(8)]
        scale = jnp.zeros((8, 128), f32)
        amul = []
        for j in range(8):
            p = 8 * k + j
            recip = 1.0 / down(cols[j], j)
            scale = jnp.where(sub == j, recip, scale)
            m = jnp.where(sub > j, -cols[j] * recip, 0.0)
            row = down(jnp.where(lane == p, 1.0, panel), j)
            panel = jnp.where((lane == p) & (sub > j), 0.0, panel) + m * row
            if not last:
                am = -acols[j] * recip
                amul.append(am)
            for i in range(j + 1, 8):
                u = down(cols[j], i)
                cols[i] = cols[i] + m * u
                if not last:
                    acols[i] = acols[i] + am * u
        panels[k] = panel
        if not last:
            inside = (lane >= 8 * k) & (lane < 8 * k + 8)
            ext = jnp.where(inside & (lane - 8 * k > sub), 0.0, panel)
            ext = jnp.where(inside & (lane - 8 * k == sub), 1.0, ext)
            ahead = jnp.where(inside, 0.0, ahead)
            for j in range(8):
                ahead = ahead + amul[j] * down(ext, j)
            panels[k + 1] = ahead
            if k < 14:
                lhs = -panel * scale
                a1, a2, a3 = split3(lhs)
                b1, b2, b3 = split3(ext)
                left = jnp.concatenate([a1, a1, a2, a2, a1, a3], axis=0).astype(bf16)
                right = jnp.concatenate([b1, b2, b1, b2, b3, b1], axis=0).astype(bf16)
                upd = lax.dot_general(left, right, DN0, preferred_element_type=f32)
                for i in range(k + 2, 16):
                    panels[i] = jnp.where(inside, 0.0, panels[i]) + upd[8 * i:8 * i + 8, :]
        yield k
    for k in range(16):
        at = lane == sub + 8 * k
        d = jnp.sum(jnp.where(at, panels[k], 0.0), axis=1, keepdims=True)
        m = jnp.where(lane < sub + 8 * k, panels[k], jnp.where(at, 1.0, 0.0))
        inv_ref[8 * k:8 * k + 8, :] = m * lax.rsqrt(d)


def kernel(
    act, cot, first, second, sketch,
    new_first, new_second, coeffs_out, basis_out,
    abuf, cbuf, pbuf, own, psend, crecv, ysend, y1recv, y1x, y2recv, xfsend, xfrecv, xsend, xrecv,
    mbuf, vbuf, dbuf, skbuf, rpart, rrecv, rfull, r_out, gpart, gcrecv, gslots, gfull,
    spart, screcv, sslots, s_own, inverse,
    lsem, ssem, rsem,
):
    f, r = lax.axis_index("fsdp"), lax.axis_index("roll")
    y, xh, c = f // 4, (f // 2) % 2, f % 2
    z, xl = r // 2, r % 2
    q = f // 2

    def dev(y=y, xh=xh, c=c, z=z, xl=xl):
        return {"fsdp": (y * 2 + xh) * 2 + c, "roll": z * 2 + xl}

    sibling = dev(c=1 - c)
    plus, minus = dev(y=(y + 1) % 4), dev(y=(y + 3) % 4)
    across = dev(xh=1 - xh)

    def chip(k):
        other = (q + k) % 8
        return {"fsdp": other * 2 + c, "roll": r}, other

    def roller(k):
        other = (r + k) % 8
        return {"fsdp": f, "roll": other}, other

    def around_x(k):
        other = (xh * 2 + xl + k) % 4
        return dev(xh=other // 2, xl=other % 2)

    used = [0]

    def remote(src, dst, where):
        i = used[0]
        used[0] += 1
        return pltpu.make_async_remote_copy(
            src_ref=src, dst_ref=dst, send_sem=ssem.at[i], recv_sem=rsem.at[i],
            device_id=where, device_id_type=MESH,
        )

    pending = []

    def send(src, dst, where):
        copy = remote(src, dst, where)
        copy.start()
        pending.append(copy)
        return copy

    loads = []
    c_load = pltpu.make_async_copy(cot, cbuf, lsem.at[8])
    c_load.start()
    for k, (dy, dxh) in enumerate(ORDER):
        block = ((y + dy) % 4) * 2 + (xh + dxh) % 2
        load = pltpu.make_async_copy(
            act.at[:, pl.ds(pl.multiple_of(block * 640, 640), 640)], abuf.at[k], lsem.at[k]
        )
        load.start()
        loads.append(load)
    late = [
        pltpu.make_async_copy(first, mbuf, lsem.at[9]),
        pltpu.make_async_copy(second, vbuf, lsem.at[10]),
        pltpu.make_async_copy(sketch, skbuf, lsem.at[11]),
    ]
    for load in late:
        load.start()

    barrier = pltpu.get_barrier_semaphore()
    greeted = [sibling] + [chip(k)[0] for k in range(1, 8)] + [roller(k)[0] for k in range(1, 8)] + [dev(xh=1 - xh, xl=1 - xl)]
    for other in greeted:
        pl.semaphore_signal(barrier, inc=1, device_id=other, device_id_type=MESH)
    c_load.wait()

    mine = pl.multiple_of(c * ROWS, ROWS)
    theirs = pl.multiple_of((1 - c) * ROWS, ROWS)
    halves = []

    def compute(k):
        loads[k].wait()
        pbuf[...] = lax.dot_general(abuf[k], cbuf[...], DN0, preferred_element_type=f32)

        def split(o):
            psend[k, pl.ds(o, 32)] = pbuf[pl.ds(theirs + o, 32)].astype(bf16)
            own[k, pl.ds(o, 32)] = pbuf[pl.ds(mine + o, 32)]
        looped(ROWS, 32, split)
        if k == 0:
            pl.semaphore_wait(barrier, len(greeted))
        halves.append(send(psend.at[k], crecv.at[k], sibling))

    step_one, step_two, first_x, one_x, two_x = {}, {}, {}, {}, {}
    ways = (plus, minus)

    def summed(k, at):
        return own[k, at] + crecv[k, at].astype(f32)

    def post(k):
        dy, dxh = ORDER[k]
        halves[k].wait_recv()
        if dxh == 1:
            def add(o):
                xfsend[dy, pl.ds(o, 32)] = summed(k, pl.ds(o, 32)).astype(bf16)
            looped(XROWS, 32, add)
            first_x[dy] = send(xfsend.at[dy], xfrecv.at[dy], across)
        if dy == 2:
            def add(o):
                at = pl.ds(XROWS + o, 32)
                ysend[k, at] = summed(k, at).astype(bf16)
            looped(ROWS - XROWS, 32, add)
            for way, where in enumerate(ways):
                step_one[way, dxh] = send(
                    ysend.at[k, pl.ds(XROWS + way * HALF, HALF)], y1recv.at[way, dxh], where)
        elif dy != 0:
            way = 0 if dy == 1 else 1
            alone = XROWS + (1 - way) * HALF

            def add(o):
                at = pl.ds(alone + o, 32)
                ysend[k, at] = summed(k, at).astype(bf16)
            looped(HALF, 32, add)
            step_two[way, dxh, 1] = send(
                ysend.at[k, pl.ds(alone, HALF)], y2recv.at[way, dxh, pl.ds(alone, HALF)], ways[way])

    def accumulate(dxh):
        for way, dy in ((0, 1), (1, 3)):
            k = ORDER.index((dy, dxh))
            step_one[way, dxh].wait_recv()
            start = XROWS + way * HALF

            def add(o):
                at = pl.ds(start + o, 32)
                ysend[k, at] = (summed(k, at) + y1recv[way, dxh, pl.ds(o, 32)].astype(f32)).astype(bf16)
            looped(HALF, 32, add)
            step_two[way, dxh, 0] = send(
                ysend.at[k, pl.ds(start, HALF)], y2recv.at[way, dxh, pl.ds(start, HALF)], ways[way])

    def crossed(dy):
        k = ORDER.index((dy, 0))
        first_x[dy].wait_recv()
        start, size = {2: (0, XROWS), 1: (XHALF, XHALF), 3: (0, XHALF)}[dy]

        def add(o):
            at = pl.ds(start + o, 32)
            ysend[k, at] = (summed(k, at) + xfrecv[dy, at].astype(f32)).astype(bf16)
        looped(size, 32, add)
        if dy == 2:
            for way, where in enumerate(ways):
                one_x[way] = send(ysend.at[k, pl.ds(way * XHALF, XHALF)], y1x.at[way], where)
        else:
            way = 0 if dy == 1 else 1
            two_x[way, 1] = send(ysend.at[k, pl.ds(start, XHALF)], y2recv.at[way, 0, pl.ds(start, XHALF)], ways[way])

    def crossed_accumulate():
        for way, dy in ((0, 1), (1, 3)):
            k = ORDER.index((dy, 0))
            one_x[way].wait_recv()
            start = way * XHALF

            def add(o):
                at = pl.ds(start + o, 32)
                ysend[k, at] = (summed(k, at) + xfrecv[dy, at].astype(f32)
                                + y1x[way, pl.ds(o, 32)].astype(f32)).astype(bf16)
            looped(XHALF, 32, add)
            two_x[way, 0] = send(ysend.at[k, pl.ds(start, XHALF)], y2recv.at[way, 0, pl.ds(start, XHALF)], ways[way])

    for k in range(8):
        compute(k)
        if k >= 1:
            post(k - 1)
        if k == 4:
            accumulate(1)
        if k == 5:
            crossed(2)
    post(7)
    accumulate(0)
    crossed(1)
    crossed(3)

    crossing = []
    for part in range(2):
        o0 = XROWS + part * HALF
        for way in range(2):
            step_two[way, 1, 0 if way == part else 1].wait_recv()

        def add(o):
            at = pl.ds(o0 + o, 32)
            xsend[pl.ds(part * HALF + o, 32)] = (
                summed(6, at) + y2recv[0, 1, at].astype(f32) + y2recv[1, 1, at].astype(f32)).astype(bf16)
        looped(HALF, 32, add)
        crossing.append(send(xsend.at[pl.ds(part * HALF, HALF)], xrecv.at[pl.ds(part * HALF, HALF)], across))
        if part == 0:
            crossed_accumulate()
    for load in late:
        load.wait()

    def adam(at, far):
        grad = summed(7, at) + y2recv[0, 0, at].astype(f32) + y2recv[1, 0, at].astype(f32) + far
        new_m = beta_one * mbuf[at] + (1.0 - beta_one) * grad
        new_v = beta_two * vbuf[at] + (1.0 - beta_two) * grad * grad
        mbuf[at] = new_m
        vbuf[at] = new_v
        dbuf[at] = new_m / (1.0 - beta_one**20) / (jnp.sqrt(new_v / (1.0 - beta_two**20)) + epsilon)

    stores = []
    first_x[0].wait_recv()
    for way in range(2):
        for part in range(2):
            two_x[way, part].wait_recv()
    looped(XROWS, 16, lambda o: adam(pl.ds(o, 16), xfrecv[0, pl.ds(o, 16)].astype(f32)))
    for part in range(2):
        for way in range(2):
            step_two[way, 0, 0 if way == part else 1].wait_recv()
        crossing[part].wait_recv()
        o0 = part * HALF
        looped(HALF, 16, lambda o: adam(pl.ds(XROWS + o0 + o, 16), xrecv[pl.ds(o0 + o, 16)].astype(f32)))
    for i, (src, dst) in enumerate(((mbuf, new_first), (vbuf, new_second))):
        store = pltpu.make_async_copy(src, dst, lsem.at[i])
        store.start()
        stores.append(store)

    rpart[...] = jnp.dot(dbuf[...], skbuf[...], precision=hp, preferred_element_type=f32)
    parts = []
    for k in range(1, 8):
        where, other = roller(k)
        parts.append(send(rpart.at[pl.ds(pl.multiple_of(other * PIECE, 8), PIECE)], rrecv.at[k - 1], where))
    my_piece = pl.ds(pl.multiple_of(r * PIECE, 8), PIECE)
    total = rpart[my_piece]
    for k in range(7):
        parts[k].wait_recv()
        total = total + rrecv[k]
    rfull[my_piece] = total
    parts = [send(rfull.at[my_piece], rfull.at[my_piece], roller(k)[0]) for k in range(1, 8)]
    swap = remote(rfull.at[my_piece], r_out.at[c, my_piece], dev(y=z, xh=xl, z=y, xl=xh))
    own_piece = pl.ds(pl.multiple_of(q * PIECE, 8), PIECE)
    swapped = (y != z) | (xh != xl)

    @pl.when(swapped)
    def _():
        swap.start()

    @pl.when(jnp.logical_not(swapped))
    def _():
        r_out[c, own_piece] = rfull[my_piece]
    for part in parts:
        part.wait_recv()

    my_half = pl.ds(pl.multiple_of(c * 64, 64), 64)
    other_half = pl.ds(pl.multiple_of((1 - c) * 64, 64), 64)
    my_rows = pl.ds(pl.multiple_of(c * 64 + q * 8, 8), 8)
    gpart[...] = lax.dot_general(rfull[...], rfull[...], DN0, precision=hp, preferred_element_type=f32)
    gcopy = send(gpart.at[other_half], gcrecv, sibling)
    spart[...] = lax.dot_general(dbuf[...], rfull[...], DN0, precision=hp, preferred_element_type=f32)
    scopy = send(spart.at[pl.ds(theirs, ROWS)], screcv, sibling)

    def scatter(part, slots, rows):
        def piece(i):
            return pl.ds(pl.multiple_of((c * 8 + i) * rows, 8), rows)
        sent = []
        for k in range(1, 8):
            where, other = chip(k)
            sent.append(send(part.at[piece(other)], slots.at[q], where))
        slots[q] = part[piece(q)]
        return sent

    def gathered(sent, slots):
        for part in sent:
            part.wait_recv()
        total = slots[0]
        for k in range(1, 8):
            total = total + slots[k]
        return total

    gcopy.wait_recv()
    gpart[my_half] = gpart[my_half] + gcrecv[...]
    gsent = scatter(gpart, gslots, 8)
    scopy.wait_recv()
    spart[pl.ds(mine, ROWS)] = spart[pl.ds(mine, ROWS)] + screcv[...]
    ssent = scatter(spart, sslots, PIECE)
    gfull[my_rows] = gathered(gsent, gslots)
    gsent = [send(gfull.at[my_rows], gfull.at[my_rows], chip(k)[0]) for k in range(1, 8)]

    @pl.when(swapped)
    def _():
        swap.wait_recv()
    rsent = [send(r_out.at[c, own_piece], r_out.at[c, own_piece], chip(k)[0]) for k in range(1, 8)]

    s, t = c * y + (1 - c) * z, c * z + (1 - c) * y
    at = pl.ds(pl.multiple_of(xh * PIECE, 8), PIECE)
    s_own[t, xl, at] = gathered(ssent, sslots)
    ssent = [send(s_own.at[t, xl, at], s_own.at[t, xl, at], around_x(k)) for k in range(1, 4)]
    for part in gsent:
        part.wait_recv()
    gcopy = send(gfull.at[my_half], gfull.at[my_half], sibling)

    def along_t(k):
        return dev(y=(y + (1 - c) * k) % 4, z=(z + c * k) % 4)

    def along_s(k):
        return dev(y=(y + c * k) % 4, z=(z + (1 - c) * k) % 4)

    gcopy.wait_recv()
    steps = factor_inverse(gfull, inverse)
    for _ in range(4):
        next(steps)
    for part in ssent:
        part.wait_recv()
    ssent = [send(s_own.at[t], s_own.at[t], along_t(k)) for k in (1, 3, 2)]
    for _ in steps:
        pass
    for part in rsent:
        part.wait_recv()
    rcopy = send(r_out.at[c], r_out.at[c], sibling)
    for part in ssent:
        part.wait_recv()
    coeffs = lax.dot_general(
        s_own[...].reshape(COLS, RANK), inverse[...], DN1, precision=hp, preferred_element_type=f32)
    coeffs_out[c, s] = coeffs.reshape(4, 2, 2 * PIECE, RANK).astype(bf16)
    ssent = [send(coeffs_out.at[c, s], coeffs_out.at[c, s], along_s(k)) for k in (1, 3, 2)]
    copies = [send(coeffs_out.at[c, s], coeffs_out.at[c, s], sibling)]
    rcopy.wait_recv()
    for core in range(2):
        basis_out[core * ROWS:(core + 1) * ROWS] = lax.dot_general(
            r_out[core], inverse[...], DN1, precision=hp, preferred_element_type=f32).astype(bf16)
    for k, part in zip((1, 3, 2), ssent):
        part.wait_recv()
        have = (s + 4 - k) % 4
        copies.append(send(coeffs_out.at[c, have], coeffs_out.at[c, have], sibling))
    for part in copies:
        part.wait_recv()

    for part in pending:
        part.wait_send()

    @pl.when(swapped)
    def _():
        swap.wait_send()
    for store in stores:
        store.wait()


def rebuild(basis, coeffs, first, second, rebuilt, new_first, new_second, bbuf, cbuf, obuf, state, sem):
    copies = [pltpu.make_async_copy(basis, bbuf, sem.at[2])]
    copies += [pltpu.make_async_copy(coeffs.at[0, i], cbuf.at[i, 0], sem.at[3 + i]) for i in range(4)]
    copies += [pltpu.make_async_copy(coeffs.at[1, :, i], cbuf.at[i, 1], sem.at[15 + i]) for i in range(4)]
    moved = [pltpu.make_async_copy(first, state.at[0], sem.at[0]), pltpu.make_async_copy(second, state.at[1], sem.at[1])]
    for copy in copies + moved:
        copy.start()
    kept = []
    copies[0].wait()
    for i in range(4):
        copies[1 + i].wait()
        copies[5 + i].wait()
        for j in range(2):
            block = jnp.concatenate([cbuf[i, core, k, j] for core in range(2) for k in range(4)], axis=0)
            obuf[2 * i + j] = lax.dot_general(bbuf[...], block, DN1, preferred_element_type=f32).astype(bf16)
            copy = pltpu.make_async_copy(obuf.at[2 * i + j], rebuilt.at[:, pl.ds((2 * i + j) * COLS, COLS)], sem.at[7 + 2 * i + j])
            copy.start()
            kept.append(copy)
        if i < 2:
            moved[i].wait()
            copy = pltpu.make_async_copy(state.at[i], (new_first, new_second)[i], sem.at[i])
            copy.start()
            kept.append(copy)
    for copy in kept:
        copy.wait()


def local(activations, cotangent, first_moment, second_moment, sketch):
    hbm, vmem = pl.BlockSpec(memory_space=pltpu.HBM), pl.BlockSpec(memory_space=pltpu.VMEM)
    state = jax.ShapeDtypeStruct((ROWS, COLS), f32)
    first, second, coeffs, basis = pl.pallas_call(
        kernel,
        name="step",
        out_shape=(
            state, state,
            jax.ShapeDtypeStruct((2, 4, 4, 2, 2 * PIECE, RANK), bf16),
            jax.ShapeDtypeStruct((2 * ROWS, RANK), bf16),
        ),
        in_specs=[hbm] * 5,
        out_specs=(hbm, hbm, vmem, vmem),
        scratch_shapes=[
            pltpu.VMEM((8, TOK, 640), bf16),
            pltpu.VMEM((TOK, COLS), bf16),
            pltpu.VMEM((640, COLS), f32),
            pltpu.VMEM((8, ROWS, COLS), f32),
            pltpu.VMEM((8, ROWS, COLS), bf16),
            pltpu.VMEM((8, ROWS, COLS), bf16),
            pltpu.VMEM((6, ROWS, COLS), bf16),
            pltpu.VMEM((2, 2, HALF, COLS), bf16),
            pltpu.VMEM((2, XHALF, COLS), bf16),
            pltpu.VMEM((2, 2, ROWS, COLS), bf16),
            pltpu.VMEM((4, XROWS, COLS), bf16),
            pltpu.VMEM((4, XROWS, COLS), bf16),
            pltpu.VMEM((2 * HALF, COLS), bf16),
            pltpu.VMEM((2 * HALF, COLS), bf16),
            pltpu.VMEM((ROWS, COLS), f32),
            pltpu.VMEM((ROWS, COLS), f32),
            pltpu.VMEM((ROWS, COLS), f32),
            pltpu.VMEM((COLS, RANK), f32),
            pltpu.VMEM((ROWS, RANK), f32),
            pltpu.VMEM((7, PIECE, RANK), f32),
            pltpu.VMEM((ROWS, RANK), f32),
            pltpu.VMEM((2, ROWS, RANK), f32),
            pltpu.VMEM((RANK, RANK), f32),
            pltpu.VMEM((64, RANK), f32),
            pltpu.VMEM((8, 8, RANK), f32),
            pltpu.VMEM((RANK, RANK), f32),
            pltpu.VMEM((COLS, RANK), f32),
            pltpu.VMEM((ROWS, RANK), f32),
            pltpu.VMEM((8, PIECE, RANK), f32),
            pltpu.VMEM((4, 2, 2 * PIECE, RANK), f32),
            pltpu.VMEM((RANK, RANK), f32),
            pltpu.SemaphoreType.DMA((12,)),
            pltpu.SemaphoreType.DMA((SEMS,)),
            pltpu.SemaphoreType.DMA((SEMS,)),
        ],
        compiler_params=pltpu.CompilerParams(
            collective_id=0, has_side_effects=True, vmem_limit_bytes=58 << 20),
    )(activations, cotangent, first_moment, second_moment, sketch)
    rebuilt, new_first, new_second = pl.pallas_call(
        rebuild,
        name="rebuild",
        out_shape=(jax.ShapeDtypeStruct((COLS, D), bf16), state, state),
        in_specs=[hbm] * 4,
        out_specs=(hbm,) * 3,
        scratch_shapes=[
            pltpu.VMEM((2 * ROWS, RANK), bf16),
            pltpu.VMEM((4, 2, 4, 2, 2 * PIECE, RANK), bf16),
            pltpu.VMEM((8, COLS, COLS), bf16),
            pltpu.VMEM((2, ROWS, COLS), f32),
            pltpu.SemaphoreType.DMA((19,)),
        ],
        compiler_params=pltpu.CompilerParams(vmem_limit_bytes=60 << 20),
    )(basis, coeffs, first, second)
    return new_first, new_second, rebuilt


def solution(mesh):
    placed = (P("fsdp", None), P("fsdp", "roll"), P("fsdp", "roll"), P("fsdp", "roll"), P("roll", None))
    return jax.shard_map(
        local,
        mesh=mesh,
        in_specs=placed,
        out_specs=(P("fsdp", "roll"), P("fsdp", "roll"), P("roll", None)),
        check_vma=False,
    )
```

```python
import functools

import jax
import jax.numpy as jnp
from jax import lax
from jax.experimental import pallas as pl
from jax.experimental.pallas import tpu as pltpu
from jax.sharding import PartitionSpec as P

beta_one = 0.9
beta_two = 0.95
epsilon = 1e-08
hp = lax.Precision.HIGHEST
MESH = pl.DeviceIdType.MESH
f32, bf16 = jnp.float32, jnp.bfloat16
DN0 = (((0,), (0,)), ((), ()))
DN1 = (((1,), (1,)), ((), ()))

D, TOK, RANK = 5120, 1024, 128
COLS = 640
ROWS = 320
XROWS = 128
XHALF = XROWS // 2
HALF = (ROWS - XROWS) // 2
PIECE = ROWS // 8
FAR_FIRST = (3, 5, 4, 1, 7, 2, 6)

ORDER = ((2, 1), (2, 0), (1, 1), (3, 1), (1, 0), (3, 0), (0, 1), (0, 0))
SEMS = 112


def looped(total, step, body):
    def one(i, carry):
        body(pl.multiple_of(i * step, step))
        return carry
    lax.fori_loop(0, total // step, one, 0, unroll=True)


def split3(v):
    a = v.astype(bf16).astype(f32); v = v - a
    b = v.astype(bf16).astype(f32)
    return a, b, (v - b).astype(bf16).astype(f32)

def factor_inverse(gram_ref, inv_ref):
    lane = lax.broadcasted_iota(jnp.int32, (8, 128), 1)
    sub = lax.broadcasted_iota(jnp.int32, (8, 128), 0)
    panels = [gram_ref[8 * i:8 * i + 8, :] for i in range(16)]

    def down(v, j):
        return jnp.broadcast_to(v[j:j + 1, :], (8, 128))

    for k in range(16):
        panel = panels[k]
        last = k == 15
        cols = [jnp.broadcast_to(panel[:, 8 * k + j:8 * k + j + 1], (8, 128)) for j in range(8)]
        if not last:
            ahead = panels[k + 1]
            acols = [jnp.broadcast_to(ahead[:, 8 * k + j:8 * k + j + 1], (8, 128)) for j in range(8)]
        scale = jnp.zeros((8, 128), f32)
        amul = []
        for j in range(8):
            p = 8 * k + j
            recip = 1.0 / down(cols[j], j)
            scale = jnp.where(sub == j, recip, scale)
            m = jnp.where(sub > j, -cols[j] * recip, 0.0)
            row = down(jnp.where(lane == p, 1.0, panel), j)
            panel = jnp.where((lane == p) & (sub > j), 0.0, panel) + m * row
            if not last:
                am = -acols[j] * recip
                amul.append(am)
            for i in range(j + 1, 8):
                u = down(cols[j], i)
                cols[i] = cols[i] + m * u
                if not last:
                    acols[i] = acols[i] + am * u
        panels[k] = panel
        if not last:
            inside = (lane >= 8 * k) & (lane < 8 * k + 8)
            ext = jnp.where(inside & (lane - 8 * k > sub), 0.0, panel)
            ext = jnp.where(inside & (lane - 8 * k == sub), 1.0, ext)
            ahead = jnp.where(inside, 0.0, ahead)
            for j in range(8):
                ahead = ahead + amul[j] * down(ext, j)
            panels[k + 1] = ahead
            if k < 14:
                lhs = -panel * scale
                a1, a2, a3 = split3(lhs)
                b1, b2, b3 = split3(ext)
                left = jnp.concatenate([a1, a1, a2, a2, a1, a3], axis=0).astype(bf16)
                right = jnp.concatenate([b1, b2, b1, b2, b3, b1], axis=0).astype(bf16)
                upd = lax.dot_general(left, right, DN0, preferred_element_type=f32)
                for i in range(k + 2, 16):
                    panels[i] = jnp.where(inside, 0.0, panels[i]) + upd[8 * i:8 * i + 8, :]
        yield k
    for k in range(16):
        at = lane == sub + 8 * k
        d = jnp.sum(jnp.where(at, panels[k], 0.0), axis=1, keepdims=True)
        m = jnp.where(lane < sub + 8 * k, panels[k], jnp.where(at, 1.0, 0.0))
        inv_ref[8 * k:8 * k + 8, :] = m * lax.rsqrt(d)


def kernel(
    act, cot, first, second, sketch,
    new_first, new_second, coeffs_out, basis_out,
    abuf, cbuf, pbuf, own, psend, crecv, ysend, y1recv, y1x, y2recv, xfsend, xfrecv, xsend, xrecv,
    mbuf, vbuf, dbuf, skbuf, rpart, rrecv, rfull, r_out, gpart, gcrecv, gslots, gfull,
    spart, screcv, sslots, s_own, inverse,
    lsem, ssem, rsem,
):
    f, r = lax.axis_index("fsdp"), lax.axis_index("roll")
    y, xh, c = f // 4, (f // 2) % 2, f % 2
    z, xl = r // 2, r % 2
    q = f // 2

    def dev(y=y, xh=xh, c=c, z=z, xl=xl):
        return {"fsdp": (y * 2 + xh) * 2 + c, "roll": z * 2 + xl}

    sibling = dev(c=1 - c)
    plus, minus = dev(y=(y + 1) % 4), dev(y=(y + 3) % 4)
    across = dev(xh=1 - xh)

    def chip(k):
        other = (q + k) % 8
        return {"fsdp": other * 2 + c, "roll": r}, other

    def roller(k):
        other = (r + k) % 8
        return {"fsdp": f, "roll": other}, other

    def around_x(k):
        other = (xh * 2 + xl + k) % 4
        return dev(xh=other // 2, xl=other % 2)

    used = [0]

    def remote(src, dst, where):
        i = used[0]
        used[0] += 1
        return pltpu.make_async_remote_copy(
            src_ref=src, dst_ref=dst, send_sem=ssem.at[i], recv_sem=rsem.at[i],
            device_id=where, device_id_type=MESH,
        )

    pending = []

    def send(src, dst, where):
        copy = remote(src, dst, where)
        copy.start()
        pending.append(copy)
        return copy

    def drain(keep=0):
        while len(pending) > keep:
            pending.pop(0).wait_send()

    loads = []
    c_load = pltpu.make_async_copy(cot, cbuf, lsem.at[8])
    c_load.start()
    for k, (dy, dxh) in enumerate(ORDER):
        block = ((y + dy) % 4) * 2 + (xh + dxh) % 2
        load = pltpu.make_async_copy(
            act.at[:, pl.ds(pl.multiple_of(block * 640, 640), 640)], abuf.at[k], lsem.at[k]
        )
        load.start()
        loads.append(load)
    late = [
        pltpu.make_async_copy(first, mbuf, lsem.at[9]),
        pltpu.make_async_copy(second, vbuf, lsem.at[10]),
        pltpu.make_async_copy(sketch, skbuf, lsem.at[11]),
    ]
    for load in late:
        load.start()

    barrier = pltpu.get_barrier_semaphore()
    greeted = [sibling] + [chip(k)[0] for k in range(1, 8)] + [roller(k)[0] for k in range(1, 8)] + [dev(xh=1 - xh, xl=1 - xl)]
    for other in greeted:
        pl.semaphore_signal(barrier, inc=1, device_id=other, device_id_type=MESH)
    c_load.wait()

    mine = pl.multiple_of(c * ROWS, ROWS)
    theirs = pl.multiple_of((1 - c) * ROWS, ROWS)
    halves = []

    def compute(k):
        loads[k].wait()
        pbuf[...] = lax.dot_general(abuf[k], cbuf[...], DN0, preferred_element_type=f32)

        def split(o):
            psend[k, pl.ds(o, 32)] = pbuf[pl.ds(theirs + o, 32)].astype(bf16)
            own[k, pl.ds(o, 32)] = pbuf[pl.ds(mine + o, 32)]
        looped(ROWS, 32, split)
        if k == 0:
            pl.semaphore_wait(barrier, len(greeted))
        halves.append(send(psend.at[k], crecv.at[k], sibling))

    step_one, step_two, first_x, one_x, two_x = {}, {}, {}, {}, {}
    ways = (plus, minus)

    def summed(k, at):
        return own[k, at] + crecv[k, at].astype(f32)

    def post(k):
        dy, dxh = ORDER[k]
        halves[k].wait_recv()
        if dxh == 1:
            def add(o):
                xfsend[dy, pl.ds(o, 32)] = summed(k, pl.ds(o, 32)).astype(bf16)
            looped(XROWS, 32, add)
            first_x[dy] = send(xfsend.at[dy], xfrecv.at[dy], across)
        if dy == 2:
            def add(o):
                at = pl.ds(XROWS + o, 32)
                ysend[k, at] = summed(k, at).astype(bf16)
            looped(ROWS - XROWS, 32, add)
            for way, where in enumerate(ways):
                step_one[way, dxh] = send(
                    ysend.at[k, pl.ds(XROWS + way * HALF, HALF)], y1recv.at[way, dxh], where)
        elif dy != 0:
            way = 0 if dy == 1 else 1
            alone = XROWS + (1 - way) * HALF

            def add(o):
                at = pl.ds(alone + o, 32)
                ysend[k, at] = summed(k, at).astype(bf16)
            looped(HALF, 32, add)
            step_two[way, dxh, 1] = send(
                ysend.at[k, pl.ds(alone, HALF)], y2recv.at[way, dxh, pl.ds(alone, HALF)], ways[way])

    def accumulate(dxh):
        for way, dy in ((0, 1), (1, 3)):
            k = ORDER.index((dy, dxh))
            step_one[way, dxh].wait_recv()
            start = XROWS + way * HALF

            def add(o):
                at = pl.ds(start + o, 32)
                ysend[k, at] = (summed(k, at) + y1recv[way, dxh, pl.ds(o, 32)].astype(f32)).astype(bf16)
            looped(HALF, 32, add)
            step_two[way, dxh, 0] = send(
                ysend.at[k, pl.ds(start, HALF)], y2recv.at[way, dxh, pl.ds(start, HALF)], ways[way])

    def crossed(dy):
        k = ORDER.index((dy, 0))
        first_x[dy].wait_recv()
        start, size = {2: (0, XROWS), 1: (XHALF, XHALF), 3: (0, XHALF)}[dy]

        def add(o):
            at = pl.ds(start + o, 32)
            ysend[k, at] = (summed(k, at) + xfrecv[dy, at].astype(f32)).astype(bf16)
        looped(size, 32, add)
        if dy == 2:
            for way, where in enumerate(ways):
                one_x[way] = send(ysend.at[k, pl.ds(way * XHALF, XHALF)], y1x.at[way], where)
        else:
            way = 0 if dy == 1 else 1
            two_x[way, 1] = send(ysend.at[k, pl.ds(start, XHALF)], y2recv.at[way, 0, pl.ds(start, XHALF)], ways[way])

    def crossed_accumulate():
        for way, dy in ((0, 1), (1, 3)):
            k = ORDER.index((dy, 0))
            one_x[way].wait_recv()
            start = way * XHALF

            def add(o):
                at = pl.ds(start + o, 32)
                ysend[k, at] = (summed(k, at) + xfrecv[dy, at].astype(f32)
                                + y1x[way, pl.ds(o, 32)].astype(f32)).astype(bf16)
            looped(XHALF, 32, add)
            two_x[way, 0] = send(ysend.at[k, pl.ds(start, XHALF)], y2recv.at[way, 0, pl.ds(start, XHALF)], ways[way])

    for k in range(8):
        compute(k)
        if k >= 1:
            post(k - 1)
        if k == 4:
            accumulate(1)
        if k == 5:
            crossed(2)
    post(7)
    accumulate(0)
    crossed(1)
    crossed(3)

    crossing = []
    for part in range(2):
        o0 = XROWS + part * HALF
        for way in range(2):
            step_two[way, 1, 0 if way == part else 1].wait_recv()

        def add(o):
            at = pl.ds(o0 + o, 32)
            xsend[pl.ds(part * HALF + o, 32)] = (
                summed(6, at) + y2recv[0, 1, at].astype(f32) + y2recv[1, 1, at].astype(f32)).astype(bf16)
        looped(HALF, 32, add)
        crossing.append(send(xsend.at[pl.ds(part * HALF, HALF)], xrecv.at[pl.ds(part * HALF, HALF)], across))
        if part == 0:
            crossed_accumulate()
    for load in late:
        load.wait()

    def adam(at, far):
        grad = summed(7, at) + y2recv[0, 0, at].astype(f32) + y2recv[1, 0, at].astype(f32) + far
        new_m = beta_one * mbuf[at] + (1.0 - beta_one) * grad
        new_v = beta_two * vbuf[at] + (1.0 - beta_two) * grad * grad
        mbuf[at] = new_m
        vbuf[at] = new_v
        dbuf[at] = new_m / (1.0 - beta_one**20) / (jnp.sqrt(new_v / (1.0 - beta_two**20)) + epsilon)

    stores = []
    first_x[0].wait_recv()
    for way in range(2):
        for part in range(2):
            two_x[way, part].wait_recv()
    looped(XROWS, 16, lambda o: adam(pl.ds(o, 16), xfrecv[0, pl.ds(o, 16)].astype(f32)))
    for part in range(2):
        for way in range(2):
            step_two[way, 0, 0 if way == part else 1].wait_recv()
        crossing[part].wait_recv()
        o0 = part * HALF
        looped(HALF, 16, lambda o: adam(pl.ds(XROWS + o0 + o, 16), xrecv[pl.ds(o0 + o, 16)].astype(f32)))
    for i, (src, dst) in enumerate(((mbuf, new_first), (vbuf, new_second))):
        store = pltpu.make_async_copy(src, dst, lsem.at[i])
        store.start()
        stores.append(store)

    rpart[...] = jnp.dot(dbuf[...], skbuf[...], precision=hp, preferred_element_type=f32)
    parts = []
    for k in FAR_FIRST:
        where, other = roller(k)
        parts.append(send(rpart.at[pl.ds(pl.multiple_of(other * PIECE, 8), PIECE)], rrecv.at[k - 1], where))
    my_piece = pl.ds(pl.multiple_of(r * PIECE, 8), PIECE)
    total = rpart[my_piece]
    for part in parts:
        part.wait_recv()
    for k in range(7):
        total = total + rrecv[k]
    rfull[my_piece] = total
    parts = [send(rfull.at[my_piece], rfull.at[my_piece], roller(k)[0]) for k in FAR_FIRST]
    swap = remote(rfull.at[my_piece], r_out.at[c, my_piece], dev(y=z, xh=xl, z=y, xl=xh))
    own_piece = pl.ds(pl.multiple_of(q * PIECE, 8), PIECE)
    swapped = (y != z) | (xh != xl)

    @pl.when(swapped)
    def _():
        swap.start()

    @pl.when(jnp.logical_not(swapped))
    def _():
        r_out[c, own_piece] = rfull[my_piece]
    for part in parts:
        part.wait_recv()

    my_half = pl.ds(pl.multiple_of(c * 64, 64), 64)
    other_half = pl.ds(pl.multiple_of((1 - c) * 64, 64), 64)
    my_rows = pl.ds(pl.multiple_of(c * 64 + q * 8, 8), 8)
    gpart[...] = lax.dot_general(rfull[...], rfull[...], DN0, precision=hp, preferred_element_type=f32)
    gcopy = send(gpart.at[other_half], gcrecv, sibling)
    spart[...] = lax.dot_general(dbuf[...], rfull[...], DN0, precision=hp, preferred_element_type=f32)
    scopy = send(spart.at[pl.ds(theirs, ROWS)], screcv, sibling)

    def scatter(part, slots, rows):
        def piece(i):
            return pl.ds(pl.multiple_of((c * 8 + i) * rows, 8), rows)
        sent = []
        for k in FAR_FIRST:
            where, other = chip(k)
            sent.append(send(part.at[piece(other)], slots.at[q], where))
        slots[q] = part[piece(q)]
        return sent

    def gathered(sent, slots):
        for part in sent:
            part.wait_recv()
        total = slots[0]
        for k in range(1, 8):
            total = total + slots[k]
        return total

    gcopy.wait_recv()
    gpart[my_half] = gpart[my_half] + gcrecv[...]
    gsent = scatter(gpart, gslots, 8)
    scopy.wait_recv()
    spart[pl.ds(mine, ROWS)] = spart[pl.ds(mine, ROWS)] + screcv[...]
    ssent = scatter(spart, sslots, PIECE)
    gfull[my_rows] = gathered(gsent, gslots)
    gsent = [send(gfull.at[my_rows], gfull.at[my_rows], chip(k)[0]) for k in FAR_FIRST]

    @pl.when(swapped)
    def _():
        swap.wait_recv()
    rsent = [send(r_out.at[c, own_piece], r_out.at[c, own_piece], chip(k)[0]) for k in FAR_FIRST]

    s, t = c * y + (1 - c) * z, c * z + (1 - c) * y
    at = pl.ds(pl.multiple_of(xh * PIECE, 8), PIECE)
    s_own[t, xl, at] = gathered(ssent, sslots)
    ssent = [send(s_own.at[t, xl, at], s_own.at[t, xl, at], around_x(k)) for k in (2, 1, 3)]

    def along_t(k):
        return dev(y=(y + (1 - c) * k) % 4, z=(z + c * k) % 4)

    def along_s(k):
        return dev(y=(y + c * k) % 4, z=(z + (1 - c) * k) % 4)

    for part in ssent:
        part.wait_recv()
    ssent = [send(s_own.at[t], s_own.at[t], along_t(k)) for k in (2, 1, 3)]
    for part in gsent:
        part.wait_recv()
    gcopy = send(gfull.at[my_half], gfull.at[my_half], sibling)
    drain(12)
    gcopy.wait_recv()
    for _ in factor_inverse(gfull, inverse):
        pass
    for part in rsent:
        part.wait_recv()
    rcopy = send(r_out.at[c], r_out.at[c], sibling)
    for part in ssent:
        part.wait_recv()
    coeffs = lax.dot_general(
        s_own[...].reshape(COLS, RANK), inverse[...], DN1, precision=hp, preferred_element_type=f32)
    coeffs_out[c, s] = coeffs.reshape(4, 2, 2 * PIECE, RANK).astype(bf16)
    ssent = [send(coeffs_out.at[c, s], coeffs_out.at[c, s], along_s(k)) for k in (2, 1, 3)]
    copies = [send(coeffs_out.at[c, s], coeffs_out.at[c, s], sibling)]
    rcopy.wait_recv()
    for core in range(2):
        basis_out[core * ROWS:(core + 1) * ROWS] = lax.dot_general(
            r_out[core], inverse[...], DN1, precision=hp, preferred_element_type=f32).astype(bf16)

    @pl.when(swapped)
    def _():
        swap.wait_send()
    for store in stores:
        store.wait()
    drain(4)
    for k, part in ((1, ssent[1]), (3, ssent[2]), (2, ssent[0])):
        part.wait_recv()
        have = (s + 4 - k) % 4
        copies.append(send(coeffs_out.at[c, have], coeffs_out.at[c, have], sibling))
    for part in copies:
        part.wait_recv()

    drain()


def rebuild(basis, coeffs, first, second, rebuilt, new_first, new_second, bbuf, cbuf, obuf, state, sem):
    copies = [pltpu.make_async_copy(basis, bbuf, sem.at[2])]
    copies += [pltpu.make_async_copy(coeffs.at[0, i], cbuf.at[i, 0], sem.at[3 + i]) for i in range(4)]
    copies += [pltpu.make_async_copy(coeffs.at[1, :, i], cbuf.at[i, 1], sem.at[15 + i]) for i in range(4)]
    moved = [pltpu.make_async_copy(first, state.at[0], sem.at[0]), pltpu.make_async_copy(second, state.at[1], sem.at[1])]
    for copy in copies + moved:
        copy.start()
    kept = []
    copies[0].wait()
    for i in range(4):
        copies[1 + i].wait()
        copies[5 + i].wait()
        for j in range(2):
            block = jnp.concatenate([cbuf[i, core, k, j] for core in range(2) for k in range(4)], axis=0)
            obuf[2 * i + j] = lax.dot_general(bbuf[...], block, DN1, preferred_element_type=f32).astype(bf16)
            copy = pltpu.make_async_copy(obuf.at[2 * i + j], rebuilt.at[:, pl.ds((2 * i + j) * COLS, COLS)], sem.at[7 + 2 * i + j])
            copy.start()
            kept.append(copy)
        if i < 2:
            moved[i].wait()
            copy = pltpu.make_async_copy(state.at[i], (new_first, new_second)[i], sem.at[i])
            copy.start()
            kept.append(copy)
    for copy in kept:
        copy.wait()


def local(activations, cotangent, first_moment, second_moment, sketch):
    hbm, vmem = pl.BlockSpec(memory_space=pltpu.HBM), pl.BlockSpec(memory_space=pltpu.VMEM)
    state = jax.ShapeDtypeStruct((ROWS, COLS), f32)
    first, second, coeffs, basis = pl.pallas_call(
        kernel,
        name="step",
        out_shape=(
            state, state,
            jax.ShapeDtypeStruct((2, 4, 4, 2, 2 * PIECE, RANK), bf16),
            jax.ShapeDtypeStruct((2 * ROWS, RANK), bf16),
        ),
        in_specs=[hbm] * 5,
        out_specs=(hbm, hbm, vmem, vmem),
        scratch_shapes=[
            pltpu.VMEM((8, TOK, 640), bf16),
            pltpu.VMEM((TOK, COLS), bf16),
            pltpu.VMEM((640, COLS), f32),
            pltpu.VMEM((8, ROWS, COLS), f32),
            pltpu.VMEM((8, ROWS, COLS), bf16),
            pltpu.VMEM((8, ROWS, COLS), bf16),
            pltpu.VMEM((6, ROWS, COLS), bf16),
            pltpu.VMEM((2, 2, HALF, COLS), bf16),
            pltpu.VMEM((2, XHALF, COLS), bf16),
            pltpu.VMEM((2, 2, ROWS, COLS), bf16),
            pltpu.VMEM((4, XROWS, COLS), bf16),
            pltpu.VMEM((4, XROWS, COLS), bf16),
            pltpu.VMEM((2 * HALF, COLS), bf16),
            pltpu.VMEM((2 * HALF, COLS), bf16),
            pltpu.VMEM((ROWS, COLS), f32),
            pltpu.VMEM((ROWS, COLS), f32),
            pltpu.VMEM((ROWS, COLS), f32),
            pltpu.VMEM((COLS, RANK), f32),
            pltpu.VMEM((ROWS, RANK), f32),
            pltpu.VMEM((7, PIECE, RANK), f32),
            pltpu.VMEM((ROWS, RANK), f32),
            pltpu.VMEM((2, ROWS, RANK), f32),
            pltpu.VMEM((RANK, RANK), f32),
            pltpu.VMEM((64, RANK), f32),
            pltpu.VMEM((8, 8, RANK), f32),
            pltpu.VMEM((RANK, RANK), f32),
            pltpu.VMEM((COLS, RANK), f32),
            pltpu.VMEM((ROWS, RANK), f32),
            pltpu.VMEM((8, PIECE, RANK), f32),
            pltpu.VMEM((4, 2, 2 * PIECE, RANK), f32),
            pltpu.VMEM((RANK, RANK), f32),
            pltpu.SemaphoreType.DMA((12,)),
            pltpu.SemaphoreType.DMA((SEMS,)),
            pltpu.SemaphoreType.DMA((SEMS,)),
        ],
        compiler_params=pltpu.CompilerParams(
            collective_id=0, has_side_effects=True, vmem_limit_bytes=58 << 20),
    )(activations, cotangent, first_moment, second_moment, sketch)
    rebuilt, new_first, new_second = pl.pallas_call(
        rebuild,
        name="rebuild",
        out_shape=(jax.ShapeDtypeStruct((COLS, D), bf16), state, state),
        in_specs=[hbm] * 4,
        out_specs=(hbm,) * 3,
        scratch_shapes=[
            pltpu.VMEM((2 * ROWS, RANK), bf16),
            pltpu.VMEM((4, 2, 4, 2, 2 * PIECE, RANK), bf16),
            pltpu.VMEM((8, COLS, COLS), bf16),
            pltpu.VMEM((2, ROWS, COLS), f32),
            pltpu.SemaphoreType.DMA((19,)),
        ],
        compiler_params=pltpu.CompilerParams(vmem_limit_bytes=60 << 20),
    )(basis, coeffs, first, second)
    return new_first, new_second, rebuilt


def solution(mesh):
    placed = (P("fsdp", None), P("fsdp", "roll"), P("fsdp", "roll"), P("fsdp", "roll"), P("roll", None))
    return jax.shard_map(
        local,
        mesh=mesh,
        in_specs=placed,
        out_specs=(P("fsdp", "roll"), P("fsdp", "roll"), P("roll", None)),
        check_vma=False,
    )
```

```python
import functools

import jax
import jax.numpy as jnp
from jax import lax
from jax.experimental import pallas as pl
from jax.experimental.pallas import tpu as pltpu
from jax.sharding import PartitionSpec as P

beta_one = 0.9
beta_two = 0.95
epsilon = 1e-08
hp = lax.Precision.HIGHEST
MESH = pl.DeviceIdType.MESH
f32, bf16 = jnp.float32, jnp.bfloat16
DN0 = (((0,), (0,)), ((), ()))
DN1 = (((1,), (1,)), ((), ()))
DN = (((1,), (0,)), ((), ()))

D, TOK, RANK = 5120, 1024, 128
COLS = 640
ROWS = 320
XROWS = 128
XHALF = XROWS // 2
HALF = (ROWS - XROWS) // 2
PIECE = ROWS // 8
FAR_FIRST = (3, 5, 4, 1, 7, 2, 6)
PLANE = ((2, 2), (1, 2), (3, 2), (2, 1), (2, 3), (1, 1), (3, 3), (1, 3), (3, 1), (2, 0), (0, 2), (1, 0), (3, 0), (0, 1), (0, 3))

ORDER = ((2, 1), (2, 0), (1, 1), (3, 1), (0, 1), (1, 0), (3, 0), (0, 0))
SEMS = 128


def split(v, parts):
    out = []
    for _ in range(parts):
        out.append(v.astype(bf16))
        v = v - out[-1].astype(f32)
    return out


def full_dot(a, b, dims):
    def d(x, y):
        return lax.dot_general(x, y, dims, preferred_element_type=f32)
    a1, a2, a3 = split(a, 3)
    b1, b2, b3 = split(b, 3)
    pair = jnp.concatenate([b1, b2], axis=1 - dims[0][1][0])
    u, w = d(a1, pair), d(a2, pair)
    return u[:, :RANK] + ((u[:, RANK:] + w[:, :RANK]) + (w[:, RANK:] + (d(a1, b3) + d(a3, b1))))


def looped(total, step, body):
    def one(i, carry):
        body(pl.multiple_of(i * step, step))
        return carry
    lax.fori_loop(0, total // step, one, 0, unroll=True)


def split3(v):
    a = v.astype(bf16).astype(f32); v = v - a
    b = v.astype(bf16).astype(f32)
    return a, b, (v - b).astype(bf16).astype(f32)

def factor_inverse(gram_ref, inv_ref):
    lane = lax.broadcasted_iota(jnp.int32, (8, 128), 1)
    sub = lax.broadcasted_iota(jnp.int32, (8, 128), 0)
    panels = [gram_ref[8 * i:8 * i + 8, :] for i in range(16)]

    def down(v, j):
        return jnp.broadcast_to(v[j:j + 1, :], (8, 128))

    for k in range(16):
        panel = panels[k]
        last = k == 15
        cols = [jnp.broadcast_to(panel[:, 8 * k + j:8 * k + j + 1], (8, 128)) for j in range(8)]
        if not last:
            ahead = panels[k + 1]
            acols = [jnp.broadcast_to(ahead[:, 8 * k + j:8 * k + j + 1], (8, 128)) for j in range(8)]
        scale = jnp.zeros((8, 128), f32)
        amul = []
        for j in range(8):
            p = 8 * k + j
            recip = 1.0 / down(cols[j], j)
            scale = jnp.where(sub == j, recip, scale)
            m = jnp.where(sub > j, -cols[j] * recip, 0.0)
            row = down(jnp.where(lane == p, 1.0, panel), j)
            panel = jnp.where((lane == p) & (sub > j), 0.0, panel) + m * row
            if not last:
                am = -acols[j] * recip
                amul.append(am)
            for i in range(j + 1, 8):
                u = down(cols[j], i)
                cols[i] = cols[i] + m * u
                if not last:
                    acols[i] = acols[i] + am * u
        panels[k] = panel
        if not last:
            inside = (lane >= 8 * k) & (lane < 8 * k + 8)
            ext = jnp.where(inside & (lane - 8 * k > sub), 0.0, panel)
            ext = jnp.where(inside & (lane - 8 * k == sub), 1.0, ext)
            ahead = jnp.where(inside, 0.0, ahead)
            for j in range(8):
                ahead = ahead + amul[j] * down(ext, j)
            panels[k + 1] = ahead
            if k < 14:
                lhs = -panel * scale
                a1, a2, a3 = split3(lhs)
                b1, b2, b3 = split3(ext)
                left = jnp.concatenate([a1, a1, a2, a2, a1, a3], axis=0).astype(bf16)
                right = jnp.concatenate([b1, b2, b1, b2, b3, b1], axis=0).astype(bf16)
                upd = lax.dot_general(left, right, DN0, preferred_element_type=f32)
                for i in range(k + 2, 16):
                    panels[i] = jnp.where(inside, 0.0, panels[i]) + upd[8 * i:8 * i + 8, :]
        yield k
    for k in range(16):
        at = lane == sub + 8 * k
        d = jnp.sum(jnp.where(at, panels[k], 0.0), axis=1, keepdims=True)
        m = jnp.where(lane < sub + 8 * k, panels[k], jnp.where(at, 1.0, 0.0))
        inv_ref[8 * k:8 * k + 8, :] = m * lax.rsqrt(d)


def kernel(
    act, cot, first, second, sketch,
    new_first, new_second, coeffs_out, basis_out,
    abuf, cbuf, pbuf, own, psend, crecv, ysend, y1recv, y1x, y2recv, xfsend, xfrecv, xsend, xrecv,
    mbuf, vbuf, dbuf, skbuf, rpart, rrecv, rfull, r_out, gpart, gown, gcrecv, gslots, gchips, gfull,
    spart, screcv, sslots, s_own, inverse, ctbuf, bbuf,
    lsem, ssem, rsem,
):
    f, r = lax.axis_index("fsdp"), lax.axis_index("roll")
    y, xh, c = f // 4, (f // 2) % 2, f % 2
    z, xl = r // 2, r % 2
    q = f // 2

    def dev(y=y, xh=xh, c=c, z=z, xl=xl):
        return {"fsdp": (y * 2 + xh) * 2 + c, "roll": z * 2 + xl}

    sibling = dev(c=1 - c)
    plus, minus = dev(y=(y + 1) % 4), dev(y=(y + 3) % 4)
    across = dev(xh=1 - xh)

    def chip(k):
        other = (q + k) % 8
        return {"fsdp": other * 2 + c, "roll": r}, other

    def roller(k):
        other = (r + k) % 8
        return {"fsdp": f, "roll": other}, other

    def plane(kx, kt):
        other = (xh * 2 + xl + kx) % 4
        return dev(xh=other // 2, xl=other % 2, y=(y + (1 - c) * kt) % 4, z=(z + c * kt) % 4)

    used = [0]

    def remote(src, dst, where):
        i = used[0]
        used[0] += 1
        return pltpu.make_async_remote_copy(
            src_ref=src, dst_ref=dst, send_sem=ssem.at[i], recv_sem=rsem.at[i],
            device_id=where, device_id_type=MESH,
        )

    pending = []

    def send(src, dst, where):
        copy = remote(src, dst, where)
        copy.start()
        pending.append(copy)
        return copy

    def drain(keep=0):
        while len(pending) > keep:
            pending.pop(0).wait_send()

    loads = []
    c_load = pltpu.make_async_copy(cot, cbuf, lsem.at[8])
    c_load.start()
    for k, (dy, dxh) in enumerate(ORDER):
        block = ((y + dy) % 4) * 2 + (xh + dxh) % 2
        load = pltpu.make_async_copy(
            act.at[:, pl.ds(pl.multiple_of(block * 640, 640), 640)], abuf.at[k], lsem.at[k]
        )
        load.start()
        loads.append(load)
    late = [
        pltpu.make_async_copy(first, mbuf, lsem.at[9]),
        pltpu.make_async_copy(second, vbuf, lsem.at[10]),
        pltpu.make_async_copy(sketch, skbuf, lsem.at[11]),
    ]
    for load in late:
        load.start()

    barrier = pltpu.get_barrier_semaphore()
    greeted = [sibling] + [chip(k)[0] for k in range(1, 8)] + [roller(k)[0] for k in range(1, 8)] + [plane(kx, kt) for kx, kt in PLANE]
    for other in greeted:
        pl.semaphore_signal(barrier, inc=1, device_id=other, device_id_type=MESH)
    c_load.wait()

    mine = pl.multiple_of(c * ROWS, ROWS)
    theirs = pl.multiple_of((1 - c) * ROWS, ROWS)
    halves = []

    def compute(k):
        loads[k].wait()
        pbuf[...] = lax.dot_general(abuf[k], cbuf[...], DN0, preferred_element_type=f32)

        def split(o):
            psend[k, pl.ds(o, 32)] = pbuf[pl.ds(theirs + o, 32)].astype(bf16)
            own[k, pl.ds(o, 32)] = pbuf[pl.ds(mine + o, 32)]
        looped(ROWS, 32, split)
        if k == 0:
            pl.semaphore_wait(barrier, len(greeted))
        halves.append(send(psend.at[k], crecv.at[k], sibling))

    step_one, step_two, first_x, one_x, two_x = {}, {}, {}, {}, {}
    ways = (plus, minus)

    def summed(k, at):
        return own[k, at] + crecv[k, at].astype(f32)

    def post(k):
        dy, dxh = ORDER[k]
        halves[k].wait_recv()
        if dxh == 1:
            def add(o):
                xfsend[dy, pl.ds(o, 32)] = summed(k, pl.ds(o, 32)).astype(bf16)
            looped(XROWS, 32, add)
            first_x[dy] = send(xfsend.at[dy], xfrecv.at[dy], across)
        if dy == 2:
            def add(o):
                at = pl.ds(XROWS + o, 32)
                ysend[k, at] = summed(k, at).astype(bf16)
            looped(ROWS - XROWS, 32, add)
            for way, where in enumerate(ways):
                step_one[way, dxh] = send(
                    ysend.at[k, pl.ds(XROWS + way * HALF, HALF)], y1recv.at[way, dxh], where)
        elif dy != 0:
            way = 0 if dy == 1 else 1
            alone = XROWS + (1 - way) * HALF

            def add(o):
                at = pl.ds(alone + o, 32)
                ysend[k, at] = summed(k, at).astype(bf16)
            looped(HALF, 32, add)
            step_two[way, dxh, 1] = send(
                ysend.at[k, pl.ds(alone, HALF)], y2recv.at[way, dxh, pl.ds(alone, HALF)], ways[way])

    def accumulate(dxh, which=(0, 1)):
        for way, dy in ((way, (1, 3)[way]) for way in which):
            k = ORDER.index((dy, dxh))
            step_one[way, dxh].wait_recv()
            start = XROWS + way * HALF

            def add(o):
                at = pl.ds(start + o, 32)
                ysend[k, at] = (summed(k, at) + y1recv[way, dxh, pl.ds(o, 32)].astype(f32)).astype(bf16)
            looped(HALF, 32, add)
            step_two[way, dxh, 0] = send(
                ysend.at[k, pl.ds(start, HALF)], y2recv.at[way, dxh, pl.ds(start, HALF)], ways[way])

    def crossed(dy):
        k = ORDER.index((dy, 0))
        first_x[dy].wait_recv()
        start, size = {2: (0, XROWS), 1: (XHALF, XHALF), 3: (0, XHALF)}[dy]

        def add(o):
            at = pl.ds(start + o, 32)
            ysend[k, at] = (summed(k, at) + xfrecv[dy, at].astype(f32)).astype(bf16)
        looped(size, 32, add)
        if dy == 2:
            for way, where in enumerate(ways):
                one_x[way] = send(ysend.at[k, pl.ds(way * XHALF, XHALF)], y1x.at[way], where)
        else:
            way = 0 if dy == 1 else 1
            two_x[way, 1] = send(ysend.at[k, pl.ds(start, XHALF)], y2recv.at[way, 0, pl.ds(start, XHALF)], ways[way])

    def crossed_accumulate(which=(0, 1)):
        for way, dy in ((way, (1, 3)[way]) for way in which):
            k = ORDER.index((dy, 0))
            one_x[way].wait_recv()
            start = way * XHALF

            def add(o):
                at = pl.ds(start + o, 32)
                ysend[k, at] = (summed(k, at) + xfrecv[dy, at].astype(f32)
                                + y1x[way, pl.ds(o, 32)].astype(f32)).astype(bf16)
            looped(XHALF, 32, add)
            two_x[way, 0] = send(ysend.at[k, pl.ds(start, XHALF)], y2recv.at[way, 0, pl.ds(start, XHALF)], ways[way])

    crossing = []

    def cross(part):
        o0 = XROWS + part * HALF
        for way in range(2):
            step_two[way, 1, 0 if way == part else 1].wait_recv()
        k = ORDER.index((0, 1))

        def add(o):
            at = pl.ds(o0 + o, 32)
            xsend[pl.ds(part * HALF + o, 32)] = (
                summed(k, at) + y2recv[0, 1, at].astype(f32) + y2recv[1, 1, at].astype(f32)).astype(bf16)
        looped(HALF, 32, add)
        crossing.append(send(xsend.at[pl.ds(part * HALF, HALF)], xrecv.at[pl.ds(part * HALF, HALF)], across))

    for k in range(8):
        compute(k)
        if k >= 1:
            post(k - 1)
        if k == 4:
            accumulate(1)
            crossed(2)
        if k == 6:
            accumulate(0, (0,))
            crossed(1)
        if k == 7:
            accumulate(0, (1,))
            crossed(3)
    cross(0)
    cross(1)
    post(7)
    crossed_accumulate()
    for load in late:
        load.wait()

    def adam(at, far):
        grad = summed(7, at) + y2recv[0, 0, at].astype(f32) + y2recv[1, 0, at].astype(f32) + far
        new_m = beta_one * mbuf[at] + (1.0 - beta_one) * grad
        new_v = beta_two * vbuf[at] + (1.0 - beta_two) * grad * grad
        mbuf[at] = new_m
        vbuf[at] = new_v
        dbuf[at] = (new_m * (1.0 / (1.0 - beta_one**20))) / (
            jnp.sqrt(new_v * (1.0 / (1.0 - beta_two**20))) + epsilon)

    stores = []
    first_x[0].wait_recv()
    for way in range(2):
        for part in range(2):
            two_x[way, part].wait_recv()
    looped(XROWS, 16, lambda o: adam(pl.ds(o, 16), xfrecv[0, pl.ds(o, 16)].astype(f32)))

    def sketched(o, n):
        rpart[o:o + n] = full_dot(dbuf[o:o + n], skbuf[...], DN)
    for part in range(2):
        for way in range(2):
            step_two[way, 0, 0 if way == part else 1].wait_recv()
        crossing[part].wait_recv()
    sketched(0, XROWS)
    looped(2 * HALF, 16, lambda o: adam(pl.ds(XROWS + o, 16), xrecv[pl.ds(o, 16)].astype(f32)))
    sketched(XROWS, ROWS - XROWS)
    for i, (src, dst) in enumerate(((mbuf, new_first), (vbuf, new_second))):
        store = pltpu.make_async_copy(src, dst, lsem.at[i])
        store.start()
        stores.append(store)

    parts = []
    for k in FAR_FIRST:
        where, other = roller(k)
        parts.append(send(rpart.at[pl.ds(pl.multiple_of(other * PIECE, 8), PIECE)], rrecv.at[k - 1], where))
    my_piece = pl.ds(pl.multiple_of(r * PIECE, 8), PIECE)
    total = rpart[my_piece]
    for part in parts:
        part.wait_recv()
    for k in range(7):
        total = total + rrecv[k]
    rfull[my_piece] = total
    parts = [send(rfull.at[my_piece], rfull.at[my_piece], roller(k)[0]) for k in FAR_FIRST]
    swap = remote(rfull.at[my_piece], r_out.at[c, my_piece], dev(y=z, xh=xl, z=y, xl=xh))
    own_piece = pl.ds(pl.multiple_of(q * PIECE, 8), PIECE)
    swapped = (y != z) | (xh != xl)

    @pl.when(swapped)
    def _():
        swap.start()

    @pl.when(jnp.logical_not(swapped))
    def _():
        r_out[c, own_piece] = rfull[my_piece]

    def gathered(sent, slots):
        for part in sent:
            part.wait_recv()
        total = slots[0]
        for k in range(1, 8):
            total = total + slots[k]
        return total

    def scatter(part, slots, peer, me, piece):
        sent = []
        for k in FAR_FIRST:
            where, other = peer(k)
            sent.append(send(part.at[piece(other)], slots.at[me], where))
        slots[me] = part[piece(me)]
        return sent

    def sixteen(i):
        return pl.ds(pl.multiple_of(i * 16, 16), 16)
    piece_rows = rfull[my_piece]
    gpart[...] = lax.dot_general(piece_rows, piece_rows, DN0, precision=hp, preferred_element_type=f32)
    gsent = scatter(gpart, gslots, roller, r, sixteen)

    give_at = pl.ds(pl.multiple_of((1 - c) * 256, 128), 384)
    keep_at = pl.ds(pl.multiple_of(c * 384, 128), 256)
    for part in parts:
        part.wait_recv()
    spart[give_at] = full_dot(dbuf[:, give_at], rfull[...], DN0)
    scopy = send(spart.at[pl.ds(theirs, ROWS)], screcv, sibling)
    gown[...] = gathered(gsent, gslots)
    gcopy = send(gown, gcrecv, sibling)
    spart[keep_at] = full_dot(dbuf[:, keep_at], rfull[...], DN0)
    gcopy.wait_recv()
    gchips[q] = gown[...] + gcrecv[...]
    gsent = [send(gchips.at[q], gchips.at[q], chip(k)[0]) for k in FAR_FIRST]
    scopy.wait_recv()
    spart[pl.ds(mine, ROWS)] = spart[pl.ds(mine, ROWS)] + screcv[...]
    ssent = scatter(spart, sslots, chip, q, lambda i: pl.ds(pl.multiple_of((c * 8 + i) * PIECE, 8), PIECE))
    gfull[sixteen(r)] = gathered(gsent, gchips)
    gsent = [send(gfull.at[sixteen(r)], gfull.at[sixteen(r)], roller(k)[0]) for k in FAR_FIRST]

    @pl.when(swapped)
    def _():
        swap.wait_recv()
    rsent = [send(r_out.at[c, own_piece], r_out.at[c, own_piece], chip(k)[0]) for k in FAR_FIRST]

    s, t = c * y + (1 - c) * z, c * z + (1 - c) * y
    at = pl.ds(pl.multiple_of(xh * PIECE, 8), PIECE)
    s_own[t, xl, at] = gathered(ssent, sslots)
    ssent = [send(s_own.at[t, xl, at], s_own.at[t, xl, at], plane(kx, kt)) for kx, kt in PLANE]

    def along_s(k):
        return dev(y=(y + c * k) % 4, z=(z + (1 - c) * k) % 4)

    for part in gsent:
        part.wait_recv()
    drain(16)
    for _ in factor_inverse(gfull, inverse):
        pass
    for part in rsent:
        part.wait_recv()
    rcopy = send(r_out.at[c], r_out.at[c], sibling)
    for part in ssent:
        part.wait_recv()
    coeffs = full_dot(s_own[...].reshape(COLS, RANK), inverse[...], DN1)
    ctbuf[c, s] = coeffs.reshape(4, 2, 2 * PIECE, RANK).astype(bf16)
    ssent = [send(ctbuf.at[c, s], ctbuf.at[c, s], along_s(k)) for k in (2, 1, 3)]
    copies = [send(ctbuf.at[c, s], ctbuf.at[c, s], sibling)]

    def keep(core, place, i):
        store = pltpu.make_async_copy(ctbuf.at[core, place], coeffs_out.at[core, place], lsem.at[i])
        store.start()
        stores.append(store)
    keep(c, s, 2)
    rcopy.wait_recv()
    for core in range(2):
        bbuf[core * ROWS:(core + 1) * ROWS] = full_dot(r_out[core], inverse[...], DN1).astype(bf16)
    stores.append(pltpu.make_async_copy(bbuf, basis_out, lsem.at[3]))
    stores[-1].start()

    @pl.when(swapped)
    def _():
        swap.wait_send()
    drain(4)
    for i, (k, part) in enumerate(((1, ssent[1]), (3, ssent[2]), (2, ssent[0]))):
        part.wait_recv()
        have = (s + 4 - k) % 4
        copies.append(send(ctbuf.at[c, have], ctbuf.at[c, have], sibling))
        keep(c, have, 4 + i)
    theirs_s = c * z + (1 - c) * y
    for i, k in enumerate((0, 1, 3, 2)):
        copies[i].wait_recv()
        keep(1 - c, (theirs_s + 4 - k) % 4, 7 + i)
    for store in stores:
        store.wait()
    drain()


def rebuild(basis, coeffs, first, second, rebuilt, new_first, new_second, bbuf, cbuf, obuf, state, sem):
    copies = [pltpu.make_async_copy(basis, bbuf, sem.at[2])]
    copies += [pltpu.make_async_copy(coeffs.at[0, i], cbuf.at[i, 0], sem.at[3 + i]) for i in range(4)]
    copies += [pltpu.make_async_copy(coeffs.at[1, :, i], cbuf.at[i, 1], sem.at[15 + i]) for i in range(4)]
    moved = [pltpu.make_async_copy(first, state.at[0], sem.at[0]), pltpu.make_async_copy(second, state.at[1], sem.at[1])]
    for copy in copies + moved:
        copy.start()
    kept = []
    copies[0].wait()
    for i in range(4):
        copies[1 + i].wait()
        copies[5 + i].wait()
        for j in range(2):
            block = jnp.concatenate([cbuf[i, core, k, j] for core in range(2) for k in range(4)], axis=0)
            obuf[2 * i + j] = lax.dot_general(bbuf[...], block, DN1, preferred_element_type=f32).astype(bf16)
            copy = pltpu.make_async_copy(obuf.at[2 * i + j], rebuilt.at[:, pl.ds((2 * i + j) * COLS, COLS)], sem.at[7 + 2 * i + j])
            copy.start()
            kept.append(copy)
        if i < 2:
            moved[i].wait()
            copy = pltpu.make_async_copy(state.at[i], (new_first, new_second)[i], sem.at[i])
            copy.start()
            kept.append(copy)
    for copy in kept:
        copy.wait()


def local(activations, cotangent, first_moment, second_moment, sketch):
    hbm = pl.BlockSpec(memory_space=pltpu.HBM)
    state = jax.ShapeDtypeStruct((ROWS, COLS), f32)
    first, second, coeffs, basis = pl.pallas_call(
        kernel,
        name="step",
        out_shape=(
            state, state,
            jax.ShapeDtypeStruct((2, 4, 4, 2, 2 * PIECE, RANK), bf16),
            jax.ShapeDtypeStruct((2 * ROWS, RANK), bf16),
        ),
        in_specs=[hbm] * 5,
        out_specs=(hbm,) * 4,
        scratch_shapes=[
            pltpu.VMEM((8, TOK, 640), bf16),
            pltpu.VMEM((TOK, COLS), bf16),
            pltpu.VMEM((640, COLS), f32),
            pltpu.VMEM((8, ROWS, COLS), f32),
            pltpu.VMEM((8, ROWS, COLS), bf16),
            pltpu.VMEM((8, ROWS, COLS), bf16),
            pltpu.VMEM((7, ROWS, COLS), bf16),
            pltpu.VMEM((2, 2, HALF, COLS), bf16),
            pltpu.VMEM((2, XHALF, COLS), bf16),
            pltpu.VMEM((2, 2, ROWS, COLS), bf16),
            pltpu.VMEM((4, XROWS, COLS), bf16),
            pltpu.VMEM((4, XROWS, COLS), bf16),
            pltpu.VMEM((2 * HALF, COLS), bf16),
            pltpu.VMEM((2 * HALF, COLS), bf16),
            pltpu.VMEM((ROWS, COLS), f32),
            pltpu.VMEM((ROWS, COLS), f32),
            pltpu.VMEM((ROWS, COLS), f32),
            pltpu.VMEM((COLS, RANK), f32),
            pltpu.VMEM((ROWS, RANK), f32),
            pltpu.VMEM((7, PIECE, RANK), f32),
            pltpu.VMEM((ROWS, RANK), f32),
            pltpu.VMEM((2, ROWS, RANK), f32),
            pltpu.VMEM((RANK, RANK), f32),
            pltpu.VMEM((16, RANK), f32),
            pltpu.VMEM((16, RANK), f32),
            pltpu.VMEM((8, 16, RANK), f32),
            pltpu.VMEM((8, 16, RANK), f32),
            pltpu.VMEM((RANK, RANK), f32),
            pltpu.VMEM((COLS, RANK), f32),
            pltpu.VMEM((ROWS, RANK), f32),
            pltpu.VMEM((8, PIECE, RANK), f32),
            pltpu.VMEM((4, 2, 2 * PIECE, RANK), f32),
            pltpu.VMEM((RANK, RANK), f32),
            pltpu.VMEM((2, 4, 4, 2, 2 * PIECE, RANK), bf16),
            pltpu.VMEM((2 * ROWS, RANK), bf16),
            pltpu.SemaphoreType.DMA((12,)),
            pltpu.SemaphoreType.DMA((SEMS,)),
            pltpu.SemaphoreType.DMA((SEMS,)),
        ],
        compiler_params=pltpu.CompilerParams(
            collective_id=0, has_side_effects=True, vmem_limit_bytes=58 << 20),
    )(activations, cotangent, first_moment, second_moment, sketch)
    rebuilt, new_first, new_second = pl.pallas_call(
        rebuild,
        name="rebuild",
        out_shape=(jax.ShapeDtypeStruct((COLS, D), bf16), state, state),
        in_specs=[hbm] * 4,
        out_specs=(hbm,) * 3,
        scratch_shapes=[
            pltpu.VMEM((2 * ROWS, RANK), bf16),
            pltpu.VMEM((4, 2, 4, 2, 2 * PIECE, RANK), bf16),
            pltpu.VMEM((8, COLS, COLS), bf16),
            pltpu.VMEM((2, ROWS, COLS), f32),
            pltpu.SemaphoreType.DMA((19,)),
        ],
        compiler_params=pltpu.CompilerParams(vmem_limit_bytes=60 << 20),
    )(basis, coeffs, first, second)
    return new_first, new_second, rebuilt


def solution(mesh):
    placed = (P("fsdp", None), P("fsdp", "roll"), P("fsdp", "roll"), P("fsdp", "roll"), P("roll", None))
    return jax.shard_map(
        local,
        mesh=mesh,
        in_specs=placed,
        out_specs=(P("fsdp", "roll"), P("fsdp", "roll"), P("roll", None)),
        check_vma=False,
    )
```

```python
import functools

import jax
import jax.numpy as jnp
from jax import lax
from jax.experimental import pallas as pl
from jax.experimental.pallas import tpu as pltpu
from jax.sharding import PartitionSpec as P

beta_one = 0.9
beta_two = 0.95
epsilon = 1e-08
hp = lax.Precision.HIGHEST
MESH = pl.DeviceIdType.MESH
f32, bf16 = jnp.float32, jnp.bfloat16
DN0 = (((0,), (0,)), ((), ()))
DN1 = (((1,), (1,)), ((), ()))
DN = (((1,), (0,)), ((), ()))

D, TOK, RANK = 5120, 1024, 128
COLS = 640
ROWS = 320
XROWS = 128
XHALF = XROWS // 2
HALF = (ROWS - XROWS) // 2
PIECE = ROWS // 8
FAR_FIRST = (3, 5, 4, 1, 7, 2, 6)
PLANE = ((2, 2), (1, 2), (3, 2), (2, 1), (2, 3), (1, 1), (3, 3), (1, 3), (3, 1), (2, 0), (0, 2), (1, 0), (3, 0), (0, 1), (0, 3))

ORDER = ((2, 1), (2, 0), (1, 1), (3, 1), (0, 1), (1, 0), (3, 0), (0, 0))
SEMS = 128


def split(v, parts):
    out = []
    for _ in range(parts):
        out.append(v.astype(bf16))
        v = v - out[-1].astype(f32)
    return out


def full_dot(a, b, dims):
    def d(x, y):
        return lax.dot_general(x, y, dims, preferred_element_type=f32)
    a1, a2, a3 = split(a, 3)
    b1, b2, b3 = split(b, 3)
    pair = jnp.concatenate([b1, b2], axis=1 - dims[0][1][0])
    u, w = d(a1, pair), d(a2, pair)
    return u[:, :RANK] + ((u[:, RANK:] + w[:, :RANK]) + (w[:, RANK:] + (d(a1, b3) + d(a3, b1))))


def looped(total, step, body):
    def one(i, carry):
        body(pl.multiple_of(i * step, step))
        return carry
    lax.fori_loop(0, total // step, one, 0, unroll=True)


def split3(v):
    a = v.astype(bf16).astype(f32); v = v - a
    b = v.astype(bf16).astype(f32)
    return a, b, (v - b).astype(bf16).astype(f32)

def factor_inverse(gram_ref, inv_ref):
    lane = lax.broadcasted_iota(jnp.int32, (8, 128), 1)
    sub = lax.broadcasted_iota(jnp.int32, (8, 128), 0)
    panels = [gram_ref[8 * i:8 * i + 8, :] for i in range(16)]

    def down(v, j):
        return jnp.broadcast_to(v[j:j + 1, :], (8, 128))

    for k in range(16):
        panel = panels[k]
        last = k == 15
        cols = [jnp.broadcast_to(panel[:, 8 * k + j:8 * k + j + 1], (8, 128)) for j in range(8)]
        if not last:
            ahead = panels[k + 1]
            acols = [jnp.broadcast_to(ahead[:, 8 * k + j:8 * k + j + 1], (8, 128)) for j in range(8)]
        scale = jnp.zeros((8, 128), f32)
        amul = []
        for j in range(8):
            p = 8 * k + j
            recip = 1.0 / down(cols[j], j)
            scale = jnp.where(sub == j, recip, scale)
            m = jnp.where(sub > j, -cols[j] * recip, 0.0)
            row = down(jnp.where(lane == p, 1.0, panel), j)
            panel = jnp.where((lane == p) & (sub > j), 0.0, panel) + m * row
            if not last:
                am = -acols[j] * recip
                amul.append(am)
            for i in range(j + 1, 8):
                u = down(cols[j], i)
                cols[i] = cols[i] + m * u
                if not last:
                    acols[i] = acols[i] + am * u
        panels[k] = panel
        if not last:
            inside = (lane >= 8 * k) & (lane < 8 * k + 8)
            ext = jnp.where(inside & (lane - 8 * k > sub), 0.0, panel)
            ext = jnp.where(inside & (lane - 8 * k == sub), 1.0, ext)
            ahead = jnp.where(inside, 0.0, ahead)
            for j in range(8):
                ahead = ahead + amul[j] * down(ext, j)
            panels[k + 1] = ahead
            if k < 14:
                lhs = -panel * scale
                a1, a2, a3 = split3(lhs)
                b1, b2, b3 = split3(ext)
                left = jnp.concatenate([a1, a1, a2, a2, a1, a3], axis=0).astype(bf16)
                right = jnp.concatenate([b1, b2, b1, b2, b3, b1], axis=0).astype(bf16)
                upd = lax.dot_general(left, right, DN0, preferred_element_type=f32)
                for i in range(k + 2, 16):
                    panels[i] = jnp.where(inside, 0.0, panels[i]) + upd[8 * i:8 * i + 8, :]
        yield k
    for k in range(16):
        at = lane == sub + 8 * k
        d = jnp.sum(jnp.where(at, panels[k], 0.0), axis=1, keepdims=True)
        m = jnp.where(lane < sub + 8 * k, panels[k], jnp.where(at, 1.0, 0.0))
        inv_ref[8 * k:8 * k + 8, :] = m * lax.rsqrt(d)


def kernel(
    act, cot, first, second, sketch,
    new_first, new_second, coeffs_out, basis_out,
    abuf, cbuf, pbuf, own, psend, crecv, ysend, y1recv, y1x, y2recv, xfsend, xfrecv, xsend, xrecv,
    mbuf, vbuf, dbuf, skbuf, rpart, rrecv, rfull, r_out, gpart, gown, gcrecv, gslots, gchips, gfull,
    spart, screcv, sslots, s_own, inverse, ctbuf, bbuf,
    lsem, ssem, rsem,
):
    f, r = lax.axis_index("fsdp"), lax.axis_index("roll")
    y, xh, c = f // 4, (f // 2) % 2, f % 2
    z, xl = r // 2, r % 2
    q = f // 2

    def dev(y=y, xh=xh, c=c, z=z, xl=xl):
        return {"fsdp": (y * 2 + xh) * 2 + c, "roll": z * 2 + xl}

    sibling = dev(c=1 - c)
    plus, minus = dev(y=(y + 1) % 4), dev(y=(y + 3) % 4)
    across = dev(xh=1 - xh)

    def chip(k):
        other = (q + k) % 8
        return {"fsdp": other * 2 + c, "roll": r}, other

    def roller(k):
        other = (r + k) % 8
        return {"fsdp": f, "roll": other}, other

    def plane(kx, kt):
        other = (xh * 2 + xl + kx) % 4
        return dev(xh=other // 2, xl=other % 2, y=(y + (1 - c) * kt) % 4, z=(z + c * kt) % 4)

    used = [0]

    def remote(src, dst, where):
        i = used[0]
        used[0] += 1
        return pltpu.make_async_remote_copy(
            src_ref=src, dst_ref=dst, send_sem=ssem.at[i], recv_sem=rsem.at[i],
            device_id=where, device_id_type=MESH,
        )

    pending = []

    def send(src, dst, where):
        copy = remote(src, dst, where)
        copy.start()
        pending.append(copy)
        return copy

    def drain(keep=0):
        while len(pending) > keep:
            pending.pop(0).wait_send()

    loads = []
    c_load = pltpu.make_async_copy(cot, cbuf, lsem.at[8])
    c_load.start()
    for k, (dy, dxh) in enumerate(ORDER):
        block = ((y + dy) % 4) * 2 + (xh + dxh) % 2
        load = pltpu.make_async_copy(
            act.at[:, pl.ds(pl.multiple_of(block * 640, 640), 640)], abuf.at[k], lsem.at[k]
        )
        load.start()
        loads.append(load)
    late = [
        pltpu.make_async_copy(first, mbuf, lsem.at[9]),
        pltpu.make_async_copy(second, vbuf, lsem.at[10]),
        pltpu.make_async_copy(sketch, skbuf, lsem.at[11]),
    ]
    for load in late:
        load.start()

    barrier = pltpu.get_barrier_semaphore()
    greeted = [sibling] + [chip(k)[0] for k in range(1, 8)] + [roller(k)[0] for k in range(1, 8)] + [plane(kx, kt) for kx, kt in PLANE]
    for other in greeted:
        pl.semaphore_signal(barrier, inc=1, device_id=other, device_id_type=MESH)
    c_load.wait()

    mine = pl.multiple_of(c * ROWS, ROWS)
    theirs = pl.multiple_of((1 - c) * ROWS, ROWS)
    halves = []

    def compute(k):
        loads[k].wait()
        pbuf[...] = lax.dot_general(abuf[k], cbuf[...], DN0, preferred_element_type=f32)

        def split(o):
            psend[k, pl.ds(o, 32)] = pbuf[pl.ds(theirs + o, 32)].astype(bf16)
            own[k, pl.ds(o, 32)] = pbuf[pl.ds(mine + o, 32)]
        looped(ROWS, 32, split)
        if k == 0:
            pl.semaphore_wait(barrier, len(greeted))
        halves.append(send(psend.at[k], crecv.at[k], sibling))

    step_one, step_two, first_x, one_x, two_x = {}, {}, {}, {}, {}
    ways = (plus, minus)

    def summed(k, at):
        return own[k, at] + crecv[k, at].astype(f32)

    def post(k):
        dy, dxh = ORDER[k]
        halves[k].wait_recv()
        if dxh == 1:
            def add(o):
                xfsend[dy, pl.ds(o, 32)] = summed(k, pl.ds(o, 32)).astype(bf16)
            looped(XROWS, 32, add)
            first_x[dy] = send(xfsend.at[dy], xfrecv.at[dy], across)
        if dy == 2:
            def add(o):
                at = pl.ds(XROWS + o, 32)
                ysend[k, at] = summed(k, at).astype(bf16)
            looped(ROWS - XROWS, 32, add)
            for way, where in enumerate(ways):
                step_one[way, dxh] = send(
                    ysend.at[k, pl.ds(XROWS + way * HALF, HALF)], y1recv.at[way, dxh], where)
        elif dy != 0:
            way = 0 if dy == 1 else 1
            alone = XROWS + (1 - way) * HALF

            def add(o):
                at = pl.ds(alone + o, 32)
                ysend[k, at] = summed(k, at).astype(bf16)
            looped(HALF, 32, add)
            step_two[way, dxh, 1] = send(
                ysend.at[k, pl.ds(alone, HALF)], y2recv.at[way, dxh, pl.ds(alone, HALF)], ways[way])

    def accumulate(dxh, which=(0, 1)):
        for way, dy in ((way, (1, 3)[way]) for way in which):
            k = ORDER.index((dy, dxh))
            step_one[way, dxh].wait_recv()
            start = XROWS + way * HALF

            def add(o):
                at = pl.ds(start + o, 32)
                ysend[k, at] = (summed(k, at) + y1recv[way, dxh, pl.ds(o, 32)].astype(f32)).astype(bf16)
            looped(HALF, 32, add)
            step_two[way, dxh, 0] = send(
                ysend.at[k, pl.ds(start, HALF)], y2recv.at[way, dxh, pl.ds(start, HALF)], ways[way])

    def crossed(dy):
        k = ORDER.index((dy, 0))
        first_x[dy].wait_recv()
        start, size = {2: (0, XROWS), 1: (XHALF, XHALF), 3: (0, XHALF)}[dy]

        def add(o):
            at = pl.ds(start + o, 32)
            ysend[k, at] = (summed(k, at) + xfrecv[dy, at].astype(f32)).astype(bf16)
        looped(size, 32, add)
        if dy == 2:
            for way, where in enumerate(ways):
                one_x[way] = send(ysend.at[k, pl.ds(way * XHALF, XHALF)], y1x.at[way], where)
        else:
            way = 0 if dy == 1 else 1
            two_x[way, 1] = send(ysend.at[k, pl.ds(start, XHALF)], y2recv.at[way, 0, pl.ds(start, XHALF)], ways[way])

    def crossed_accumulate(which=(0, 1)):
        for way, dy in ((way, (1, 3)[way]) for way in which):
            k = ORDER.index((dy, 0))
            one_x[way].wait_recv()
            start = way * XHALF

            def add(o):
                at = pl.ds(start + o, 32)
                ysend[k, at] = (summed(k, at) + xfrecv[dy, at].astype(f32)
                                + y1x[way, pl.ds(o, 32)].astype(f32)).astype(bf16)
            looped(XHALF, 32, add)
            two_x[way, 0] = send(ysend.at[k, pl.ds(start, XHALF)], y2recv.at[way, 0, pl.ds(start, XHALF)], ways[way])

    crossing = []

    def cross(part):
        o0 = XROWS + part * HALF
        for way in range(2):
            step_two[way, 1, 0 if way == part else 1].wait_recv()
        k = ORDER.index((0, 1))

        def add(o):
            at = pl.ds(o0 + o, 32)
            xsend[pl.ds(part * HALF + o, 32)] = (
                summed(k, at) + y2recv[0, 1, at].astype(f32) + y2recv[1, 1, at].astype(f32)).astype(bf16)
        looped(HALF, 32, add)
        crossing.append(send(xsend.at[pl.ds(part * HALF, HALF)], xrecv.at[pl.ds(part * HALF, HALF)], across))

    for k in range(8):
        compute(k)
        if k >= 1:
            post(k - 1)
        if k == 4:
            accumulate(1)
            crossed(2)
        if k == 6:
            accumulate(0, (0,))
            crossed(1)
        if k == 7:
            accumulate(0, (1,))
            crossed(3)
    cross(0)
    cross(1)
    post(7)
    crossed_accumulate()
    for load in late:
        load.wait()

    def adam(at, far):
        grad = summed(7, at) + y2recv[0, 0, at].astype(f32) + y2recv[1, 0, at].astype(f32) + far
        new_m = beta_one * mbuf[at] + (1.0 - beta_one) * grad
        new_v = beta_two * vbuf[at] + (1.0 - beta_two) * grad * grad
        mbuf[at] = new_m
        vbuf[at] = new_v
        dbuf[at] = (new_m * (1.0 / (1.0 - beta_one**20))) / (
            jnp.sqrt(new_v * (1.0 / (1.0 - beta_two**20))) + epsilon)

    stores = []
    first_x[0].wait_recv()
    for way in range(2):
        for part in range(2):
            two_x[way, part].wait_recv()
    looped(XROWS, 16, lambda o: adam(pl.ds(o, 16), xfrecv[0, pl.ds(o, 16)].astype(f32)))

    def sketched(o, n):
        rpart[o:o + n] = full_dot(dbuf[o:o + n], skbuf[...], DN)
    for part in range(2):
        for way in range(2):
            step_two[way, 0, 0 if way == part else 1].wait_recv()
        crossing[part].wait_recv()
    sketched(0, XROWS)
    looped(2 * HALF, 16, lambda o: adam(pl.ds(XROWS + o, 16), xrecv[pl.ds(o, 16)].astype(f32)))
    sketched(XROWS, ROWS - XROWS)
    for i, (src, dst) in enumerate(((mbuf, new_first), (vbuf, new_second))):
        store = pltpu.make_async_copy(src, dst, lsem.at[i])
        store.start()
        stores.append(store)

    parts = []
    for k in FAR_FIRST:
        where, other = roller(k)
        parts.append(send(rpart.at[pl.ds(pl.multiple_of(other * PIECE, 8), PIECE)], rrecv.at[k - 1], where))
    my_piece = pl.ds(pl.multiple_of(r * PIECE, 8), PIECE)
    total = rpart[my_piece]
    for part in parts:
        part.wait_recv()
    for k in range(7):
        total = total + rrecv[k]
    rfull[my_piece] = total
    parts = [send(rfull.at[my_piece], rfull.at[my_piece], roller(k)[0]) for k in FAR_FIRST]
    swap = remote(rfull.at[my_piece], r_out.at[c, my_piece], dev(y=z, xh=xl, z=y, xl=xh))
    own_piece = pl.ds(pl.multiple_of(q * PIECE, 8), PIECE)
    swapped = (y != z) | (xh != xl)

    @pl.when(swapped)
    def _():
        swap.start()

    @pl.when(jnp.logical_not(swapped))
    def _():
        r_out[c, own_piece] = rfull[my_piece]

    def gathered(sent, slots):
        for part in sent:
            part.wait_recv()
        total = slots[0]
        for k in range(1, 8):
            total = total + slots[k]
        return total

    def scatter(part, slots, peer, me, piece):
        sent = []
        for k in FAR_FIRST:
            where, other = peer(k)
            sent.append(send(part.at[piece(other)], slots.at[me], where))
        slots[me] = part[piece(me)]
        return sent

    def sixteen(i):
        return pl.ds(pl.multiple_of(i * 16, 16), 16)
    piece_rows = rfull[my_piece]
    gpart[...] = lax.dot_general(piece_rows, piece_rows, DN0, precision=hp, preferred_element_type=f32)
    gsent = scatter(gpart, gslots, roller, r, sixteen)

    give_at = pl.ds(pl.multiple_of((1 - c) * 256, 128), 384)
    keep_at = pl.ds(pl.multiple_of(c * 384, 128), 256)
    for part in parts:
        part.wait_recv()
    spart[give_at] = full_dot(dbuf[:, give_at], rfull[...], DN0)
    scopy = send(spart.at[pl.ds(theirs, ROWS)], screcv, sibling)
    gown[...] = gathered(gsent, gslots)
    gcopy = send(gown, gcrecv, sibling)
    spart[keep_at] = full_dot(dbuf[:, keep_at], rfull[...], DN0)
    gcopy.wait_recv()
    gchips[q] = gown[...] + gcrecv[...]
    gsent = [send(gchips.at[q], gchips.at[q], chip(k)[0]) for k in FAR_FIRST]
    scopy.wait_recv()
    spart[pl.ds(mine, ROWS)] = spart[pl.ds(mine, ROWS)] + screcv[...]
    ssent = scatter(spart, sslots, chip, q, lambda i: pl.ds(pl.multiple_of((c * 8 + i) * PIECE, 8), PIECE))
    gfull[sixteen(r)] = gathered(gsent, gchips)
    gsent = [send(gfull.at[sixteen(r)], gfull.at[sixteen(r)], roller(k)[0]) for k in FAR_FIRST]


    s, t = c * y + (1 - c) * z, c * z + (1 - c) * y
    at = pl.ds(pl.multiple_of(xh * PIECE, 8), PIECE)
    s_own[t, xl, at] = gathered(ssent, sslots)
    ssent = [send(s_own.at[t, xl, at], s_own.at[t, xl, at], plane(kx, kt)) for kx, kt in PLANE]

    def along_s(k):
        return dev(y=(y + c * k) % 4, z=(z + (1 - c) * k) % 4)

    for part in gsent:
        part.wait_recv()
    drain(16)
    for _ in factor_inverse(gfull, inverse):
        pass
    @pl.when(swapped)
    def _():
        swap.wait_recv()
    rsent = [send(r_out.at[c, own_piece], r_out.at[c, own_piece], chip(k)[0]) for k in FAR_FIRST]
    for part in ssent:
        part.wait_recv()
    coeffs = full_dot(s_own[...].reshape(COLS, RANK), inverse[...], DN1)
    ctbuf[c, s] = coeffs.reshape(4, 2, 2 * PIECE, RANK).astype(bf16)
    ssent = [send(ctbuf.at[c, s], ctbuf.at[c, s], along_s(k)) for k in (2, 1, 3)]
    copies = [send(ctbuf.at[c, s], ctbuf.at[c, s], sibling)]

    def keep(core, place, i):
        store = pltpu.make_async_copy(ctbuf.at[core, place], coeffs_out.at[core, place], lsem.at[i])
        store.start()
        stores.append(store)
    keep(c, s, 2)
    for part in rsent:
        part.wait_recv()
    rcopy = send(r_out.at[c], r_out.at[c], sibling)
    rcopy.wait_recv()
    for core in range(2):
        bbuf[core * ROWS:(core + 1) * ROWS] = full_dot(r_out[core], inverse[...], DN1).astype(bf16)
    stores.append(pltpu.make_async_copy(bbuf, basis_out, lsem.at[3]))
    stores[-1].start()

    @pl.when(swapped)
    def _():
        swap.wait_send()
    drain(4)
    for i, (k, part) in enumerate(((1, ssent[1]), (3, ssent[2]), (2, ssent[0]))):
        part.wait_recv()
        have = (s + 4 - k) % 4
        copies.append(send(ctbuf.at[c, have], ctbuf.at[c, have], sibling))
        keep(c, have, 4 + i)
    theirs_s = c * z + (1 - c) * y
    for i, k in enumerate((0, 1, 3, 2)):
        copies[i].wait_recv()
        keep(1 - c, (theirs_s + 4 - k) % 4, 7 + i)
    for store in stores:
        store.wait()
    drain()


def rebuild(basis, coeffs, first, second, rebuilt, new_first, new_second, bbuf, cbuf, obuf, state, sem):
    copies = [pltpu.make_async_copy(basis, bbuf, sem.at[2])]
    copies += [pltpu.make_async_copy(coeffs.at[0, i], cbuf.at[i, 0], sem.at[3 + i]) for i in range(4)]
    copies += [pltpu.make_async_copy(coeffs.at[1, :, i], cbuf.at[i, 1], sem.at[15 + i]) for i in range(4)]
    moved = [pltpu.make_async_copy(first, state.at[0], sem.at[0]), pltpu.make_async_copy(second, state.at[1], sem.at[1])]
    for copy in copies + moved:
        copy.start()
    kept = []
    copies[0].wait()
    for i in range(4):
        copies[1 + i].wait()
        copies[5 + i].wait()
        for j in range(2):
            block = jnp.concatenate([cbuf[i, core, k, j] for core in range(2) for k in range(4)], axis=0)
            obuf[2 * i + j] = lax.dot_general(bbuf[...], block, DN1, preferred_element_type=f32).astype(bf16)
            copy = pltpu.make_async_copy(obuf.at[2 * i + j], rebuilt.at[:, pl.ds((2 * i + j) * COLS, COLS)], sem.at[7 + 2 * i + j])
            copy.start()
            kept.append(copy)
        if i < 2:
            moved[i].wait()
            copy = pltpu.make_async_copy(state.at[i], (new_first, new_second)[i], sem.at[i])
            copy.start()
            kept.append(copy)
    for copy in kept:
        copy.wait()


def local(activations, cotangent, first_moment, second_moment, sketch):
    hbm = pl.BlockSpec(memory_space=pltpu.HBM)
    state = jax.ShapeDtypeStruct((ROWS, COLS), f32)
    first, second, coeffs, basis = pl.pallas_call(
        kernel,
        name="step",
        out_shape=(
            state, state,
            jax.ShapeDtypeStruct((2, 4, 4, 2, 2 * PIECE, RANK), bf16),
            jax.ShapeDtypeStruct((2 * ROWS, RANK), bf16),
        ),
        in_specs=[hbm] * 5,
        out_specs=(hbm,) * 4,
        scratch_shapes=[
            pltpu.VMEM((8, TOK, 640), bf16),
            pltpu.VMEM((TOK, COLS), bf16),
            pltpu.VMEM((640, COLS), f32),
            pltpu.VMEM((8, ROWS, COLS), f32),
            pltpu.VMEM((8, ROWS, COLS), bf16),
            pltpu.VMEM((8, ROWS, COLS), bf16),
            pltpu.VMEM((7, ROWS, COLS), bf16),
            pltpu.VMEM((2, 2, HALF, COLS), bf16),
            pltpu.VMEM((2, XHALF, COLS), bf16),
            pltpu.VMEM((2, 2, ROWS, COLS), bf16),
            pltpu.VMEM((4, XROWS, COLS), bf16),
            pltpu.VMEM((4, XROWS, COLS), bf16),
            pltpu.VMEM((2 * HALF, COLS), bf16),
            pltpu.VMEM((2 * HALF, COLS), bf16),
            pltpu.VMEM((ROWS, COLS), f32),
            pltpu.VMEM((ROWS, COLS), f32),
            pltpu.VMEM((ROWS, COLS), f32),
            pltpu.VMEM((COLS, RANK), f32),
            pltpu.VMEM((ROWS, RANK), f32),
            pltpu.VMEM((7, PIECE, RANK), f32),
            pltpu.VMEM((ROWS, RANK), f32),
            pltpu.VMEM((2, ROWS, RANK), f32),
            pltpu.VMEM((RANK, RANK), f32),
            pltpu.VMEM((16, RANK), f32),
            pltpu.VMEM((16, RANK), f32),
            pltpu.VMEM((8, 16, RANK), f32),
            pltpu.VMEM((8, 16, RANK), f32),
            pltpu.VMEM((RANK, RANK), f32),
            pltpu.VMEM((COLS, RANK), f32),
            pltpu.VMEM((ROWS, RANK), f32),
            pltpu.VMEM((8, PIECE, RANK), f32),
            pltpu.VMEM((4, 2, 2 * PIECE, RANK), f32),
            pltpu.VMEM((RANK, RANK), f32),
            pltpu.VMEM((2, 4, 4, 2, 2 * PIECE, RANK), bf16),
            pltpu.VMEM((2 * ROWS, RANK), bf16),
            pltpu.SemaphoreType.DMA((12,)),
            pltpu.SemaphoreType.DMA((SEMS,)),
            pltpu.SemaphoreType.DMA((SEMS,)),
        ],
        compiler_params=pltpu.CompilerParams(
            collective_id=0, has_side_effects=True, vmem_limit_bytes=58 << 20),
    )(activations, cotangent, first_moment, second_moment, sketch)
    rebuilt, new_first, new_second = pl.pallas_call(
        rebuild,
        name="rebuild",
        out_shape=(jax.ShapeDtypeStruct((COLS, D), bf16), state, state),
        in_specs=[hbm] * 4,
        out_specs=(hbm,) * 3,
        scratch_shapes=[
            pltpu.VMEM((2 * ROWS, RANK), bf16),
            pltpu.VMEM((4, 2, 4, 2, 2 * PIECE, RANK), bf16),
            pltpu.VMEM((8, COLS, COLS), bf16),
            pltpu.VMEM((2, ROWS, COLS), f32),
            pltpu.SemaphoreType.DMA((19,)),
        ],
        compiler_params=pltpu.CompilerParams(vmem_limit_bytes=60 << 20),
    )(basis, coeffs, first, second)
    return new_first, new_second, rebuilt


def solution(mesh):
    placed = (P("fsdp", None), P("fsdp", "roll"), P("fsdp", "roll"), P("fsdp", "roll"), P("roll", None))
    return jax.shard_map(
        local,
        mesh=mesh,
        in_specs=placed,
        out_specs=(P("fsdp", "roll"), P("fsdp", "roll"), P("roll", None)),
        check_vma=False,
    )
```

```python
import functools

import jax
import jax.numpy as jnp
from jax import lax
from jax.experimental import pallas as pl
from jax.experimental.pallas import tpu as pltpu
from jax.sharding import PartitionSpec as P

beta_one = 0.9
beta_two = 0.95
epsilon = 1e-08
hp = lax.Precision.HIGHEST
MESH = pl.DeviceIdType.MESH
f32, bf16 = jnp.float32, jnp.bfloat16
DN0 = (((0,), (0,)), ((), ()))
DN1 = (((1,), (1,)), ((), ()))
DN = (((1,), (0,)), ((), ()))

D, TOK, RANK = 5120, 1024, 128
COLS = 640
ROWS = 320
XROWS = 128
XHALF = XROWS // 2
HALF = (ROWS - XROWS) // 2
PIECE = ROWS // 8
FAR_FIRST = (3, 5, 4, 1, 7, 2, 6)
PLANE = ((2, 2), (1, 2), (3, 2), (2, 1), (2, 3), (1, 1), (3, 3), (1, 3), (3, 1), (2, 0), (0, 2), (1, 0), (3, 0), (0, 1), (0, 3))

ORDER = ((2, 1), (2, 0), (1, 1), (3, 1), (0, 1), (1, 0), (3, 0), (0, 0))
SEMS = 128


def split(v, parts):
    out = []
    for _ in range(parts):
        out.append(v.astype(bf16))
        v = v - out[-1].astype(f32)
    return out


def full_dot(a, b, dims):
    def d(x, y):
        return lax.dot_general(x, y, dims, preferred_element_type=f32)
    a1, a2, a3 = split(a, 3)
    b1, b2, b3 = split(b, 3)
    pair = jnp.concatenate([b1, b2], axis=1 - dims[0][1][0])
    u, w = d(a1, pair), d(a2, pair)
    return u[:, :RANK] + ((u[:, RANK:] + w[:, :RANK]) + (w[:, RANK:] + (d(a1, b3) + d(a3, b1))))


def looped(total, step, body):
    def one(i, carry):
        body(pl.multiple_of(i * step, step))
        return carry
    lax.fori_loop(0, total // step, one, 0, unroll=True)


def split3(v):
    a = v.astype(bf16).astype(f32); v = v - a
    b = v.astype(bf16).astype(f32)
    return a, b, (v - b).astype(bf16).astype(f32)

def factor_inverse(gram_ref, inv_ref):
    lane = lax.broadcasted_iota(jnp.int32, (8, 128), 1)
    sub = lax.broadcasted_iota(jnp.int32, (8, 128), 0)
    panels = [gram_ref[8 * i:8 * i + 8, :] for i in range(16)]

    def down(v, j):
        return jnp.broadcast_to(v[j:j + 1, :], (8, 128))

    for k in range(16):
        panel = panels[k]
        last = k == 15
        cols = [jnp.broadcast_to(panel[:, 8 * k + j:8 * k + j + 1], (8, 128)) for j in range(8)]
        if not last:
            ahead = panels[k + 1]
            acols = [jnp.broadcast_to(ahead[:, 8 * k + j:8 * k + j + 1], (8, 128)) for j in range(8)]
        scale = jnp.zeros((8, 128), f32)
        amul = []
        for j in range(8):
            p = 8 * k + j
            recip = 1.0 / down(cols[j], j)
            scale = jnp.where(sub == j, recip, scale)
            m = jnp.where(sub > j, -cols[j] * recip, 0.0)
            row = down(jnp.where(lane == p, 1.0, panel), j)
            panel = jnp.where((lane == p) & (sub > j), 0.0, panel) + m * row
            if not last:
                am = -acols[j] * recip
                amul.append(am)
            for i in range(j + 1, 8):
                u = down(cols[j], i)
                cols[i] = cols[i] + m * u
                if not last:
                    acols[i] = acols[i] + am * u
        panels[k] = panel
        if not last:
            inside = (lane >= 8 * k) & (lane < 8 * k + 8)
            ext = jnp.where(inside & (lane - 8 * k > sub), 0.0, panel)
            ext = jnp.where(inside & (lane - 8 * k == sub), 1.0, ext)
            ahead = jnp.where(inside, 0.0, ahead)
            for j in range(8):
                ahead = ahead + amul[j] * down(ext, j)
            panels[k + 1] = ahead
            if k < 14:
                lhs = -panel * scale
                a1, a2, a3 = split3(lhs)
                b1, b2, b3 = split3(ext)
                left = jnp.concatenate([a1, a1, a2, a2, a1, a3], axis=0).astype(bf16)
                right = jnp.concatenate([b1, b2, b1, b2, b3, b1], axis=0).astype(bf16)
                upd = lax.dot_general(left, right, DN0, preferred_element_type=f32)
                for i in range(k + 2, 16):
                    panels[i] = jnp.where(inside, 0.0, panels[i]) + upd[8 * i:8 * i + 8, :]
        yield k
    for k in range(16):
        at = lane == sub + 8 * k
        d = jnp.sum(jnp.where(at, panels[k], 0.0), axis=1, keepdims=True)
        m = jnp.where(lane < sub + 8 * k, panels[k], jnp.where(at, 1.0, 0.0))
        inv_ref[8 * k:8 * k + 8, :] = m * lax.rsqrt(d)


def kernel(
    act, cot, first, second, sketch,
    new_first, new_second, coeffs_out, basis_out,
    abuf, cbuf, pbuf, own, psend, crecv, ysend, y1recv, y1x, y2recv, xfsend, xfrecv, xsend, xrecv,
    mbuf, vbuf, dbuf, skbuf, rpart, rrecv, rfull, r_out, gpart, gown, gcrecv, gslots, gchips, gfull,
    spart, screcv, sslots, s_own, inverse, ctbuf, bbuf,
    lsem, ssem, rsem,
):
    f, r = lax.axis_index("fsdp"), lax.axis_index("roll")
    y, xh, c = f // 4, (f // 2) % 2, f % 2
    z, xl = r // 2, r % 2
    q = f // 2

    def dev(y=y, xh=xh, c=c, z=z, xl=xl):
        return {"fsdp": (y * 2 + xh) * 2 + c, "roll": z * 2 + xl}

    sibling = dev(c=1 - c)
    plus, minus = dev(y=(y + 1) % 4), dev(y=(y + 3) % 4)
    across = dev(xh=1 - xh)

    def chip(k):
        other = (q + k) % 8
        return {"fsdp": other * 2 + c, "roll": r}, other

    def roller(k):
        other = (r + k) % 8
        return {"fsdp": f, "roll": other}, other

    def plane(kx, kt):
        other = (xh * 2 + xl + kx) % 4
        return dev(xh=other // 2, xl=other % 2, y=(y + (1 - c) * kt) % 4, z=(z + c * kt) % 4)

    used = [0]

    def remote(src, dst, where):
        i = used[0]
        used[0] += 1
        return pltpu.make_async_remote_copy(
            src_ref=src, dst_ref=dst, send_sem=ssem.at[i], recv_sem=rsem.at[i],
            device_id=where, device_id_type=MESH,
        )

    pending = []

    def send(src, dst, where):
        copy = remote(src, dst, where)
        copy.start()
        pending.append(copy)
        return copy

    def drain(keep=0):
        while len(pending) > keep:
            pending.pop(0).wait_send()

    loads = []
    c_load = pltpu.make_async_copy(cot, cbuf, lsem.at[8])
    c_load.start()
    for k, (dy, dxh) in enumerate(ORDER):
        block = ((y + dy) % 4) * 2 + (xh + dxh) % 2
        load = pltpu.make_async_copy(
            act.at[:, pl.ds(pl.multiple_of(block * 640, 640), 640)], abuf.at[k], lsem.at[k]
        )
        load.start()
        loads.append(load)
    late = [
        pltpu.make_async_copy(first, mbuf, lsem.at[9]),
        pltpu.make_async_copy(second, vbuf, lsem.at[10]),
        pltpu.make_async_copy(sketch, skbuf, lsem.at[11]),
    ]
    for load in late:
        load.start()

    barrier = pltpu.get_barrier_semaphore()
    greeted = [sibling] + [chip(k)[0] for k in range(1, 8)] + [roller(k)[0] for k in range(1, 8)] + [plane(kx, kt) for kx, kt in PLANE]
    for other in greeted:
        pl.semaphore_signal(barrier, inc=1, device_id=other, device_id_type=MESH)
    c_load.wait()

    mine = pl.multiple_of(c * ROWS, ROWS)
    theirs = pl.multiple_of((1 - c) * ROWS, ROWS)
    halves = []

    def compute(k):
        loads[k].wait()
        pbuf[...] = lax.dot_general(abuf[k], cbuf[...], DN0, preferred_element_type=f32)

        def split(o):
            psend[k, pl.ds(o, 32)] = pbuf[pl.ds(theirs + o, 32)].astype(bf16)
            own[k, pl.ds(o, 32)] = pbuf[pl.ds(mine + o, 32)]
        looped(ROWS, 32, split)
        if k == 0:
            pl.semaphore_wait(barrier, len(greeted))
        halves.append(send(psend.at[k], crecv.at[k], sibling))

    step_one, step_two, first_x, one_x, two_x = {}, {}, {}, {}, {}
    ways = (plus, minus)

    def summed(k, at):
        return own[k, at] + crecv[k, at].astype(f32)

    def post(k):
        dy, dxh = ORDER[k]
        halves[k].wait_recv()
        if dxh == 1:
            def add(o):
                xfsend[dy, pl.ds(o, 32)] = summed(k, pl.ds(o, 32)).astype(bf16)
            looped(XROWS, 32, add)
            first_x[dy] = send(xfsend.at[dy], xfrecv.at[dy], across)
        if dy == 2:
            def add(o):
                at = pl.ds(XROWS + o, 32)
                ysend[k, at] = summed(k, at).astype(bf16)
            looped(ROWS - XROWS, 32, add)
            for way, where in enumerate(ways):
                step_one[way, dxh] = send(
                    ysend.at[k, pl.ds(XROWS + way * HALF, HALF)], y1recv.at[way, dxh], where)
        elif dy != 0:
            way = 0 if dy == 1 else 1
            alone = XROWS + (1 - way) * HALF

            def add(o):
                at = pl.ds(alone + o, 32)
                ysend[k, at] = summed(k, at).astype(bf16)
            looped(HALF, 32, add)
            step_two[way, dxh, 1] = send(
                ysend.at[k, pl.ds(alone, HALF)], y2recv.at[way, dxh, pl.ds(alone, HALF)], ways[way])

    def accumulate(dxh, which=(0, 1)):
        for way, dy in ((way, (1, 3)[way]) for way in which):
            k = ORDER.index((dy, dxh))
            step_one[way, dxh].wait_recv()
            start = XROWS + way * HALF

            def add(o):
                at = pl.ds(start + o, 32)
                ysend[k, at] = (summed(k, at) + y1recv[way, dxh, pl.ds(o, 32)].astype(f32)).astype(bf16)
            looped(HALF, 32, add)
            step_two[way, dxh, 0] = send(
                ysend.at[k, pl.ds(start, HALF)], y2recv.at[way, dxh, pl.ds(start, HALF)], ways[way])

    def crossed(dy):
        k = ORDER.index((dy, 0))
        first_x[dy].wait_recv()
        start, size = {2: (0, XROWS), 1: (XHALF, XHALF), 3: (0, XHALF)}[dy]

        def add(o):
            at = pl.ds(start + o, 32)
            ysend[k, at] = (summed(k, at) + xfrecv[dy, at].astype(f32)).astype(bf16)
        looped(size, 32, add)
        if dy == 2:
            for way, where in enumerate(ways):
                one_x[way] = send(ysend.at[k, pl.ds(way * XHALF, XHALF)], y1x.at[way], where)
        else:
            way = 0 if dy == 1 else 1
            two_x[way, 1] = send(ysend.at[k, pl.ds(start, XHALF)], y2recv.at[way, 0, pl.ds(start, XHALF)], ways[way])

    def crossed_accumulate(which=(0, 1)):
        for way, dy in ((way, (1, 3)[way]) for way in which):
            k = ORDER.index((dy, 0))
            one_x[way].wait_recv()
            start = way * XHALF

            def add(o):
                at = pl.ds(start + o, 32)
                ysend[k, at] = (summed(k, at) + xfrecv[dy, at].astype(f32)
                                + y1x[way, pl.ds(o, 32)].astype(f32)).astype(bf16)
            looped(XHALF, 32, add)
            two_x[way, 0] = send(ysend.at[k, pl.ds(start, XHALF)], y2recv.at[way, 0, pl.ds(start, XHALF)], ways[way])

    crossing = []

    def cross(part):
        o0 = XROWS + part * HALF
        for way in range(2):
            step_two[way, 1, 0 if way == part else 1].wait_recv()
        k = ORDER.index((0, 1))

        def add(o):
            at = pl.ds(o0 + o, 32)
            xsend[pl.ds(part * HALF + o, 32)] = (
                summed(k, at) + y2recv[0, 1, at].astype(f32) + y2recv[1, 1, at].astype(f32)).astype(bf16)
        looped(HALF, 32, add)
        crossing.append(send(xsend.at[pl.ds(part * HALF, HALF)], xrecv.at[pl.ds(part * HALF, HALF)], across))

    for k in range(8):
        compute(k)
        if k >= 1:
            post(k - 1)
        if k == 4:
            accumulate(1)
            crossed(2)
        if k == 6:
            accumulate(0, (0,))
            crossed(1)
        if k == 7:
            accumulate(0, (1,))
            crossed(3)
    cross(0)
    cross(1)
    post(7)
    crossed_accumulate()
    for load in late:
        load.wait()

    def adam(at, far):
        grad = summed(7, at) + y2recv[0, 0, at].astype(f32) + y2recv[1, 0, at].astype(f32) + far
        new_m = beta_one * mbuf[at] + (1.0 - beta_one) * grad
        new_v = beta_two * vbuf[at] + (1.0 - beta_two) * grad * grad
        mbuf[at] = new_m
        vbuf[at] = new_v
        dbuf[at] = (new_m * (1.0 / (1.0 - beta_one**20))) / (
            jnp.sqrt(new_v * (1.0 / (1.0 - beta_two**20))) + epsilon)

    stores = []
    first_x[0].wait_recv()
    for way in range(2):
        for part in range(2):
            two_x[way, part].wait_recv()
    looped(XROWS, 16, lambda o: adam(pl.ds(o, 16), xfrecv[0, pl.ds(o, 16)].astype(f32)))

    def sketched(o, n):
        rpart[o:o + n] = full_dot(dbuf[o:o + n], skbuf[...], DN)
    for part in range(2):
        for way in range(2):
            step_two[way, 0, 0 if way == part else 1].wait_recv()
        crossing[part].wait_recv()
        o0 = part * HALF
        sketched(*((0, XROWS) if part == 0 else (XROWS, HALF)))
        looped(HALF, 16, lambda o: adam(pl.ds(XROWS + o0 + o, 16), xrecv[pl.ds(o0 + o, 16)].astype(f32)))
    sketched(XROWS + HALF, HALF)
    for i, (src, dst) in enumerate(((mbuf, new_first), (vbuf, new_second))):
        store = pltpu.make_async_copy(src, dst, lsem.at[i])
        store.start()
        stores.append(store)

    parts = []
    for k in FAR_FIRST:
        where, other = roller(k)
        parts.append(send(rpart.at[pl.ds(pl.multiple_of(other * PIECE, 8), PIECE)], rrecv.at[k - 1], where))
    my_piece = pl.ds(pl.multiple_of(r * PIECE, 8), PIECE)
    total = rpart[my_piece]
    for part in parts:
        part.wait_recv()
    for k in range(7):
        total = total + rrecv[k]
    rfull[my_piece] = total
    parts = [send(rfull.at[my_piece], rfull.at[my_piece], roller(k)[0]) for k in FAR_FIRST]
    swap = remote(rfull.at[my_piece], r_out.at[c, my_piece], dev(y=z, xh=xl, z=y, xl=xh))
    own_piece = pl.ds(pl.multiple_of(q * PIECE, 8), PIECE)
    swapped = (y != z) | (xh != xl)

    @pl.when(swapped)
    def _():
        swap.start()

    @pl.when(jnp.logical_not(swapped))
    def _():
        r_out[c, own_piece] = rfull[my_piece]

    def gathered(sent, slots):
        for part in sent:
            part.wait_recv()
        total = slots[0]
        for k in range(1, 8):
            total = total + slots[k]
        return total

    def scatter(part, slots, peer, me, piece):
        sent = []
        for k in FAR_FIRST:
            where, other = peer(k)
            sent.append(send(part.at[piece(other)], slots.at[me], where))
        slots[me] = part[piece(me)]
        return sent

    def sixteen(i):
        return pl.ds(pl.multiple_of(i * 16, 16), 16)
    piece_rows = rfull[my_piece]
    gpart[...] = lax.dot_general(piece_rows, piece_rows, DN0, precision=hp, preferred_element_type=f32)
    gsent = scatter(gpart, gslots, roller, r, sixteen)

    give_at = pl.ds(pl.multiple_of((1 - c) * 256, 128), 384)
    keep_at = pl.ds(pl.multiple_of(c * 384, 128), 256)
    for part in parts:
        part.wait_recv()
    spart[give_at] = full_dot(dbuf[:, give_at], rfull[...], DN0)
    scopy = send(spart.at[pl.ds(theirs, ROWS)], screcv, sibling)
    gown[...] = gathered(gsent, gslots)
    gcopy = send(gown, gcrecv, sibling)
    spart[keep_at] = full_dot(dbuf[:, keep_at], rfull[...], DN0)
    gcopy.wait_recv()
    gchips[q] = gown[...] + gcrecv[...]
    gsent = [send(gchips.at[q], gchips.at[q], chip(k)[0]) for k in FAR_FIRST]
    scopy.wait_recv()
    spart[pl.ds(mine, ROWS)] = spart[pl.ds(mine, ROWS)] + screcv[...]
    ssent = scatter(spart, sslots, chip, q, lambda i: pl.ds(pl.multiple_of((c * 8 + i) * PIECE, 8), PIECE))
    gfull[sixteen(r)] = gathered(gsent, gchips)
    gsent = [send(gfull.at[sixteen(r)], gfull.at[sixteen(r)], roller(k)[0]) for k in FAR_FIRST]


    s, t = c * y + (1 - c) * z, c * z + (1 - c) * y
    at = pl.ds(pl.multiple_of(xh * PIECE, 8), PIECE)
    s_own[t, xl, at] = gathered(ssent, sslots)
    ssent = [send(s_own.at[t, xl, at], s_own.at[t, xl, at], plane(kx, kt)) for kx, kt in PLANE]

    def along_s(k):
        return dev(y=(y + c * k) % 4, z=(z + (1 - c) * k) % 4)

    for part in gsent:
        part.wait_recv()
    drain(16)
    for _ in factor_inverse(gfull, inverse):
        pass
    @pl.when(swapped)
    def _():
        swap.wait_recv()
    rsent = [send(r_out.at[c, own_piece], r_out.at[c, own_piece], chip(k)[0]) for k in FAR_FIRST]
    for part in ssent:
        part.wait_recv()
    coeffs = full_dot(s_own[...].reshape(COLS, RANK), inverse[...], DN1)
    ctbuf[c, s] = coeffs.reshape(4, 2, 2 * PIECE, RANK).astype(bf16)
    ssent = [send(ctbuf.at[c, s], ctbuf.at[c, s], along_s(k)) for k in (2, 1, 3)]
    copies = [send(ctbuf.at[c, s], ctbuf.at[c, s], sibling)]

    def keep(core, place, i):
        store = pltpu.make_async_copy(ctbuf.at[core, place], coeffs_out.at[core, place], lsem.at[i])
        store.start()
        stores.append(store)
    keep(c, s, 2)
    for part in rsent:
        part.wait_recv()
    rcopy = send(r_out.at[c], r_out.at[c], sibling)
    rcopy.wait_recv()
    for core in range(2):
        bbuf[core * ROWS:(core + 1) * ROWS] = full_dot(r_out[core], inverse[...], DN1).astype(bf16)
    stores.append(pltpu.make_async_copy(bbuf, basis_out, lsem.at[3]))
    stores[-1].start()

    @pl.when(swapped)
    def _():
        swap.wait_send()
    drain(4)
    for i, (k, part) in enumerate(((1, ssent[1]), (3, ssent[2]), (2, ssent[0]))):
        part.wait_recv()
        have = (s + 4 - k) % 4
        copies.append(send(ctbuf.at[c, have], ctbuf.at[c, have], sibling))
        keep(c, have, 4 + i)
    theirs_s = c * z + (1 - c) * y
    for i, k in enumerate((0, 1, 3, 2)):
        copies[i].wait_recv()
        keep(1 - c, (theirs_s + 4 - k) % 4, 7 + i)
    for store in stores:
        store.wait()
    drain()


def rebuild(basis, coeffs, first, second, rebuilt, new_first, new_second, bbuf, cbuf, obuf, state, sem):
    copies = [pltpu.make_async_copy(basis, bbuf, sem.at[2])]
    copies += [pltpu.make_async_copy(coeffs.at[0, i], cbuf.at[i, 0], sem.at[3 + i]) for i in range(4)]
    copies += [pltpu.make_async_copy(coeffs.at[1, :, i], cbuf.at[i, 1], sem.at[15 + i]) for i in range(4)]
    moved = [pltpu.make_async_copy(first, state.at[0], sem.at[0]), pltpu.make_async_copy(second, state.at[1], sem.at[1])]
    for copy in copies + moved:
        copy.start()
    kept = []
    copies[0].wait()
    for i in range(4):
        copies[1 + i].wait()
        copies[5 + i].wait()
        for j in range(2):
            block = jnp.concatenate([cbuf[i, core, k, j] for core in range(2) for k in range(4)], axis=0)
            obuf[2 * i + j] = lax.dot_general(bbuf[...], block, DN1, preferred_element_type=f32).astype(bf16)
            copy = pltpu.make_async_copy(obuf.at[2 * i + j], rebuilt.at[:, pl.ds((2 * i + j) * COLS, COLS)], sem.at[7 + 2 * i + j])
            copy.start()
            kept.append(copy)
        if i == 1:
            for j, kept_state in enumerate((new_first, new_second)):
                moved[j].wait()
                copy = pltpu.make_async_copy(state.at[j], kept_state, sem.at[j])
                copy.start()
                kept.append(copy)
    for copy in kept:
        copy.wait()


def local(activations, cotangent, first_moment, second_moment, sketch):
    hbm = pl.BlockSpec(memory_space=pltpu.HBM)
    state = jax.ShapeDtypeStruct((ROWS, COLS), f32)
    first, second, coeffs, basis = pl.pallas_call(
        kernel,
        name="step",
        out_shape=(
            state, state,
            jax.ShapeDtypeStruct((2, 4, 4, 2, 2 * PIECE, RANK), bf16),
            jax.ShapeDtypeStruct((2 * ROWS, RANK), bf16),
        ),
        in_specs=[hbm] * 5,
        out_specs=(hbm,) * 4,
        scratch_shapes=[
            pltpu.VMEM((8, TOK, 640), bf16),
            pltpu.VMEM((TOK, COLS), bf16),
            pltpu.VMEM((640, COLS), f32),
            pltpu.VMEM((8, ROWS, COLS), f32),
            pltpu.VMEM((8, ROWS, COLS), bf16),
            pltpu.VMEM((8, ROWS, COLS), bf16),
            pltpu.VMEM((7, ROWS, COLS), bf16),
            pltpu.VMEM((2, 2, HALF, COLS), bf16),
            pltpu.VMEM((2, XHALF, COLS), bf16),
            pltpu.VMEM((2, 2, ROWS, COLS), bf16),
            pltpu.VMEM((4, XROWS, COLS), bf16),
            pltpu.VMEM((4, XROWS, COLS), bf16),
            pltpu.VMEM((2 * HALF, COLS), bf16),
            pltpu.VMEM((2 * HALF, COLS), bf16),
            pltpu.VMEM((ROWS, COLS), f32),
            pltpu.VMEM((ROWS, COLS), f32),
            pltpu.VMEM((ROWS, COLS), f32),
            pltpu.VMEM((COLS, RANK), f32),
            pltpu.VMEM((ROWS, RANK), f32),
            pltpu.VMEM((7, PIECE, RANK), f32),
            pltpu.VMEM((ROWS, RANK), f32),
            pltpu.VMEM((2, ROWS, RANK), f32),
            pltpu.VMEM((RANK, RANK), f32),
            pltpu.VMEM((16, RANK), f32),
            pltpu.VMEM((16, RANK), f32),
            pltpu.VMEM((8, 16, RANK), f32),
            pltpu.VMEM((8, 16, RANK), f32),
            pltpu.VMEM((RANK, RANK), f32),
            pltpu.VMEM((COLS, RANK), f32),
            pltpu.VMEM((ROWS, RANK), f32),
            pltpu.VMEM((8, PIECE, RANK), f32),
            pltpu.VMEM((4, 2, 2 * PIECE, RANK), f32),
            pltpu.VMEM((RANK, RANK), f32),
            pltpu.VMEM((2, 4, 4, 2, 2 * PIECE, RANK), bf16),
            pltpu.VMEM((2 * ROWS, RANK), bf16),
            pltpu.SemaphoreType.DMA((12,)),
            pltpu.SemaphoreType.DMA((SEMS,)),
            pltpu.SemaphoreType.DMA((SEMS,)),
        ],
        compiler_params=pltpu.CompilerParams(
            collective_id=0, has_side_effects=True, vmem_limit_bytes=58 << 20),
    )(activations, cotangent, first_moment, second_moment, sketch)
    rebuilt, new_first, new_second = pl.pallas_call(
        rebuild,
        name="rebuild",
        out_shape=(jax.ShapeDtypeStruct((COLS, D), bf16), state, state),
        in_specs=[hbm] * 4,
        out_specs=(hbm,) * 3,
        scratch_shapes=[
            pltpu.VMEM((2 * ROWS, RANK), bf16),
            pltpu.VMEM((4, 2, 4, 2, 2 * PIECE, RANK), bf16),
            pltpu.VMEM((8, COLS, COLS), bf16),
            pltpu.VMEM((2, ROWS, COLS), f32),
            pltpu.SemaphoreType.DMA((19,)),
        ],
        compiler_params=pltpu.CompilerParams(vmem_limit_bytes=60 << 20),
    )(basis, coeffs, first, second)
    return new_first, new_second, rebuilt


def solution(mesh):
    placed = (P("fsdp", None), P("fsdp", "roll"), P("fsdp", "roll"), P("fsdp", "roll"), P("roll", None))
    return jax.shard_map(
        local,
        mesh=mesh,
        in_specs=placed,
        out_specs=(P("fsdp", "roll"), P("fsdp", "roll"), P("roll", None)),
        check_vma=False,
    )
```

```python
import functools

import jax
import jax.numpy as jnp
from jax import lax
from jax.experimental import pallas as pl
from jax.experimental.pallas import tpu as pltpu
from jax.sharding import PartitionSpec as P

beta_one = 0.9
beta_two = 0.95
epsilon = 1e-08
hp = lax.Precision.HIGHEST
MESH = pl.DeviceIdType.MESH
f32, bf16 = jnp.float32, jnp.bfloat16
DN0 = (((0,), (0,)), ((), ()))
DN1 = (((1,), (1,)), ((), ()))
DN = (((1,), (0,)), ((), ()))

D, TOK, RANK = 5120, 1024, 128
COLS = 640
ROWS = 320
XROWS = 128
XHALF = XROWS // 2
HALF = (ROWS - XROWS) // 2
PIECE = ROWS // 8
FAR_FIRST = (3, 5, 4, 1, 7, 2, 6)
PLANE = ((2, 2), (1, 2), (3, 2), (2, 1), (2, 3), (1, 1), (3, 3), (1, 3), (3, 1), (2, 0), (0, 2), (1, 0), (3, 0), (0, 1), (0, 3))

ORDER = ((2, 1), (2, 0), (1, 1), (3, 1), (0, 1), (1, 0), (3, 0), (0, 0))
SEMS = 128


def split(v, parts):
    out = []
    for _ in range(parts):
        out.append(v.astype(bf16))
        v = v - out[-1].astype(f32)
    return out


def full_dot(a, b, dims):
    def d(x, y):
        return lax.dot_general(x, y, dims, preferred_element_type=f32)
    a1, a2, a3 = split(a, 3)
    b1, b2, b3 = split(b, 3)
    pair = jnp.concatenate([b1, b2], axis=1 - dims[0][1][0])
    u, w = d(a1, pair), d(a2, pair)
    return u[:, :RANK] + ((u[:, RANK:] + w[:, :RANK]) + (w[:, RANK:] + (d(a1, b3) + d(a3, b1))))


def looped(total, step, body):
    def one(i, carry):
        body(pl.multiple_of(i * step, step))
        return carry
    lax.fori_loop(0, total // step, one, 0, unroll=True)


def split3(v):
    a = v.astype(bf16).astype(f32); v = v - a
    b = v.astype(bf16).astype(f32)
    return a, b, (v - b).astype(bf16).astype(f32)

def factor_inverse(gram_ref, inv_ref):
    lane = lax.broadcasted_iota(jnp.int32, (8, 128), 1)
    sub = lax.broadcasted_iota(jnp.int32, (8, 128), 0)
    panels = [gram_ref[8 * i:8 * i + 8, :] for i in range(16)]

    def down(v, j):
        return jnp.broadcast_to(v[j:j + 1, :], (8, 128))

    for k in range(16):
        panel = panels[k]
        last = k == 15
        cols = [jnp.broadcast_to(panel[:, 8 * k + j:8 * k + j + 1], (8, 128)) for j in range(8)]
        if not last:
            ahead = panels[k + 1]
            acols = [jnp.broadcast_to(ahead[:, 8 * k + j:8 * k + j + 1], (8, 128)) for j in range(8)]
        scale = jnp.zeros((8, 128), f32)
        amul = []
        for j in range(8):
            p = 8 * k + j
            recip = 1.0 / down(cols[j], j)
            scale = jnp.where(sub == j, recip, scale)
            m = jnp.where(sub > j, -cols[j] * recip, 0.0)
            row = down(jnp.where(lane == p, 1.0, panel), j)
            panel = jnp.where((lane == p) & (sub > j), 0.0, panel) + m * row
            if not last:
                am = -acols[j] * recip
                amul.append(am)
            for i in range(j + 1, 8):
                u = down(cols[j], i)
                cols[i] = cols[i] + m * u
                if not last:
                    acols[i] = acols[i] + am * u
        panels[k] = panel
        if not last:
            inside = (lane >= 8 * k) & (lane < 8 * k + 8)
            ext = jnp.where(inside & (lane - 8 * k > sub), 0.0, panel)
            ext = jnp.where(inside & (lane - 8 * k == sub), 1.0, ext)
            ahead = jnp.where(inside, 0.0, ahead)
            for j in range(8):
                ahead = ahead + amul[j] * down(ext, j)
            panels[k + 1] = ahead
            if k < 14:
                lhs = -panel * scale
                a1, a2, a3 = split3(lhs)
                b1, b2, b3 = split3(ext)
                left = jnp.concatenate([a1, a1, a2, a2, a1, a3], axis=0).astype(bf16)
                right = jnp.concatenate([b1, b2, b1, b2, b3, b1], axis=0).astype(bf16)
                upd = lax.dot_general(left, right, DN0, preferred_element_type=f32)
                for i in range(k + 2, 16):
                    panels[i] = jnp.where(inside, 0.0, panels[i]) + upd[8 * i:8 * i + 8, :]
        yield k
    for k in range(16):
        at = lane == sub + 8 * k
        d = jnp.sum(jnp.where(at, panels[k], 0.0), axis=1, keepdims=True)
        m = jnp.where(lane < sub + 8 * k, panels[k], jnp.where(at, 1.0, 0.0))
        inv_ref[8 * k:8 * k + 8, :] = m * lax.rsqrt(d)


def kernel(
    act, cot, first, second, sketch,
    new_first, new_second, coeffs_out, basis_out,
    abuf, cbuf, pbuf, own, psend, crecv, ysend, y1recv, y1x, y2recv, xfsend, xfrecv, xsend, xrecv,
    mbuf, vbuf, dbuf, skbuf, rpart, rrecv, rfull, r_out, gpart, gown, gcrecv, gslots, gchips, gfull,
    spart, screcv, sslots, s_own, inverse, ctbuf, bbuf,
    lsem, ssem, rsem,
):
    f, r = lax.axis_index("fsdp"), lax.axis_index("roll")
    y, xh, c = f // 4, (f // 2) % 2, f % 2
    z, xl = r // 2, r % 2
    q = f // 2

    def dev(y=y, xh=xh, c=c, z=z, xl=xl):
        return {"fsdp": (y * 2 + xh) * 2 + c, "roll": z * 2 + xl}

    sibling = dev(c=1 - c)
    plus, minus = dev(y=(y + 1) % 4), dev(y=(y + 3) % 4)
    across = dev(xh=1 - xh)

    def chip(k):
        other = (q + k) % 8
        return {"fsdp": other * 2 + c, "roll": r}, other

    def roller(k):
        other = (r + k) % 8
        return {"fsdp": f, "roll": other}, other

    def plane(kx, kt):
        other = (xh * 2 + xl + kx) % 4
        return dev(xh=other // 2, xl=other % 2, y=(y + (1 - c) * kt) % 4, z=(z + c * kt) % 4)

    used = [0]

    def remote(src, dst, where):
        i = used[0]
        used[0] += 1
        return pltpu.make_async_remote_copy(
            src_ref=src, dst_ref=dst, send_sem=ssem.at[i], recv_sem=rsem.at[i],
            device_id=where, device_id_type=MESH,
        )

    pending = []

    def send(src, dst, where):
        copy = remote(src, dst, where)
        copy.start()
        pending.append(copy)
        return copy

    def drain(keep=0):
        while len(pending) > keep:
            pending.pop(0).wait_send()

    loads = []
    c_load = pltpu.make_async_copy(cot, cbuf, lsem.at[8])
    c_load.start()
    for k, (dy, dxh) in enumerate(ORDER):
        block = ((y + dy) % 4) * 2 + (xh + dxh) % 2
        load = pltpu.make_async_copy(
            act.at[:, pl.ds(pl.multiple_of(block * 640, 640), 640)], abuf.at[k], lsem.at[k]
        )
        load.start()
        loads.append(load)
    late = [
        pltpu.make_async_copy(first, mbuf, lsem.at[9]),
        pltpu.make_async_copy(second, vbuf, lsem.at[10]),
        pltpu.make_async_copy(sketch, skbuf, lsem.at[11]),
    ]
    for load in late:
        load.start()

    barrier = pltpu.get_barrier_semaphore()
    greeted = [sibling] + [chip(k)[0] for k in range(1, 8)] + [roller(k)[0] for k in range(1, 8)] + [plane(kx, kt) for kx, kt in PLANE]
    for other in greeted:
        pl.semaphore_signal(barrier, inc=1, device_id=other, device_id_type=MESH)
    c_load.wait()

    mine = pl.multiple_of(c * ROWS, ROWS)
    theirs = pl.multiple_of((1 - c) * ROWS, ROWS)
    halves = []

    def compute(k):
        loads[k].wait()
        pbuf[...] = lax.dot_general(abuf[k], cbuf[...], DN0, preferred_element_type=f32)

        def split(o):
            psend[k, pl.ds(o, 32)] = pbuf[pl.ds(theirs + o, 32)].astype(bf16)
            own[k, pl.ds(o, 32)] = pbuf[pl.ds(mine + o, 32)]
        looped(ROWS, 32, split)
        if k == 0:
            pl.semaphore_wait(barrier, len(greeted))
        halves.append(send(psend.at[k], crecv.at[k], sibling))

    step_one, step_two, first_x, one_x, two_x = {}, {}, {}, {}, {}
    ways = (plus, minus)

    def summed(k, at):
        return own[k, at] + crecv[k, at].astype(f32)

    def post(k):
        dy, dxh = ORDER[k]
        halves[k].wait_recv()
        if dxh == 1:
            def add(o):
                xfsend[dy, pl.ds(o, 32)] = summed(k, pl.ds(o, 32)).astype(bf16)
            looped(XROWS, 32, add)
            first_x[dy] = send(xfsend.at[dy], xfrecv.at[dy], across)
        if dy == 2:
            def add(o):
                at = pl.ds(XROWS + o, 32)
                ysend[k, at] = summed(k, at).astype(bf16)
            looped(ROWS - XROWS, 32, add)
            for way, where in enumerate(ways):
                step_one[way, dxh] = send(
                    ysend.at[k, pl.ds(XROWS + way * HALF, HALF)], y1recv.at[way, dxh], where)
        elif dy != 0:
            way = 0 if dy == 1 else 1
            alone = XROWS + (1 - way) * HALF

            def add(o):
                at = pl.ds(alone + o, 32)
                ysend[k, at] = summed(k, at).astype(bf16)
            looped(HALF, 32, add)
            step_two[way, dxh, 1] = send(
                ysend.at[k, pl.ds(alone, HALF)], y2recv.at[way, dxh, pl.ds(alone, HALF)], ways[way])

    def accumulate(dxh, which=(0, 1)):
        for way, dy in ((way, (1, 3)[way]) for way in which):
            k = ORDER.index((dy, dxh))
            step_one[way, dxh].wait_recv()
            start = XROWS + way * HALF

            def add(o):
                at = pl.ds(start + o, 32)
                ysend[k, at] = (summed(k, at) + y1recv[way, dxh, pl.ds(o, 32)].astype(f32)).astype(bf16)
            looped(HALF, 32, add)
            step_two[way, dxh, 0] = send(
                ysend.at[k, pl.ds(start, HALF)], y2recv.at[way, dxh, pl.ds(start, HALF)], ways[way])

    def crossed(dy):
        k = ORDER.index((dy, 0))
        first_x[dy].wait_recv()
        start, size = {2: (0, XROWS), 1: (XHALF, XHALF), 3: (0, XHALF)}[dy]

        def add(o):
            at = pl.ds(start + o, 32)
            ysend[k, at] = (summed(k, at) + xfrecv[dy, at].astype(f32)).astype(bf16)
        looped(size, 32, add)
        if dy == 2:
            for way, where in enumerate(ways):
                one_x[way] = send(ysend.at[k, pl.ds(way * XHALF, XHALF)], y1x.at[way], where)
        else:
            way = 0 if dy == 1 else 1
            two_x[way, 1] = send(ysend.at[k, pl.ds(start, XHALF)], y2recv.at[way, 0, pl.ds(start, XHALF)], ways[way])

    def crossed_accumulate(which=(0, 1)):
        for way, dy in ((way, (1, 3)[way]) for way in which):
            k = ORDER.index((dy, 0))
            one_x[way].wait_recv()
            start = way * XHALF

            def add(o):
                at = pl.ds(start + o, 32)
                ysend[k, at] = (summed(k, at) + xfrecv[dy, at].astype(f32)
                                + y1x[way, pl.ds(o, 32)].astype(f32)).astype(bf16)
            looped(XHALF, 32, add)
            two_x[way, 0] = send(ysend.at[k, pl.ds(start, XHALF)], y2recv.at[way, 0, pl.ds(start, XHALF)], ways[way])

    crossing = []

    def cross(part):
        o0 = XROWS + part * HALF
        for way in range(2):
            step_two[way, 1, 0 if way == part else 1].wait_recv()
        k = ORDER.index((0, 1))

        def add(o):
            at = pl.ds(o0 + o, 32)
            xsend[pl.ds(part * HALF + o, 32)] = (
                summed(k, at) + y2recv[0, 1, at].astype(f32) + y2recv[1, 1, at].astype(f32)).astype(bf16)
        looped(HALF, 32, add)
        crossing.append(send(xsend.at[pl.ds(part * HALF, HALF)], xrecv.at[pl.ds(part * HALF, HALF)], across))

    for k in range(8):
        compute(k)
        if k >= 1:
            post(k - 1)
        if k == 4:
            accumulate(1)
            crossed(2)
        if k == 6:
            accumulate(0, (0,))
            crossed(1)
        if k == 7:
            accumulate(0, (1,))
            crossed(3)
    cross(0)
    cross(1)
    post(7)
    crossed_accumulate()
    for load in late:
        load.wait()

    def adam(at, far):
        grad = summed(7, at) + y2recv[0, 0, at].astype(f32) + y2recv[1, 0, at].astype(f32) + far
        new_m = beta_one * mbuf[at] + (1.0 - beta_one) * grad
        new_v = beta_two * vbuf[at] + (1.0 - beta_two) * grad * grad
        mbuf[at] = new_m
        vbuf[at] = new_v
        dbuf[at] = (new_m * (1.0 / (1.0 - beta_one**20))) / (
            jnp.sqrt(new_v * (1.0 / (1.0 - beta_two**20))) + epsilon)

    stores = []
    first_x[0].wait_recv()
    for way in range(2):
        for part in range(2):
            two_x[way, part].wait_recv()
    looped(XROWS, 16, lambda o: adam(pl.ds(o, 16), xfrecv[0, pl.ds(o, 16)].astype(f32)))

    def sketched(o, n):
        rpart[o:o + n] = full_dot(dbuf[o:o + n], skbuf[...], DN)
    for part in range(2):
        for way in range(2):
            step_two[way, 0, 0 if way == part else 1].wait_recv()
        crossing[part].wait_recv()
    sketched(0, XROWS)
    looped(2 * HALF, 16, lambda o: adam(pl.ds(XROWS + o, 16), xrecv[pl.ds(o, 16)].astype(f32)))
    sketched(XROWS, ROWS - XROWS)
    for i, (src, dst) in enumerate(((mbuf, new_first), (vbuf, new_second))):
        store = pltpu.make_async_copy(src, dst, lsem.at[i])
        store.start()
        stores.append(store)

    parts = []
    for k in FAR_FIRST:
        where, other = roller(k)
        parts.append(send(rpart.at[pl.ds(pl.multiple_of(other * PIECE, 8), PIECE)], rrecv.at[k - 1], where))
    my_piece = pl.ds(pl.multiple_of(r * PIECE, 8), PIECE)
    total = rpart[my_piece]
    for part in parts:
        part.wait_recv()
    for k in range(7):
        total = total + rrecv[k]
    rfull[my_piece] = total
    parts = [send(rfull.at[my_piece], rfull.at[my_piece], roller(k)[0]) for k in FAR_FIRST]
    swap = remote(rfull.at[my_piece], r_out.at[c, my_piece], dev(y=z, xh=xl, z=y, xl=xh))
    own_piece = pl.ds(pl.multiple_of(q * PIECE, 8), PIECE)
    swapped = (y != z) | (xh != xl)

    @pl.when(swapped)
    def _():
        swap.start()

    @pl.when(jnp.logical_not(swapped))
    def _():
        r_out[c, own_piece] = rfull[my_piece]

    def gathered(sent, slots):
        for part in sent:
            part.wait_recv()
        total = slots[0]
        for k in range(1, 8):
            total = total + slots[k]
        return total

    def scatter(part, slots, peer, me, piece):
        sent = []
        for k in FAR_FIRST:
            where, other = peer(k)
            sent.append(send(part.at[piece(other)], slots.at[me], where))
        slots[me] = part[piece(me)]
        return sent

    def sixteen(i):
        return pl.ds(pl.multiple_of(i * 16, 16), 16)
    piece_rows = rfull[my_piece]
    gpart[...] = lax.dot_general(piece_rows, piece_rows, DN0, precision=hp, preferred_element_type=f32)
    gsent = scatter(gpart, gslots, roller, r, sixteen)

    give_at = pl.ds(pl.multiple_of((1 - c) * 256, 128), 384)
    keep_at = pl.ds(pl.multiple_of(c * 384, 128), 256)
    for part in parts:
        part.wait_recv()
    spart[give_at] = full_dot(dbuf[:, give_at], rfull[...], DN0)
    scopy = send(spart.at[pl.ds(theirs, ROWS)], screcv, sibling)
    gown[...] = gathered(gsent, gslots)
    gcopy = send(gown, gcrecv, sibling)
    spart[keep_at] = full_dot(dbuf[:, keep_at], rfull[...], DN0)
    gcopy.wait_recv()
    gchips[q] = gown[...] + gcrecv[...]
    gsent = [send(gchips.at[q], gchips.at[q], chip(k)[0]) for k in FAR_FIRST]
    scopy.wait_recv()
    spart[pl.ds(mine, ROWS)] = spart[pl.ds(mine, ROWS)] + screcv[...]
    ssent = scatter(spart, sslots, chip, q, lambda i: pl.ds(pl.multiple_of((c * 8 + i) * PIECE, 8), PIECE))
    gfull[sixteen(r)] = gathered(gsent, gchips)
    gsent = [send(gfull.at[sixteen(r)], gfull.at[sixteen(r)], roller(k)[0]) for k in FAR_FIRST]


    s, t = c * y + (1 - c) * z, c * z + (1 - c) * y
    at = pl.ds(pl.multiple_of(xh * PIECE, 8), PIECE)
    s_own[t, xl, at] = gathered(ssent, sslots)
    ssent = [send(s_own.at[t, xl, at], s_own.at[t, xl, at], plane(kx, kt)) for kx, kt in PLANE]

    def along_s(k):
        return dev(y=(y + c * k) % 4, z=(z + (1 - c) * k) % 4)

    for part in gsent:
        part.wait_recv()
    drain(16)
    for _ in factor_inverse(gfull, inverse):
        pass
    for part in ssent:
        part.wait_recv()
    coeffs = full_dot(s_own[...].reshape(COLS, RANK), inverse[...], DN1)
    ctbuf[c, s] = coeffs.reshape(4, 2, 2 * PIECE, RANK).astype(bf16)
    ssent = [send(ctbuf.at[c, s], ctbuf.at[c, s], along_s(k)) for k in (2, 1, 3)]
    copies = [send(ctbuf.at[c, s], ctbuf.at[c, s], sibling)]

    def keep(core, place, i):
        store = pltpu.make_async_copy(ctbuf.at[core, place], coeffs_out.at[core, place], lsem.at[i])
        store.start()
        stores.append(store)
    keep(c, s, 2)
    @pl.when(swapped)
    def _():
        swap.wait_recv()
    rsent = [send(r_out.at[c, own_piece], r_out.at[c, own_piece], chip(k)[0]) for k in FAR_FIRST]

    @pl.when(swapped)
    def _():
        swap.wait_send()
    drain(11)
    for i, (k, part) in enumerate(((1, ssent[1]), (3, ssent[2]), (2, ssent[0]))):
        part.wait_recv()
        have = (s + 4 - k) % 4
        copies.append(send(ctbuf.at[c, have], ctbuf.at[c, have], sibling))
        keep(c, have, 4 + i)
        if k == 3:
            for part in rsent:
                part.wait_recv()
            rcopy = send(r_out.at[c], r_out.at[c], sibling)
    rcopy.wait_recv()
    for core in range(2):
        bbuf[core * ROWS:(core + 1) * ROWS] = full_dot(r_out[core], inverse[...], DN1).astype(bf16)
    stores.append(pltpu.make_async_copy(bbuf, basis_out, lsem.at[3]))
    stores[-1].start()
    theirs_s = c * z + (1 - c) * y
    for i, k in enumerate((0, 1, 3, 2)):
        copies[i].wait_recv()
        keep(1 - c, (theirs_s + 4 - k) % 4, 7 + i)
    for store in stores:
        store.wait()
    drain()


def rebuild(basis, coeffs, first, second, rebuilt, new_first, new_second, bbuf, cbuf, obuf, state, sem):
    copies = [pltpu.make_async_copy(basis, bbuf, sem.at[2])]
    copies += [pltpu.make_async_copy(coeffs.at[0, i], cbuf.at[i, 0], sem.at[3 + i]) for i in range(4)]
    copies += [pltpu.make_async_copy(coeffs.at[1, :, i], cbuf.at[i, 1], sem.at[15 + i]) for i in range(4)]
    moved = [pltpu.make_async_copy(first, state.at[0], sem.at[0]), pltpu.make_async_copy(second, state.at[1], sem.at[1])]
    for copy in copies + moved:
        copy.start()
    kept = []
    copies[0].wait()
    for i in range(4):
        copies[1 + i].wait()
        copies[5 + i].wait()
        for j in range(2):
            block = jnp.concatenate([cbuf[i, core, k, j] for core in range(2) for k in range(4)], axis=0)
            obuf[2 * i + j] = lax.dot_general(bbuf[...], block, DN1, preferred_element_type=f32).astype(bf16)
            copy = pltpu.make_async_copy(obuf.at[2 * i + j], rebuilt.at[:, pl.ds((2 * i + j) * COLS, COLS)], sem.at[7 + 2 * i + j])
            copy.start()
            kept.append(copy)
        if i < 2:
            moved[i].wait()
            copy = pltpu.make_async_copy(state.at[i], (new_first, new_second)[i], sem.at[i])
            copy.start()
            kept.append(copy)
    for copy in kept:
        copy.wait()


def local(activations, cotangent, first_moment, second_moment, sketch):
    hbm = pl.BlockSpec(memory_space=pltpu.HBM)
    state = jax.ShapeDtypeStruct((ROWS, COLS), f32)
    first, second, coeffs, basis = pl.pallas_call(
        kernel,
        name="step",
        out_shape=(
            state, state,
            jax.ShapeDtypeStruct((2, 4, 4, 2, 2 * PIECE, RANK), bf16),
            jax.ShapeDtypeStruct((2 * ROWS, RANK), bf16),
        ),
        in_specs=[hbm] * 5,
        out_specs=(hbm,) * 4,
        scratch_shapes=[
            pltpu.VMEM((8, TOK, 640), bf16),
            pltpu.VMEM((TOK, COLS), bf16),
            pltpu.VMEM((640, COLS), f32),
            pltpu.VMEM((8, ROWS, COLS), f32),
            pltpu.VMEM((8, ROWS, COLS), bf16),
            pltpu.VMEM((8, ROWS, COLS), bf16),
            pltpu.VMEM((7, ROWS, COLS), bf16),
            pltpu.VMEM((2, 2, HALF, COLS), bf16),
            pltpu.VMEM((2, XHALF, COLS), bf16),
            pltpu.VMEM((2, 2, ROWS, COLS), bf16),
            pltpu.VMEM((4, XROWS, COLS), bf16),
            pltpu.VMEM((4, XROWS, COLS), bf16),
            pltpu.VMEM((2 * HALF, COLS), bf16),
            pltpu.VMEM((2 * HALF, COLS), bf16),
            pltpu.VMEM((ROWS, COLS), f32),
            pltpu.VMEM((ROWS, COLS), f32),
            pltpu.VMEM((ROWS, COLS), f32),
            pltpu.VMEM((COLS, RANK), f32),
            pltpu.VMEM((ROWS, RANK), f32),
            pltpu.VMEM((7, PIECE, RANK), f32),
            pltpu.VMEM((ROWS, RANK), f32),
            pltpu.VMEM((2, ROWS, RANK), f32),
            pltpu.VMEM((RANK, RANK), f32),
            pltpu.VMEM((16, RANK), f32),
            pltpu.VMEM((16, RANK), f32),
            pltpu.VMEM((8, 16, RANK), f32),
            pltpu.VMEM((8, 16, RANK), f32),
            pltpu.VMEM((RANK, RANK), f32),
            pltpu.VMEM((COLS, RANK), f32),
            pltpu.VMEM((ROWS, RANK), f32),
            pltpu.VMEM((8, PIECE, RANK), f32),
            pltpu.VMEM((4, 2, 2 * PIECE, RANK), f32),
            pltpu.VMEM((RANK, RANK), f32),
            pltpu.VMEM((2, 4, 4, 2, 2 * PIECE, RANK), bf16),
            pltpu.VMEM((2 * ROWS, RANK), bf16),
            pltpu.SemaphoreType.DMA((12,)),
            pltpu.SemaphoreType.DMA((SEMS,)),
            pltpu.SemaphoreType.DMA((SEMS,)),
        ],
        compiler_params=pltpu.CompilerParams(
            collective_id=0, has_side_effects=True, vmem_limit_bytes=58 << 20),
    )(activations, cotangent, first_moment, second_moment, sketch)
    rebuilt, new_first, new_second = pl.pallas_call(
        rebuild,
        name="rebuild",
        out_shape=(jax.ShapeDtypeStruct((COLS, D), bf16), state, state),
        in_specs=[hbm] * 4,
        out_specs=(hbm,) * 3,
        scratch_shapes=[
            pltpu.VMEM((2 * ROWS, RANK), bf16),
            pltpu.VMEM((4, 2, 4, 2, 2 * PIECE, RANK), bf16),
            pltpu.VMEM((8, COLS, COLS), bf16),
            pltpu.VMEM((2, ROWS, COLS), f32),
            pltpu.SemaphoreType.DMA((19,)),
        ],
        compiler_params=pltpu.CompilerParams(vmem_limit_bytes=60 << 20),
    )(basis, coeffs, first, second)
    return new_first, new_second, rebuilt


def solution(mesh):
    placed = (P("fsdp", None), P("fsdp", "roll"), P("fsdp", "roll"), P("fsdp", "roll"), P("roll", None))
    return jax.shard_map(
        local,
        mesh=mesh,
        in_specs=placed,
        out_specs=(P("fsdp", "roll"), P("fsdp", "roll"), P("roll", None)),
        check_vma=False,
    )
```
